32 devices in a mesh: fsdp: 4 (over z), ctx: 4 (over y, x), tp: 2 (over core).
Axes of the slice: x: 2, y: 2, z: 4, core: 2. Of those that a mesh axis runs over, the one named last changes fastest.
Arguments:
- inputs: bfloat16 [2, 4, 1024, 2048], P(None, 'fsdp', 'ctx'), may hold values from -6 to 6
- segment_ids: int32 [2, 4, 1024], P(None, 'fsdp'), may hold values from 0 to 2, never falling along the last dimension, each value on 1 to 512 neighbouring positions
- cotangent: bfloat16 [2, 4, 1024, 2048], P(None, 'fsdp', 'ctx'), may hold values from -6 to 6
- w_qkv: float32 [3, 2048, 2048], P(None, ('fsdp', 'ctx'), 'tp'), may hold values from -0.125 to 0.125
- w_out: float32 [2048, 2048], P('tp', ('fsdp', 'ctx')), may hold values from -1 to 1
- w_up: float32 [2048, 8192], P(('fsdp', 'ctx'), 'tp'), may hold values from -0.125 to 0.125
- w_down: float32 [8192, 2048], P('tp', ('fsdp', 'ctx')), may hold values from -0.0625 to 0.0625
- bias_qv: float32 [2, 2048], P(None, 'tp'), may hold values from -3 to 3
- bias_up: float32 [8192], P('tp'), may hold values from -3 to 3
- bias_res: float32 [2, 2048], replicated, may hold values from -3 to 3
- norm_gain: float32 [2, 2048], replicated, may hold values from 0.5 to 1.5
- norm_shift: float32 [2, 2048], replicated, may hold values from -3 to 3
- moment_qkv: float32 [3, 2048, 2048], P(None, ('fsdp', 'ctx'), 'tp'), may hold values from -28 to 28
- moment_out: float32 [2048, 2048], P('tp', ('fsdp', 'ctx')), may hold values from -28 to 28
- moment_up: float32 [2048, 8192], P(('fsdp', 'ctx'), 'tp'), may hold values from -28 to 28
- moment_down: float32 [8192, 2048], P('tp', ('fsdp', 'ctx')), may hold values from -28 to 28
- moment_bqv: float32 [2, 2048], P(None, 'tp'), may hold values from -256 to 256
- moment_bup: float32 [8192], P('tp'), may hold values from -256 to 256
- moment_bres: float32 [2, 2048], replicated, may hold values from -256 to 256
- moment_gain: float32 [2, 2048], replicated, may hold values from -256 to 256
- moment_shift: float32 [2, 2048], replicated, may hold values from -256 to 256
Outputs:
- layer_out: bfloat16 [2, 4, 1024, 2048], P(None, 'fsdp', 'ctx')
- input_grad: float32 [2, 4, 1024, 2048], P(None, 'fsdp', 'ctx')
- grad_qkv: float32 [3, 2048, 2048], P(None, ('fsdp', 'ctx'), 'tp')
- grad_out: float32 [2048, 2048], P('tp', ('fsdp', 'ctx'))
- grad_up: float32 [2048, 8192], P(('fsdp', 'ctx'), 'tp')
- grad_down: float32 [8192, 2048], P('tp', ('fsdp', 'ctx'))
- grad_bqv: float32 [2, 2048], P(None, 'tp')
- grad_bup: float32 [8192], P('tp')
- grad_bres: float32 [2, 2048], replicated
- grad_gain: float32 [2, 2048], replicated
- grad_shift: float32 [2, 2048], replicated
- state_qkv: float32 [3, 2048, 2048], P(None, ('fsdp', 'ctx'), 'tp')
- state_out: float32 [2048, 2048], P('tp', ('fsdp', 'ctx'))
- state_up: float32 [2048, 8192], P(('fsdp', 'ctx'), 'tp')
- state_down: float32 [8192, 2048], P('tp', ('fsdp', 'ctx'))
- state_bqv: float32 [2, 2048], P(None, 'tp')
- state_bup: float32 [8192], P('tp')
- state_bres: float32 [2, 2048], replicated
- state_gain: float32 [2, 2048], replicated
- state_shift: float32 [2, 2048], replicated
- master_qkv: float32 [3, 2048, 2048], P(None, ('fsdp', 'ctx'), 'tp')
- master_out: float32 [2048, 2048], P('tp', ('fsdp', 'ctx'))
- master_up: float32 [2048, 8192], P(('fsdp', 'ctx'), 'tp')
- master_down: float32 [8192, 2048], P('tp', ('fsdp', 'ctx'))
- master_bqv: float32 [2, 2048], P(None, 'tp')
- master_bup: float32 [8192], P('tp')
- master_bres: float32 [2, 2048], replicated
- master_gain: float32 [2, 2048], replicated
- master_shift: float32 [2, 2048], replicated
The draws below stay inside these ranges and needn't reach their ends.
Inputs may be any that keep to these rules, and one draw needn't show every extreme that they name: `segment_ids`: segment numbers never fall along a sequence.
All inputs are finite; a program needn't handle non-finite values.
Results may differ from the reference program's by a relative error of at most 0.025.
Values may be sent and summed in bfloat16 or wider, within the bound.
A program may use at most 320 MiB of HBM per device.

```python
import math
from functools import partial
import jax
import jax.numpy as jnp
import numpy as np
from jax import lax

D = 2048
HEADS = 16
HDIM = 128
FF = 8192
WINDOW = 1024
MICRO = 2
NS_STEPS = 5
HALF = 512
SEQS = 4
LENGTH = 1024
TOKENS = 8192


def levels(key, shape, shards, least, high):
    def one(position, shards_of):
        draws = jax.random.uniform(jax.random.fold_in(jax.random.fold_in(key, 6), position), (shards_of,), jnp.float32, least / len(shards), high / len(shards))
        return jnp.repeat(jnp.exp(draws), shape[position] // shards_of).reshape((-1,) + (1,) * (len(shape) - position - 1))

    gain = one(*shards[0])
    for cut in shards[1:]:
        gain = gain * one(*cut)
    return gain


def split_up(amount, total, most, lean):
    portions = [(1 << 20) // math.isqrt(standing ** lean) + 1 for standing in range(2, amount + 1)]
    spare, holding = total - most - (amount - 1), [1] * (amount - 1)
    while spare > 0:
        movable = [i for i in range(amount - 1) if holding[i] < most]
        mass, remaining = sum([portions[i] for i in movable]), spare
        for i in movable:
            more = min(most - holding[i], max(1, remaining * portions[i] // mass), spare)
            holding[i] = holding[i] + more
            spare = spare - more
    return np.array([most] + holding)


def uneven_parts(own_key, count, total, most, lean):
    if count == 2:
        one = jax.random.randint(own_key, (), max(1, total - most), min(most, total - 1) + 1)
        return jnp.stack([one, total - one])
    lengths = jnp.asarray(split_up(count, total, most, lean), jnp.int32)
    pairs = (count - 1) // 2
    source_of, taker = lengths[1:1 + 2 * pairs:2], lengths[2:2 + 2 * pairs:2]
    margin = jnp.minimum(source_of - 1, most - taker)
    shifted = jax.random.randint(jax.random.fold_in(own_key, 1), (pairs,), 0, 1 << 20) % (margin + 1)
    lengths = lengths.at[1:1 + 2 * pairs:2].set(source_of - shifted).at[2:2 + 2 * pairs:2].set(taker + shifted)
    return lengths[jax.random.permutation(jax.random.fold_in(own_key, 2), count)]


def normal_values(own_key, dims, scale, reach, cuts=(), held_as=jnp.bfloat16):
    gain = levels(own_key, dims, cuts, -0.22, 0.18) if cuts else 1.0
    drawn = jax.random.normal(own_key, dims, jnp.float32) * scale * gain
    return jnp.minimum(jnp.maximum(drawn, -reach), reach).astype(held_as)


def setup_inputs(seed: int = 0) -> dict:
    keys = jax.random.split(jax.random.key(seed), 22)
    return {
        "inputs": normal_values(keys[0], (MICRO, SEQS, LENGTH, D), 1.0, 6.0, ((1, 4), (2, 4))),
        "segment_ids": jax.vmap(lambda own: jnp.searchsorted(jnp.cumsum(uneven_parts(own, max(3, LENGTH // 1024), LENGTH, LENGTH // 2, 0)), jnp.arange(LENGTH), side="right"))(jax.random.split(keys[1], MICRO * SEQS)).reshape((MICRO, SEQS, LENGTH)).astype(jnp.int32),
        "cotangent": normal_values(keys[2], (MICRO, SEQS, LENGTH, D), 1.0, 6.0, ((1, 4), (2, 4))),
        "w_qkv": normal_values(keys[3], (3, D, D), D ** -0.5, 0.125, ((1, 16), (2, 2)), jnp.float32),
        "w_out": normal_values(keys[4], (D, D), (D * 16 // WINDOW) ** -0.5, 1.0, ((0, 2), (1, 16)), jnp.float32),
        "w_up": normal_values(keys[5], (D, FF), D ** -0.5, 0.125, ((0, 16), (1, 2)), jnp.float32),
        "w_down": normal_values(keys[6], (FF, D), FF ** -0.5, 0.0625, ((0, 2), (1, 16)), jnp.float32),
        "bias_qv": normal_values(keys[7], (2, D), 0.5, 3.0, ((1, 2),), jnp.float32),
        "bias_up": normal_values(keys[8], (FF,), 0.5, 3.0, ((0, 2),), jnp.float32),
        "bias_res": normal_values(keys[9], (2, D), 0.5, 3.0, (), jnp.float32),
        "norm_gain": jnp.clip(1.0 + 0.1 * jax.random.normal(keys[10], (2, D), jnp.float32), 0.5, 1.5),
        "norm_shift": normal_values(keys[11], (2, D), 0.5, 3.0, (), jnp.float32),
        "moment_qkv": normal_values(keys[12], (3, D, D), (0.05 * TOKENS ** 0.5), 28.0, ((1, 16), (2, 2)), jnp.float32),
        "moment_out": normal_values(keys[13], (D, D), (0.05 * TOKENS ** 0.5), 28.0, ((0, 2), (1, 16)), jnp.float32),
        "moment_up": normal_values(keys[14], (D, FF), (0.05 * TOKENS ** 0.5), 28.0, ((0, 16), (1, 2)), jnp.float32),
        "moment_down": normal_values(keys[15], (FF, D), (0.05 * TOKENS ** 0.5), 28.0, ((0, 2), (1, 16)), jnp.float32),
        "moment_bqv": normal_values(keys[16], (2, D), (0.5 * TOKENS ** 0.5), 256.0, ((1, 2),), jnp.float32),
        "moment_bup": normal_values(keys[17], (FF,), (0.5 * TOKENS ** 0.5), 256.0, ((0, 2),), jnp.float32),
        "moment_bres": normal_values(keys[18], (2, D), (0.5 * TOKENS ** 0.5), 256.0, (), jnp.float32),
        "moment_gain": normal_values(keys[19], (2, D), (0.5 * TOKENS ** 0.5), 256.0, (), jnp.float32),
        "moment_shift": normal_values(keys[20], (2, D), (0.5 * TOKENS ** 0.5), 256.0, (), jnp.float32),
    }


@jax.custom_vjp
def low(v):
    return lax.optimization_barrier(v.astype(jnp.bfloat16)).astype(jnp.float32)

@jax.custom_vjp
def low_back(v):
    return v

def low_keep(v):
    return (low(v), None)

def low_pass(kept, grad):
    return (grad,)

def back_keep(v):
    return (v, None)

def back_low(kept, grad):
    return (low(grad),)
low.defvjp(low_keep, low_pass)
low_back.defvjp(back_keep, back_low)
highest = lax.Precision.HIGHEST
norm_epsilon = 1e-05
ortho_epsilon = 1e-07
coef_first = 3.4445
coef_second = -4.775
coef_third = 2.0315
decay_rate = 0.5
matrix_rate = 0.25
masked_value = -1000000000.0

def matmul(left_side, right_side):
    return jnp.dot(left_side, right_side, precision=highest, preferred_element_type=jnp.float32)

def gelu_tanh(values):
    return jax.nn.gelu(values, approximate=True)

def layer_norm(values, gain_row, shift_row):
    center = values - lax.optimization_barrier(jnp.mean(values, axis=-1, keepdims=True))
    inverse = lax.rsqrt(lax.optimization_barrier(jnp.mean(center * center, axis=-1, keepdims=True)) + norm_epsilon)
    return center * inverse * gain_row + shift_row

def attention(queries, key_rows, value_rows, segment_row):
    length = queries.shape[0]
    block_rows = min(512, length)
    count_blocks = length // block_rows
    query_heads = queries.reshape(length, HEADS, HDIM)
    key_pad = jnp.pad(key_rows.reshape(length, HEADS, HDIM), ((HALF, HALF), (0, 0), (0, 0)))
    value_pad = jnp.pad(value_rows.reshape(length, HEADS, HDIM), ((HALF, HALF), (0, 0), (0, 0)))
    seg_pad = jnp.pad(segment_row, (HALF, HALF), constant_values=-1)
    scale_factor = 1.0 / math.sqrt(HDIM)

    def one_block(block_index):
        first_row = block_index * block_rows
        query_part = lax.dynamic_slice_in_dim(query_heads, first_row, block_rows, 0)
        key_part = lax.dynamic_slice_in_dim(key_pad, first_row, block_rows + 2 * HALF, 0)
        value_part = lax.dynamic_slice_in_dim(value_pad, first_row, block_rows + 2 * HALF, 0)
        query_seg = lax.dynamic_slice_in_dim(segment_row, first_row, block_rows, 0)
        key_seg = lax.dynamic_slice_in_dim(seg_pad, first_row, block_rows + 2 * HALF, 0)
        distance = jnp.arange(block_rows, dtype=jnp.int32)[:, None] - (jnp.arange(block_rows + 2 * HALF, dtype=jnp.int32)[None, :] - HALF)
        allowed = (query_seg[:, None] == key_seg[None, :]) & (jnp.abs(distance) <= HALF)
        scores = jnp.einsum('qhd,khd->hqk', query_part, key_part, precision=highest) * scale_factor
        scores = low_back(scores)
        scores = jnp.where(allowed[None], scores, masked_value)
        weights = jax.nn.softmax(scores, axis=-1)
        return jnp.einsum('hqk,khd->qhd', low(weights), value_part, precision=highest)
    blocks = lax.map(jax.checkpoint(one_block), jnp.arange(count_blocks, dtype=jnp.int32))
    return blocks.reshape(length, HEADS * HDIM)

def sequence_forward(params, sequence_pair):
    w_query, w_key, w_value, w_proj, w_expand, w_reduce, bias_qv, bias_up, bias_res, norm_gain, norm_shift = params
    row_values, segment_row = sequence_pair
    queries = low_back(low(matmul(row_values, w_query) + bias_qv[0]))
    key_rows = low_back(low(matmul(row_values, w_key)))
    value_rows = low_back(low(matmul(row_values, w_value) + bias_qv[1]))
    context = low_back(low(attention(queries, key_rows, value_rows, segment_row)))
    attended = low_back(matmul(context, w_proj) + bias_res[0])
    first = layer_norm(row_values + attended, norm_gain[0], norm_shift[0])
    pre_act = low_back(matmul(low(first), w_expand) + bias_up)
    activated = low(gelu_tanh(pre_act))
    branch = low_back(matmul(activated, w_reduce) + bias_res[1])
    return layer_norm(first + branch, norm_gain[1], norm_shift[1])

def forward(segment_all, rows_all, w_qkv, w_out, w_up, w_down, bias_qv, bias_up, bias_res, norm_gain, norm_shift):
    params = (low(w_qkv[0]), low(w_qkv[1]), low(w_qkv[2]), low(w_out), low(w_up), low(w_down), bias_qv, bias_up, bias_res, norm_gain, norm_shift)
    return lax.map(jax.checkpoint(partial(sequence_forward, params)), (rows_all, segment_all))

def orthogonalize(slabs):
    slab_norm = jnp.sqrt(lax.optimization_barrier(jnp.sum(slabs * slabs, axis=(1, 2), keepdims=True)))
    current = slabs / (slab_norm + ortho_epsilon)
    for sweep_index in range(NS_STEPS):
        gram_matrix = jnp.einsum('ndk,ndl->nkl', current, current, precision=highest)
        polynomial = coef_second * gram_matrix + coef_third * jnp.einsum('nkl,nlm->nkm', gram_matrix, gram_matrix, precision=highest)
        current = coef_first * current + jnp.einsum('ndk,nkl->ndl', current, polynomial, precision=highest)
    return current

def reference(inputs, segment_ids, cotangent, w_qkv, w_out, w_up, w_down, bias_qv, bias_up, bias_res, norm_gain, norm_shift, moment_qkv, moment_out, moment_up, moment_down, moment_bqv, moment_bup, moment_bres, moment_gain, moment_shift):
    count_seqs = MICRO * SEQS
    rows_all = inputs.astype(jnp.float32).reshape(count_seqs, LENGTH, D)
    segment_all = segment_ids.reshape(count_seqs, LENGTH).astype(jnp.int32)
    outputs, pullback = jax.vjp(partial(forward, segment_all), rows_all, w_qkv, w_out, w_up, w_down, bias_qv, bias_up, bias_res, norm_gain, norm_shift)
    cot_rows = cotangent.astype(jnp.float32).reshape(count_seqs, LENGTH, D)
    grad_rows, grad_qkv, grad_out, grad_up, grad_down, grad_bqv, grad_bup, grad_bres, grad_gain, grad_shift = pullback(cot_rows)
    layer_out = outputs.reshape(MICRO, SEQS, LENGTH, D).astype(jnp.bfloat16)
    input_grad = grad_rows.reshape(MICRO, SEQS, LENGTH, D)
    state_qkv = decay_rate * moment_qkv + grad_qkv
    state_out = decay_rate * moment_out + grad_out
    state_up = decay_rate * moment_up + grad_up
    state_down = decay_rate * moment_down + grad_down
    slab_qkv = state_qkv.reshape(3, D, HEADS, HDIM).transpose(0, 2, 1, 3).reshape(3 * HEADS, D, HDIM)
    ortho_qkv = orthogonalize(slab_qkv).reshape(3, HEADS, D, HDIM).transpose(0, 2, 1, 3).reshape(3, D, D)
    slab_out = state_out.reshape(HEADS, HDIM, D).transpose(0, 2, 1)
    ortho_out = orthogonalize(slab_out).transpose(0, 2, 1).reshape(D, D)
    slab_up = state_up.reshape(D, FF // HDIM, HDIM).transpose(1, 0, 2)
    ortho_up = orthogonalize(slab_up).transpose(1, 0, 2).reshape(D, FF)
    slab_down = state_down.reshape(FF // HDIM, HDIM, D).transpose(0, 2, 1)
    ortho_down = orthogonalize(slab_down).transpose(0, 2, 1).reshape(FF, D)
    step_scale = matrix_rate * math.sqrt(D / HDIM)
    master_qkv = w_qkv - step_scale * ortho_qkv
    master_out = w_out - step_scale * ortho_out
    master_up = w_up - step_scale * ortho_up
    master_down = w_down - step_scale * ortho_down
    vector_step = 1.0 / math.sqrt(TOKENS)
    state_bqv = decay_rate * moment_bqv + grad_bqv
    state_bup = decay_rate * moment_bup + grad_bup
    state_bres = decay_rate * moment_bres + grad_bres
    state_gain = decay_rate * moment_gain + grad_gain
    state_shift = decay_rate * moment_shift + grad_shift
    master_bqv = bias_qv - vector_step * state_bqv
    master_bup = bias_up - vector_step * state_bup
    master_bres = bias_res - vector_step * state_bres
    master_gain = norm_gain - vector_step * state_gain
    master_shift = norm_shift - vector_step * state_shift
    return (layer_out, input_grad, grad_qkv, grad_out, grad_up, grad_down, grad_bqv, grad_bup, grad_bres, grad_gain, grad_shift, state_qkv, state_out, state_up, state_down, state_bqv, state_bup, state_bres, state_gain, state_shift, master_qkv, master_out, master_up, master_down, master_bqv, master_bup, master_bres, master_gain, master_shift)
```

```python
import math

import jax
import jax.numpy as jnp
from jax import lax
from jax.experimental import pallas as pl
from jax.experimental.pallas import tpu as pltpu
from jax.sharding import PartitionSpec as P

HDIM = 128
NS_STEPS = 5
HALF = 512

bf16 = jnp.bfloat16
f32 = jnp.float32
highest = lax.Precision.HIGHEST
norm_epsilon = 1e-05
ortho_epsilon = 1e-07
coef_first = 3.4445
coef_second = -4.775
coef_third = 2.0315
decay_rate = 0.5
matrix_rate = 0.25
masked_value = -1e30

CORE = [(0, 1), (1, 0)]


def xor_pairs(size, mask):
    return [(i, i ^ mask) for i in range(size)]


def swap_core(value):
    return lax.ppermute(value, "tp", CORE)


def swap_ctx(value, mask):
    return lax.ppermute(value, "ctx", xor_pairs(4, mask))


def swap_fsdp(value, mask):
    return lax.ppermute(value, "fsdp", xor_pairs(4, mask))


def mm(left, right, dims):
    return lax.dot_general(left, right, ((dims[:1], dims[1:]), ((), ())), preferred_element_type=f32)


def spread(own):
    if lax.axis_size("ctx") != 4:
        whole = lax.all_gather(own, "ctx", axis=0, tiled=False)
        return [whole[i] for i in range(whole.shape[0])]
    half = own.shape[0] // 2
    from_x = swap_ctx(own, 1)
    from_y = swap_ctx(own, 2)
    top = swap_ctx(from_x[:half], 2)
    low = swap_ctx(from_y[half:], 1)
    return [own, from_x, from_y, jnp.concatenate([top, low], axis=0)]


def collect(partial):
    count = lax.axis_size("ctx")
    rows = partial.shape[0] // count
    if count != 4:
        return lax.psum_scatter(partial, "ctx", scatter_dimension=0, tiled=True).astype(f32)
    half = rows // 2
    part = [partial[k * rows : (k + 1) * rows] for k in range(4)]
    over_x = swap_ctx(jnp.concatenate([part[1][:half], part[3][:half]], axis=0), 1).astype(f32)
    over_y = swap_ctx(jnp.concatenate([part[2][half:], part[3][half:]], axis=0), 2).astype(f32)
    then_y = swap_ctx((part[2][:half].astype(f32) + over_x[half:]).astype(bf16), 2)
    then_x = swap_ctx((part[1][half:].astype(f32) + over_y[half:]).astype(bf16), 1)
    own = part[0].astype(f32)
    return jnp.concatenate(
        [
            own[:half] + over_x[:half] + then_y.astype(f32),
            own[half:] + over_y[:half] + then_x.astype(f32),
        ],
        axis=0,
    )


def layer_norm(values, gain_row, shift_row):
    center = values - jnp.mean(values, axis=-1, keepdims=True)
    inverse = lax.rsqrt(jnp.mean(center * center, axis=-1, keepdims=True) + norm_epsilon)
    normed = center * inverse
    return (normed * gain_row + shift_row, normed, inverse)


def layer_norm_back(grad_upper, normed, inverse, gain_row):
    grad_normed = grad_upper * gain_row
    mean_grad = jnp.mean(grad_normed, axis=-1, keepdims=True)
    mean_dot = jnp.mean(grad_normed * normed, axis=-1, keepdims=True)
    grad_in = inverse * (grad_normed - mean_grad - normed * mean_dot)
    return (grad_in, jnp.sum(grad_upper * normed, axis=0), jnp.sum(grad_upper, axis=0))


def gelu_tanh(values):
    return jax.nn.gelu(values, approximate=True)


def block_weights(query, keys, place_rows, place_cols):
    scores = mm(query, keys, (1, 1))
    scores = jnp.where(jnp.abs(place_rows - place_cols) <= HALF, scores, masked_value)
    top = jnp.max(scores, axis=-1, keepdims=True)
    weights = jnp.exp((scores - top) * HDIM**-0.5)
    return weights, 1.0 / jnp.sum(weights, axis=-1, keepdims=True)


def attend_kernel(block, q_ref, k_ref, v_ref, rows_ref, cols_ref, out_ref):
    for start in range(0, q_ref.shape[0], block):
        span = pl.ds(start, block)
        weights, inverse = block_weights(q_ref[span, :], k_ref[...], rows_ref[span, :], cols_ref[...])
        out_ref[span, :] = (mm(weights.astype(bf16), v_ref[...], (1, 0)) * inverse).astype(bf16)


def attend_forward(qkv, place):
    length = qkv.shape[0]
    heads = qkv.shape[1] // (3 * HDIM)
    piece = lambda which: pl.BlockSpec((length, HDIM), lambda h, w=which: (0, w * heads + h))
    return pl.pallas_call(
        lambda *refs: attend_kernel(256, *refs),
        out_shape=jax.ShapeDtypeStruct((length, heads * HDIM), bf16),
        grid=(heads,),
        in_specs=[
            piece(0),
            piece(1),
            piece(2),
            pl.BlockSpec((length, 1), lambda h: (0, 0)),
            pl.BlockSpec((1, length), lambda h: (0, 0)),
        ],
        out_specs=pl.BlockSpec((length, HDIM), lambda h: (0, h)),
        compiler_params=pltpu.CompilerParams(vmem_limit_bytes=40 << 20),
        cost_estimate=pl.CostEstimate(
            flops=4 * heads * length * length * HDIM,
            bytes_accessed=8 * heads * length * HDIM,
            transcendentals=heads * length * length,
        ),
        name="attend_forward",
    )(qkv, qkv, qkv, place[:, None], place[None, :])


def attend_back_kernel(
    block, q_ref, k_ref, v_ref, up_ref, rows_ref, cols_ref, gq_ref, gk_ref, gv_ref, sum_k, sum_v
):
    scale = HDIM**-0.5
    for start in range(0, q_ref.shape[0], block):
        span = pl.ds(start, block)
        query = q_ref[span, :]
        upper = up_ref[span, :]
        weights, inverse = block_weights(query, k_ref[...], rows_ref[span, :], cols_ref[...])
        probs = weights * inverse
        grad_probs = mm(upper, v_ref[...], (1, 1))
        inner = jnp.sum(probs * grad_probs, axis=-1, keepdims=True)
        grad_scores = (probs * (grad_probs - inner)).astype(bf16)
        gq_ref[span, :] = (mm(grad_scores, k_ref[...], (1, 0)) * scale).astype(bf16)
        add_k = mm(grad_scores, query, (0, 0))
        add_v = mm(probs.astype(bf16), upper, (0, 0))
        if start == 0:
            sum_k[...] = add_k
            sum_v[...] = add_v
        else:
            sum_k[...] += add_k
            sum_v[...] += add_v
    gk_ref[...] = (sum_k[...] * scale).astype(bf16)
    gv_ref[...] = sum_v[...].astype(bf16)


def attend_backward(qkv, upper, place):
    length = qkv.shape[0]
    heads = qkv.shape[1] // (3 * HDIM)
    piece = lambda which: pl.BlockSpec((length, HDIM), lambda h, w=which: (0, w * heads + h))
    one = jax.ShapeDtypeStruct((length, heads * HDIM), bf16)
    outs = pl.pallas_call(
        lambda *refs: attend_back_kernel(256, *refs),
        out_shape=(one, one, one),
        grid=(heads,),
        in_specs=[
            piece(0),
            piece(1),
            piece(2),
            piece(0),
            pl.BlockSpec((length, 1), lambda h: (0, 0)),
            pl.BlockSpec((1, length), lambda h: (0, 0)),
        ],
        out_specs=(piece(0), piece(0), piece(0)),
        scratch_shapes=[pltpu.VMEM((length, HDIM), f32), pltpu.VMEM((length, HDIM), f32)],
        compiler_params=pltpu.CompilerParams(vmem_limit_bytes=48 << 20),
        cost_estimate=pl.CostEstimate(
            flops=10 * heads * length * length * HDIM,
            bytes_accessed=14 * heads * length * HDIM,
            transcendentals=heads * length * length,
        ),
        name="attend_backward",
    )(qkv, qkv, qkv, upper, place[:, None], place[None, :])
    return jnp.concatenate(outs, axis=1)


def polynomial_kernel(gram_ref, out_ref):
    count, width, _ = gram_ref.shape
    same = lax.broadcasted_iota(jnp.int32, (width, width), 0) == lax.broadcasted_iota(
        jnp.int32, (width, width), 1
    )
    unit = same.astype(f32)
    dot = lambda a, b: jnp.dot(a, b, precision=highest, preferred_element_type=f32)
    grams, totals = [], []
    for n in range(count):
        gram = gram_ref[n]
        square = jnp.sum(jnp.sum(gram * unit, axis=1, keepdims=True), axis=0, keepdims=True)
        inverse = 1.0 / (jnp.sqrt(square) + ortho_epsilon)
        grams.append(gram * (inverse * inverse))
        totals.append(unit * inverse)
    for step in range(NS_STEPS):
        squares = [dot(g, g) for g in grams]
        polys = [
            coef_first * unit + coef_second * g + coef_third * s for g, s in zip(grams, squares)
        ]
        totals = [dot(q, p) for q, p in zip(totals, polys)]
        if step + 1 < NS_STEPS:
            halves = [dot(g, p) for g, p in zip(grams, polys)]
            grams = [dot(p, h) for p, h in zip(polys, halves)]
    for n in range(count):
        out_ref[n] = totals[n]


def polynomials(grams):
    count, width, _ = grams.shape
    return pl.pallas_call(
        polynomial_kernel,
        out_shape=jax.ShapeDtypeStruct(grams.shape, f32),
        in_specs=[pl.BlockSpec(memory_space=pltpu.VMEM)],
        out_specs=pl.BlockSpec(memory_space=pltpu.VMEM),
        compiler_params=pltpu.CompilerParams(vmem_limit_bytes=32 << 20),
        cost_estimate=pl.CostEstimate(
            flops=2 * 6 * 20 * count * width**3,
            bytes_accessed=8 * count * width**2,
            transcendentals=0,
        ),
        name="polynomials",
    )(grams)


def orthogonal(state):
    slabs = state.reshape(state.shape[0], -1, HDIM)
    count = slabs.shape[1]
    grams = jnp.einsum("dnk,dnl->nkl", slabs, slabs, precision=highest)
    size = lax.axis_size("fsdp")
    if size == 4 and count % 4 == 0:
        mine = lax.axis_index("fsdp")
        cut = grams.reshape(4, count // 4, HDIM, HDIM)
        take = lambda k: lax.dynamic_index_in_dim(cut, mine ^ k, 0, keepdims=False)
        total = take(0) + swap_fsdp(take(1), 1) + swap_fsdp(take(2), 2) + swap_fsdp(take(3), 3)
        own = polynomials(total)
        full = jnp.zeros(cut.shape, f32)
        for k in range(4):
            got = own if k == 0 else swap_fsdp(own, k)
            full = lax.dynamic_update_index_in_dim(full, got, mine ^ k, 0)
        full = full.reshape(count, HDIM, HDIM)
    else:
        full = polynomials(lax.psum(grams, "fsdp"))
    return jnp.einsum("dnk,nkl->dnl", slabs, full, precision=highest).reshape(state.shape)


def pack(matrices):
    qkv, out, up, down = matrices
    count = lax.axis_size("ctx")
    rows = up.shape[0]
    low = lambda v: v.astype(bf16)
    four = jnp.concatenate([low(qkv), low(out).T[None]], axis=0)
    attn = four.reshape(4, rows, count, -1).transpose(2, 1, 0, 3).reshape(count, rows, -1)
    up_cut = low(up).reshape(rows, count, -1).transpose(1, 0, 2)
    down_cut = low(down).T.reshape(rows, count, -1).transpose(1, 0, 2)
    return attn, up_cut, down_cut


def unpack(attn, up, down):
    count, rows, _ = up.shape
    four = attn.reshape(count, rows, 4, -1).transpose(2, 1, 0, 3).reshape(4, rows, -1)
    flat = lambda v: v.transpose(1, 0, 2).reshape(rows, -1)
    return four[:3], four[3].T, flat(up), flat(down).T


def over_ctx(stack):
    return lax.all_to_all(stack, "ctx", split_axis=0, concat_axis=0, tiled=True)


def to_blocks(stack):
    moved = over_ctx(stack)
    return moved.reshape(-1, moved.shape[-1])


def from_blocks(block):
    return over_ctx(block.reshape(lax.axis_size("ctx"), -1, block.shape[-1]))


def sum_everywhere(vector):
    if lax.axis_size("ctx") != 4 or lax.axis_size("fsdp") != 4:
        return lax.psum(vector, ("fsdp", "ctx", "tp"))
    vector = vector + swap_core(vector)
    vector = vector + swap_ctx(vector, 1)
    vector = vector + swap_ctx(vector, 2)
    vector = vector + swap_fsdp(vector, 1)
    return vector + swap_fsdp(vector, 2)


def body(
    inputs,
    segment_ids,
    cotangent,
    w_qkv,
    w_out,
    w_up,
    w_down,
    bias_qv,
    bias_up,
    bias_res,
    norm_gain,
    norm_shift,
    moment_qkv,
    moment_out,
    moment_up,
    moment_down,
    moment_bqv,
    moment_bup,
    moment_bres,
    moment_gain,
    moment_shift,
):
    count_c = lax.axis_size("ctx")
    count_f = lax.axis_size("fsdp")
    c = lax.axis_index("ctx")
    t = lax.axis_index("tp")
    rows = inputs.shape[2]
    width = inputs.shape[3]
    length = rows * count_c
    token_total = inputs.shape[0] * inputs.shape[1] * count_f * length
    e = w_qkv.shape[2] // count_c
    u = w_up.shape[1] // count_c

    own_micro = lambda v: lax.dynamic_index_in_dim(v, t, 0, keepdims=False)[0]
    row_low = own_micro(inputs)
    row_values = row_low.astype(f32)
    upper = own_micro(cotangent).astype(f32)
    segments = own_micro(segment_ids)
    index = jnp.arange(count_c)
    order = index ^ c if count_c == 4 else index
    place = (segments * (length + HALF + 1) + jnp.arange(length, dtype=jnp.int32)).reshape(count_c, rows)
    place = jnp.take(place, order, axis=0).reshape(length)

    weights = [to_blocks(s) for s in pack((w_qkv, w_out, w_up, w_down))]
    moments = [to_blocks(s) for s in pack((moment_qkv, moment_out, moment_up, moment_down))]
    gathered = [lax.all_gather(w, "fsdp", axis=0, tiled=True) for w in weights]
    attn_w, up_w, down_w = [(g, swap_core(g)) for g in gathered]

    bias_q = lax.dynamic_slice_in_dim(bias_qv, c * e, e, 1)
    bias_u = lax.dynamic_slice_in_dim(bias_up, c * u, u, 0)
    small = jnp.concatenate([bias_q.reshape(-1), bias_u])
    small_pair = (small, swap_core(small))
    cores = range(2)

    xs = jnp.concatenate(spread(row_low), axis=0)
    qkv = []
    for i in cores:
        shift = jnp.concatenate([small_pair[i][:e], jnp.zeros((e,), f32), small_pair[i][e : 2 * e]])
        qkv.append((mm(xs, attn_w[i][:, : 3 * e], (1, 0)) + shift).astype(bf16))
    context = [attend_forward(qkv[i], place) for i in cores]
    part = sum(mm(context[i], attn_w[i][:, 3 * e :], (1, 1)) for i in cores).astype(bf16)
    attended = collect(part) + bias_res[0]
    first, first_unit, first_inverse = layer_norm(row_values + attended, norm_gain[0], norm_shift[0])
    first_all = jnp.concatenate(spread(first.astype(bf16)), axis=0)
    pre_act = [mm(first_all, up_w[i], (1, 0)) + small_pair[i][2 * e :] for i in cores]
    active = [gelu_tanh(p).astype(bf16) for p in pre_act]
    part = sum(mm(active[i], down_w[i], (1, 1)) for i in cores).astype(bf16)
    branch = collect(part) + bias_res[1]
    out_rows, second_unit, second_inverse = layer_norm(first + branch, norm_gain[1], norm_shift[1])
    out_rows = out_rows.astype(bf16)

    grad_second, gain_second, shift_second = layer_norm_back(
        upper, second_unit, second_inverse, norm_gain[1]
    )
    grad_branch = grad_second.astype(bf16)
    branch_all = jnp.concatenate(spread(grad_branch), axis=0)
    grad_pre = []
    for i in cores:
        grad_act = mm(branch_all, down_w[i], (1, 0))
        grad_pre.append(jax.vjp(gelu_tanh, pre_act[i])[1](grad_act)[0].astype(bf16))
    part = sum(mm(grad_pre[i], up_w[i], (1, 1)) for i in cores).astype(bf16)
    term_down = [mm(branch_all, active[i], (0, 0)) for i in cores]
    term_up = [mm(first_all, grad_pre[i], (0, 0)) for i in cores]
    grad_first_out = grad_second + collect(part)
    grad_first, gain_first, shift_first = layer_norm_back(
        grad_first_out, first_unit, first_inverse, norm_gain[0]
    )
    grad_attended = grad_first.astype(bf16)
    attended_all = jnp.concatenate(spread(grad_attended), axis=0)
    grad_qkv_low = []
    for i in cores:
        grad_context = mm(attended_all, attn_w[i][:, 3 * e :], (1, 0)).astype(bf16)
        grad_qkv_low.append(attend_backward(qkv[i], grad_context, place))
    part = sum(mm(grad_qkv_low[i], attn_w[i][:, : 3 * e], (1, 1)) for i in cores).astype(bf16)
    term_attn = [
        jnp.concatenate(
            [mm(xs, grad_qkv_low[i], (0, 0)), mm(attended_all, context[i], (0, 0))], axis=1
        )
        for i in cores
    ]
    input_rows = grad_first + collect(part)

    both = lambda own, other: jnp.stack([jnp.where(t == m, own, other) for m in range(2)])[:, None]
    layer_out = both(out_rows, swap_core(out_rows))
    input_grad = both(input_rows, swap_core(input_rows))

    def to_owner(terms):
        total = terms[0] + swap_core(terms[1].astype(bf16)).astype(f32)
        return lax.psum_scatter(total.astype(bf16), "fsdp", scatter_dimension=0, tiled=True)

    sums = [to_owner(term) for term in (term_attn, term_up, term_down)]
    grads = [g.astype(f32) for g in unpack(*[from_blocks(s) for s in sums])]
    orthos = []
    for total, moment in zip(sums, moments):
        state = decay_rate * moment.astype(f32) + total.astype(f32)
        orthos.append(from_blocks(orthogonal(state).astype(bf16)))
    orthos = [o.astype(f32) for o in unpack(*orthos)]
    step_scale = matrix_rate * math.sqrt(width / HDIM)
    states = [
        decay_rate * m + g
        for m, g in zip((moment_qkv, moment_out, moment_up, moment_down), grads)
    ]
    masters = [w - step_scale * o for w, o in zip((w_qkv, w_out, w_up, w_down), orthos)]

    qv_sums = []
    for i in cores:
        sums_i = jnp.sum(grad_qkv_low[i].astype(f32), axis=0)
        qv_sums.append(jnp.stack([sums_i[:e], sums_i[2 * e :]]))
    up_sums = [jnp.sum(g.astype(f32), axis=0) for g in grad_pre]
    side = lambda pair: [jnp.where(t == m, pair[0], pair[1]) for m in range(2)]
    bqv_all = jnp.stack(
        [
            lax.dynamic_update_slice_in_dim(jnp.zeros((2, count_c * e), f32), v, c * e, 1)
            for v in side(qv_sums)
        ]
    )
    bup_all = jnp.stack(
        [
            lax.dynamic_update_slice_in_dim(jnp.zeros((count_c * u,), f32), v, c * u, 0)
            for v in side(up_sums)
        ]
    )
    rest = jnp.stack(
        [
            jnp.sum(grad_attended.astype(f32), axis=0),
            jnp.sum(grad_branch.astype(f32), axis=0),
            gain_first,
            gain_second,
            shift_first,
            shift_second,
        ]
    )
    flat = sum_everywhere(
        jnp.concatenate([bqv_all.reshape(-1), bup_all.reshape(-1), rest.reshape(-1)])
    )
    cut = bqv_all.size
    cut_two = cut + bup_all.size
    grad_bqv = lax.dynamic_index_in_dim(flat[:cut].reshape(bqv_all.shape), t, 0, keepdims=False)
    grad_bup = lax.dynamic_index_in_dim(flat[cut:cut_two].reshape(bup_all.shape), t, 0, keepdims=False)
    rest = flat[cut_two:].reshape(3, 2, width)
    vector_grads = (grad_bqv, grad_bup, rest[0], rest[1], rest[2])
    vector_states = [
        decay_rate * m + g
        for m, g in zip(
            (moment_bqv, moment_bup, moment_bres, moment_gain, moment_shift), vector_grads
        )
    ]
    vector_step = 1.0 / math.sqrt(token_total)
    vector_masters = [
        v - vector_step * s
        for v, s in zip((bias_qv, bias_up, bias_res, norm_gain, norm_shift), vector_states)
    ]
    return (
        layer_out,
        input_grad,
        *grads,
        *vector_grads,
        *states,
        *vector_states,
        *masters,
        *vector_masters,
    )


def solution(mesh):
    rows = P(None, "fsdp", "ctx", None)
    matrices = (
        P(None, ("fsdp", "ctx"), "tp"),
        P("tp", ("fsdp", "ctx")),
        P(("fsdp", "ctx"), "tp"),
        P("tp", ("fsdp", "ctx")),
    )
    vectors = (P(None, "tp"), P("tp"), P(), P(), P())
    return jax.shard_map(
        body,
        mesh=mesh,
        in_specs=(rows, P(None, "fsdp", None), rows, *matrices, *vectors, *matrices, *vectors),
        out_specs=(rows, rows, *((*matrices, *vectors) * 3)),
        check_vma=False,
    )
```

```python
import math

import jax
import jax.numpy as jnp
from jax import lax
from jax.experimental import pallas as pl
from jax.experimental.pallas import tpu as pltpu
from jax.sharding import PartitionSpec as P

HDIM = 128
NS_STEPS = 5
HALF = 512

bf16 = jnp.bfloat16
f32 = jnp.float32
highest = lax.Precision.HIGHEST
norm_epsilon = 1e-05
ortho_epsilon = 1e-07
coef_first = 3.4445
coef_second = -4.775
coef_third = 2.0315
decay_rate = 0.5
matrix_rate = 0.25
masked_value = -1e30

CORE = [(0, 1), (1, 0)]


def xor_pairs(size, mask):
    return [(i, i ^ mask) for i in range(size)]


def swap_core(value):
    return lax.ppermute(value, "tp", CORE)


def swap_ctx(value, mask):
    return lax.ppermute(value, "ctx", xor_pairs(4, mask))


def swap_fsdp(value, mask):
    return lax.ppermute(value, "fsdp", xor_pairs(4, mask))


def mm(left, right, dims):
    return lax.dot_general(left, right, ((dims[:1], dims[1:]), ((), ())), preferred_element_type=f32)


def spread(own):
    if lax.axis_size("ctx") != 4:
        whole = lax.all_gather(own, "ctx", axis=0, tiled=False)
        return [whole[i] for i in range(whole.shape[0])]
    half = own.shape[0] // 2
    from_x = swap_ctx(own, 1)
    from_y = swap_ctx(own, 2)
    top = swap_ctx(from_x[:half], 2)
    low = swap_ctx(from_y[half:], 1)
    return [own, from_x, from_y, jnp.concatenate([top, low], axis=0)]


def collect(partial):
    count = lax.axis_size("ctx")
    rows = partial.shape[0] // count
    if count != 4:
        return lax.psum_scatter(partial, "ctx", scatter_dimension=0, tiled=True).astype(f32)
    half = rows // 2
    part = [partial[k * rows : (k + 1) * rows] for k in range(4)]
    over_x = swap_ctx(jnp.concatenate([part[1][:half], part[3][:half]], axis=0), 1).astype(f32)
    over_y = swap_ctx(jnp.concatenate([part[2][half:], part[3][half:]], axis=0), 2).astype(f32)
    then_y = swap_ctx((part[2][:half].astype(f32) + over_x[half:]).astype(bf16), 2)
    then_x = swap_ctx((part[1][half:].astype(f32) + over_y[half:]).astype(bf16), 1)
    own = part[0].astype(f32)
    return jnp.concatenate(
        [
            own[:half] + over_x[:half] + then_y.astype(f32),
            own[half:] + over_y[:half] + then_x.astype(f32),
        ],
        axis=0,
    )


def layer_norm(values, gain_row, shift_row):
    center = values - jnp.mean(values, axis=-1, keepdims=True)
    inverse = lax.rsqrt(jnp.mean(center * center, axis=-1, keepdims=True) + norm_epsilon)
    normed = center * inverse
    return (normed * gain_row + shift_row, normed, inverse)


def layer_norm_back(grad_upper, normed, inverse, gain_row):
    grad_normed = grad_upper * gain_row
    mean_grad = jnp.mean(grad_normed, axis=-1, keepdims=True)
    mean_dot = jnp.mean(grad_normed * normed, axis=-1, keepdims=True)
    return inverse * (grad_normed - mean_grad - normed * mean_dot)


def gelu_tanh(values):
    return jax.nn.gelu(values, approximate=True)


MESH = pl.DeviceIdType.MESH


def remote(source, target, send, receive, axis, index):
    return pltpu.make_async_remote_copy(
        src_ref=source,
        dst_ref=target,
        send_sem=send,
        recv_sem=receive,
        device_id={axis: index},
        device_id_type=MESH,
    )


def greet(axis_indices):
    barrier = pltpu.get_barrier_semaphore()
    for axis, index in axis_indices:
        pl.semaphore_signal(barrier, inc=1, device_id={axis: index}, device_id_type=MESH)
    pl.semaphore_wait(barrier, len(axis_indices))


class RowSums:
    def __init__(self, part, from_x, from_y, then_y, then_x, to_y, to_x, send, receive):
        self.part, self.send, self.receive = part, send, receive
        self.from_x, self.from_y, self.then_y, self.then_x = from_x, from_y, then_y, then_x
        self.to_y, self.to_x = to_y, to_x
        self.pieces, self.count = to_y.shape[:2]
        self.span = [pl.ds(j * self.count, self.count) for j in range(self.pieces)]
        c = lax.axis_index("ctx")
        self.x_side = c + 1 - 2 * (c % 2)
        self.y_side = c + 2 - 4 * (c // 2)
        self.one, self.two = [], []

    def copy(self, stage, j, source, target, side):
        copy = remote(source, target, self.send.at[stage, j], self.receive.at[stage, j], "ctx", side)
        copy.start()
        return copy

    def first(self):
        for j in range(self.pieces):
            self.one.append(
                (
                    self.copy(0, j, self.part.at[:, 1, 0, self.span[j]], self.from_x.at[j], self.x_side),
                    self.copy(1, j, self.part.at[1, :, 1, self.span[j]], self.from_y.at[j], self.y_side),
                )
            )

    def second(self):
        for j in range(self.pieces):
            at = self.span[j]
            self.one[j][0].wait_recv()
            value = self.part[1, 0, 0, at].astype(f32) + self.from_x[j, 1].astype(f32)
            self.to_y[j] = value.astype(bf16)
            over_y = self.copy(2, j, self.to_y.at[j], self.then_y.at[j], self.y_side)
            self.one[j][1].wait_recv()
            value = self.part[0, 1, 1, at].astype(f32) + self.from_y[j, 1].astype(f32)
            self.to_x[j] = value.astype(bf16)
            over_x = self.copy(3, j, self.to_x.at[j], self.then_x.at[j], self.x_side)
            self.two.append((over_y, over_x))

    def third(self, j):
        at = self.span[j]
        self.two[j][0].wait_recv()
        self.two[j][1].wait_recv()
        top = self.part[0, 0, 0, at].astype(f32) + self.from_x[j, 0].astype(f32)
        low = self.part[0, 0, 1, at].astype(f32) + self.from_y[j, 0].astype(f32)
        top = top + self.then_y[j].astype(f32)
        low = low + self.then_x[j].astype(f32)
        return at, jnp.concatenate([top, low], axis=0)

    def end(self):
        for pair in (*self.one, *self.two):
            for one in pair:
                one.wait_send()


def row_scratch(half, width, pieces=4):
    count = half // pieces
    return [
        pltpu.VMEM((pieces, 2, count, width), bf16),
        pltpu.VMEM((pieces, 2, count, width), bf16),
        *[pltpu.VMEM((pieces, count, width), bf16)] * 4,
        pltpu.SemaphoreType.DMA((4, pieces)),
        pltpu.SemaphoreType.DMA((4, pieces)),
    ]


def exchange_kernel(step, n_in, n_vec, n_out, n_sum, *refs):
    part = refs[0]
    ins = refs[1 : 1 + n_in]
    vectors = refs[1 + n_in : 1 + n_in + n_vec]
    rest = refs[1 + n_in + n_vec :]
    whole = rest[0]
    outs = rest[1 : 1 + n_out]
    sums_ref = rest[1 + n_out]
    own, send, receive, local = rest[2 + n_out : 6 + n_out]
    row_sums = RowSums(part, *rest[6 + n_out :])
    x_side, y_side, span, count = row_sums.x_side, row_sums.y_side, row_sums.span, row_sums.count
    greet([("ctx", x_side), ("ctx", y_side)])

    def copy(stage, j, source, target, side):
        one = remote(source, target, send.at[stage, j], receive.at[stage, j], "ctx", side)
        one.start()
        return one

    row_sums.first()
    row_sums.second()
    params = [v[...] for v in vectors]
    third, fourth, kept = [], [], []
    totals = None
    for j in range(row_sums.pieces):
        at, total = row_sums.third(j)
        both = lambda ref: jnp.concatenate([ref[0, at], ref[1, at]], axis=0)
        sent, rows, sums = step(total, [both(r) for r in ins], params)
        own[0, at] = sent[:count]
        own[1, at] = sent[count:]
        third.append(
            (
                copy(0, j, own.at[:, at], whole.at[1, :, at], x_side),
                copy(1, j, own.at[:, at], whole.at[2, :, at], y_side),
            )
        )
        keep = pltpu.make_async_copy(own.at[:, at], whole.at[0, :, at], local.at[j])
        keep.start()
        kept.append(keep)
        for out, value in zip(outs, rows):
            out[0, at] = value[:count]
            out[1, at] = value[count:]
        totals = sums if totals is None else [a + b for a, b in zip(totals, sums)]
    for k in range(n_sum):
        sums_ref[k : k + 1] = totals[k]
    for j, at in enumerate(span):
        third[j][0].wait_recv()
        over_y = copy(2, j, whole.at[1, 0, at], whole.at[3, 0, at], y_side)
        third[j][1].wait_recv()
        over_x = copy(3, j, whole.at[2, 1, at], whole.at[3, 1, at], x_side)
        fourth.append((over_y, over_x))
    row_sums.end()
    for pair in third:
        for one in pair:
            one.wait_send()
    for pair in fourth:
        for one in pair:
            one.wait()
    for one in kept:
        one.wait()


def exchange(name, number, step, part, ins, vectors, out_types, n_sum):
    rows, width = ins[0].shape
    if lax.axis_size("ctx") != 4 or rows % 128:
        sent, outs, sums = step(collect(part), ins, vectors)
        return jnp.concatenate(spread(sent), axis=0), outs, sums
    pieces = 4
    half = rows // 2
    vmem = pl.BlockSpec(memory_space=pltpu.VMEM)
    halves = lambda v: v.reshape(2, half, width)
    whole, *outs, sums = pl.pallas_call(
        lambda *refs: exchange_kernel(step, len(ins), len(vectors), len(out_types), n_sum, *refs),
        out_shape=[
            jax.ShapeDtypeStruct((4, 2, half, width), bf16),
            *[jax.ShapeDtypeStruct((2, half, width), d) for d in out_types],
            jax.ShapeDtypeStruct((8, width), f32),
        ],
        in_specs=[vmem] * (1 + len(ins) + len(vectors)),
        out_specs=[pl.BlockSpec(memory_space=pl.ANY), *[vmem] * (len(out_types) + 1)],
        scratch_shapes=[
            pltpu.VMEM((2, half, width), bf16),
            pltpu.SemaphoreType.DMA((4, pieces)),
            pltpu.SemaphoreType.DMA((4, pieces)),
            pltpu.SemaphoreType.DMA((pieces,)),
            *row_scratch(half, width, pieces),
        ],
        compiler_params=pltpu.CompilerParams(
            collective_id=number, has_side_effects=True, vmem_limit_bytes=36 << 20
        ),
        cost_estimate=pl.CostEstimate(
            flops=60 * rows * width, bytes_accessed=130 << 20, transcendentals=0
        ),
        name=name,
    )(part.reshape(2, 2, 2, half, width), *map(halves, ins), *vectors)
    return (
        whole.reshape(4 * rows, width),
        [o.reshape(rows, width) for o in outs],
        [sums[k : k + 1] for k in range(n_sum)],
    )


def column_sum(values):
    return jnp.sum(values, axis=0, keepdims=True)


def first_step(total, rows, vectors):
    bias, gain, shift = vectors
    first, unit, inverse = layer_norm(rows[0].astype(f32) + total + bias, gain, shift)
    return first.astype(bf16), [unit, jnp.broadcast_to(inverse, unit.shape)], []


def second_step(total, rows, vectors):
    bias, gain_one, shift_one, gain, shift = vectors
    first = rows[0] * gain_one + shift_one
    out, unit, inverse = layer_norm(first + total + bias, gain, shift)
    upper = rows[1].astype(f32)
    grad = layer_norm_back(upper, unit, inverse, gain)
    low = grad.astype(bf16)
    sums = [column_sum(upper * unit), column_sum(upper), column_sum(low.astype(f32))]
    return low, [out.astype(bf16), grad], sums


def third_step(total, rows, vectors):
    (gain,) = vectors
    unit, inverse, upper = rows
    upper = upper + total
    grad = layer_norm_back(upper, unit, inverse, gain)
    low = grad.astype(bf16)
    sums = [column_sum(upper * unit), column_sum(upper), column_sum(low.astype(f32))]
    return low, [grad], sums


def block_weights(query, keys, place_rows, place_cols):
    scores = mm(query, keys, (1, 1))
    scores = jnp.where(jnp.abs(place_rows - place_cols) <= HALF, scores, masked_value)
    top = jnp.max(scores, axis=-1, keepdims=True)
    weights = jnp.exp((scores - top) * HDIM**-0.5)
    return weights, 1.0 / jnp.sum(weights, axis=-1, keepdims=True)


def attend_kernel(block, q_ref, k_ref, v_ref, rows_ref, cols_ref, out_ref):
    for start in range(0, q_ref.shape[0], block):
        span = pl.ds(start, block)
        weights, inverse = block_weights(q_ref[span, :], k_ref[...], rows_ref[span, :], cols_ref[...])
        out_ref[span, :] = (mm(weights.astype(bf16), v_ref[...], (1, 0)) * inverse).astype(bf16)


def attend_forward(qkv, place):
    length = qkv.shape[0]
    heads = qkv.shape[1] // (3 * HDIM)
    piece = lambda which: pl.BlockSpec((length, HDIM), lambda h, w=which: (0, w * heads + h))
    return pl.pallas_call(
        lambda *refs: attend_kernel(256, *refs),
        out_shape=jax.ShapeDtypeStruct((length, heads * HDIM), bf16),
        grid=(heads,),
        in_specs=[
            piece(0),
            piece(1),
            piece(2),
            pl.BlockSpec((length, 1), lambda h: (0, 0)),
            pl.BlockSpec((1, length), lambda h: (0, 0)),
        ],
        out_specs=pl.BlockSpec((length, HDIM), lambda h: (0, h)),
        compiler_params=pltpu.CompilerParams(vmem_limit_bytes=40 << 20),
        cost_estimate=pl.CostEstimate(
            flops=4 * heads * length * length * HDIM,
            bytes_accessed=8 * heads * length * HDIM,
            transcendentals=heads * length * length,
        ),
        name="attend_forward",
    )(qkv, qkv, qkv, place[:, None], place[None, :])


def attend_back_kernel(
    block, heads, q_ref, k_ref, v_ref, up_ref, rows_ref, cols_ref, out_ref, sum_k, sum_v
):
    scale = HDIM**-0.5
    head = pl.program_id(0)
    column = lambda which: pl.ds(pl.multiple_of((which * heads + head) * HDIM, HDIM), HDIM)
    for start in range(0, q_ref.shape[0], block):
        span = pl.ds(start, block)
        query = q_ref[span, :]
        upper = up_ref[span, :]
        weights, inverse = block_weights(query, k_ref[...], rows_ref[span, :], cols_ref[...])
        probs = weights * inverse
        grad_probs = mm(upper, v_ref[...], (1, 1))
        inner = jnp.sum(probs * grad_probs, axis=-1, keepdims=True)
        grad_scores = (probs * (grad_probs - inner)).astype(bf16)
        out_ref[span, column(0)] = (mm(grad_scores, k_ref[...], (1, 0)) * scale).astype(bf16)
        add_k = mm(grad_scores, query, (0, 0))
        add_v = mm(probs.astype(bf16), upper, (0, 0))
        if start == 0:
            sum_k[...] = add_k
            sum_v[...] = add_v
        else:
            sum_k[...] += add_k
            sum_v[...] += add_v
    out_ref[:, column(1)] = (sum_k[...] * scale).astype(bf16)
    out_ref[:, column(2)] = sum_v[...].astype(bf16)


def attend_backward(qkv, upper, place):
    length = qkv.shape[0]
    heads = qkv.shape[1] // (3 * HDIM)
    piece = lambda which: pl.BlockSpec((length, HDIM), lambda h, w=which: (0, w * heads + h))
    return pl.pallas_call(
        lambda *refs: attend_back_kernel(256, heads, *refs),
        out_shape=jax.ShapeDtypeStruct(qkv.shape, bf16),
        grid=(heads,),
        in_specs=[
            piece(0),
            piece(1),
            piece(2),
            piece(0),
            pl.BlockSpec((length, 1), lambda h: (0, 0)),
            pl.BlockSpec((1, length), lambda h: (0, 0)),
        ],
        out_specs=pl.BlockSpec(qkv.shape, lambda h: (0, 0)),
        scratch_shapes=[pltpu.VMEM((length, HDIM), f32), pltpu.VMEM((length, HDIM), f32)],
        compiler_params=pltpu.CompilerParams(vmem_limit_bytes=48 << 20),
        cost_estimate=pl.CostEstimate(
            flops=10 * heads * length * length * HDIM,
            bytes_accessed=14 * heads * length * HDIM,
            transcendentals=heads * length * length,
        ),
        name="attend_backward",
    )(qkv, qkv, qkv, upper, place[:, None], place[None, :])


def gram_of(moment_ref, total_ref, n):
    span = pl.ds(n * HDIM, HDIM)
    state = decay_rate * moment_ref[:, span].astype(f32) + total_ref[:, span].astype(f32)
    return lax.dot_general(
        state, state, (((0,), (0,)), ((), ())), precision=highest, preferred_element_type=f32
    )


def gram_kernel(moment_ref, total_ref, out_ref):
    for n in range(out_ref.shape[0]):
        out_ref[n] = gram_of(moment_ref, total_ref, n)


def apply_kernel(moment_ref, total_ref, factor_ref, out_ref):
    for n in range(factor_ref.shape[0]):
        span = pl.ds(n * HDIM, HDIM)
        state = decay_rate * moment_ref[:, span].astype(f32) + total_ref[:, span].astype(f32)
        out_ref[:, span] = jnp.dot(
            state, factor_ref[n], precision=highest, preferred_element_type=f32
        ).astype(bf16)


def whole_call(kernel, name, out, *operands, flops):
    vmem = pl.BlockSpec(memory_space=pltpu.VMEM)
    return pl.pallas_call(
        kernel,
        out_shape=out,
        in_specs=[vmem] * len(operands),
        out_specs=vmem,
        compiler_params=pltpu.CompilerParams(vmem_limit_bytes=32 << 20),
        cost_estimate=pl.CostEstimate(
            flops=flops, bytes_accessed=sum(o.size * o.dtype.itemsize for o in operands), transcendentals=0
        ),
        name=name,
    )(*operands)


def polynomial(grams):
    width = grams[0].shape[0]
    same = lax.broadcasted_iota(jnp.int32, (width, width), 0) == lax.broadcasted_iota(
        jnp.int32, (width, width), 1
    )
    unit = same.astype(f32)
    dot = lambda a, b: jnp.dot(a, b, precision=highest, preferred_element_type=f32)
    scaled, totals = [], []
    for gram in grams:
        square = jnp.sum(jnp.sum(gram * unit, axis=1, keepdims=True), axis=0, keepdims=True)
        inverse = 1.0 / (jnp.sqrt(square) + ortho_epsilon)
        scaled.append(gram * (inverse * inverse))
        totals.append(unit * inverse)
    for step in range(NS_STEPS):
        squares = [dot(g, g) for g in scaled]
        polys = [
            coef_first * unit + coef_second * g + coef_third * s for g, s in zip(scaled, squares)
        ]
        totals = [dot(q, p) for q, p in zip(totals, polys)]
        if step + 1 < NS_STEPS:
            halves = [dot(g, p) for g, p in zip(scaled, polys)]
            scaled = [dot(p, h) for p, h in zip(polys, halves)]
    return totals


def polynomial_kernel(gram_ref, out_ref):
    for n, total in enumerate(polynomial([gram_ref[n] for n in range(gram_ref.shape[0])])):
        out_ref[n] = total


def slab_kernel(groups, with_rows, *refs):
    moments, totals, refs = refs[:groups], refs[groups : 2 * groups], refs[2 * groups :]
    if with_rows:
        part, base, vector, refs = refs[0], refs[1], refs[2], refs[3:]
    grads, orthos, refs = refs[:groups], refs[groups : 2 * groups], refs[2 * groups :]
    if with_rows:
        summed, vector_out, refs = refs[0], refs[1], refs[2:]
    grams, pieces, factors, stage, send_c, receive_c, send_f, receive_f, local = refs[:9]
    rows = totals[0].shape[0] // 4
    each_group = totals[0].shape[1] // HDIM
    count = grams.shape[0]
    c = lax.axis_index("ctx")
    f = lax.axis_index("fsdp")
    sides = [(c + i) % 4 for i in range(4)]
    planes = [(f + i) % 4 for i in range(4)]
    peers = [("ctx", sides[i]) for i in (1, 2, 3)] + [("fsdp", planes[i]) for i in (1, 2, 3)]
    if with_rows:
        t = lax.axis_index("tp")
        partners = [
            ("tp", 1 - t),
            ("ctx", c + 1 - 2 * (c % 2)),
            ("ctx", c + 2 - 4 * (c // 2)),
            ("fsdp", f + 1 - 2 * (f % 2)),
            ("fsdp", f + 2 - 4 * (f // 2)),
        ]
        peers.append(partners[0])
        sent_v, got_v, send_v, receive_v = refs[9:13]
        sent_v[0] = vector[...]
    greet(peers)

    def vector_start(k):
        one = remote(sent_v.at[k], got_v.at[k], send_v.at[k], receive_v.at[k], *partners[k])
        one.start()
        vector_copies.append(one)

    def vector_next(k):
        if not with_rows:
            return
        vector_copies[k].wait_recv()
        if k < 4:
            sent_v[k + 1] = sent_v[k] + got_v[k]
            vector_start(k + 1)
        else:
            vector_out[...] = sent_v[k] + got_v[k]
            for one in vector_copies:
                one.wait_send()

    vector_copies = []
    place = lambda index: pl.ds(pl.multiple_of(index * rows, rows), rows)
    started = []

    def begin(copy):
        copy.start()
        started.append(copy)

    def to_side(source, target, kind, i):
        begin(
            remote(
                source, target, send_c.at[kind, i - 1], receive_c.at[kind, i - 1], "ctx", sides[i]
            )
        )

    if with_rows:
        vector_start(0)
        sum_rows = RowSums(part, *refs[13:])
        sum_rows.first()
    for g in range(groups):
        for i in (3, 1, 2):
            to_side(totals[g].at[place(sides[i])], grads[g].at[c], g, i)
        begin(pltpu.make_async_copy(totals[g].at[place(c)], grads[g].at[c], local.at[0, g]))

    size = min(each_group, count // 2)
    batches = range(count // size)
    each = size // 4

    def to_planes(kind, b, source, target):
        copies = []
        for i in (1, 2, 3):
            sems = send_f.at[2 * b + kind, i - 1], receive_f.at[2 * b + kind, i - 1]
            one = remote(source(i), target(i), *sems, "fsdp", planes[i])
            one.start()
            copies.append(one)
        return copies

    summing, sharing = [], []
    for b in batches:
        first = b * size
        for n in range(first, first + size):
            g = n // each_group
            grams[n] = gram_of(moments[g], totals[g], n % each_group)
        summing.append(
            to_planes(
                0,
                b,
                lambda i: grams.at[pl.ds(first + planes[i] * each, each)],
                lambda i: pieces.at[i - 1, pl.ds(b * each, each)],
            )
        )
    vector_next(0)
    if with_rows:
        sum_rows.second()
    for b in batches:
        own = b * size + f * each
        sums = [grams[own + n] for n in range(each)]
        for i in (1, 2, 3):
            summing[b][i - 1].wait()
            sums = [s + pieces[i - 1, b * each + n] for n, s in enumerate(sums)]
        for n, total in enumerate(polynomial(sums)):
            factors[own + n] = total
        part_of = lambda i: factors.at[pl.ds(own, each)]
        sharing.append(to_planes(1, b, part_of, part_of))
        vector_next(1 + b)
    if with_rows:
        for j in range(sum_rows.pieces):
            span, total = sum_rows.third(j)
            for h in range(2):
                value = total[h * sum_rows.count : (h + 1) * sum_rows.count]
                summed[h, span] = base[h, span] + value
    vector_next(3)
    for b in batches:
        for one in sharing[b]:
            one.wait()
        g, first = b * size // each_group, b * size % each_group
        wide = pl.ds(first * HDIM, size * HDIM)
        for i in (3, 1, 2, 0):
            span = place(sides[i])
            for n in range(first, first + size):
                column = pl.ds(n * HDIM, HDIM)
                state = decay_rate * moments[g][span, column].astype(f32)
                state = state + totals[g][span, column].astype(f32)
                stage[g, i, :, column] = jnp.dot(
                    state, factors[g * each_group + n], precision=highest, preferred_element_type=f32
                ).astype(bf16)
            source, target = stage.at[g, i, :, wide], orthos[g].at[c, :, wide]
            if i:
                to_side(source, target, groups + b, i)
            else:
                begin(pltpu.make_async_copy(source, target, local.at[1, b]))
    vector_next(4)
    for one in started:
        one.wait()
    if with_rows:
        sum_rows.end()


def gradients_and_orthogonal(name, number, moments, totals, part=None, base=None, vector=None):
    rows, columns = totals[0].shape
    groups = len(totals)
    count = groups * columns // HDIM
    flops = 2 * 6 * rows * columns * HDIM * groups
    vmem = pl.BlockSpec(memory_space=pltpu.VMEM)
    with_rows = part is not None
    if lax.axis_size("fsdp") == 4 and lax.axis_size("ctx") == 4 and count in (8, 16) and groups == count // 8:
        blocks = jax.ShapeDtypeStruct((4, rows // 4, columns), bf16)
        anywhere = pl.BlockSpec(memory_space=pl.ANY)
        out_shape, out_specs = [blocks] * (2 * groups), [anywhere] * (2 * groups)
        operands, more = [*moments, *totals], []
        if with_rows:
            height, width = base.shape
            half = height // 2
            lines = vector.size // HDIM
            operands += [part.reshape(2, 2, 2, half, width), base.reshape(2, half, width)]
            operands.append(vector.reshape(lines, HDIM))
            out_shape.append(jax.ShapeDtypeStruct((2, half, width), f32))
            out_shape.append(jax.ShapeDtypeStruct((lines, HDIM), f32))
            out_specs += [vmem, vmem]
            more = [
                pltpu.VMEM((5, lines, HDIM), f32),
                pltpu.VMEM((5, lines, HDIM), f32),
                pltpu.SemaphoreType.DMA((5,)),
                pltpu.SemaphoreType.DMA((5,)),
                *row_scratch(half, width),
            ]
        outs = pl.pallas_call(
            lambda *refs: slab_kernel(groups, with_rows, *refs),
            out_shape=out_shape,
            in_specs=[vmem] * len(operands),
            out_specs=out_specs,
            scratch_shapes=[
                pltpu.VMEM((count, HDIM, HDIM), f32),
                pltpu.VMEM((3, count // 4, HDIM, HDIM), f32),
                pltpu.VMEM((count, HDIM, HDIM), f32),
                pltpu.VMEM((groups, 4, rows // 4, columns), bf16),
                pltpu.SemaphoreType.DMA((groups + 2, 3)),
                pltpu.SemaphoreType.DMA((groups + 2, 3)),
                pltpu.SemaphoreType.DMA((4, 3)),
                pltpu.SemaphoreType.DMA((4, 3)),
                pltpu.SemaphoreType.DMA((2, 2)),
                *more,
            ],
            compiler_params=pltpu.CompilerParams(
                collective_id=number, has_side_effects=True, vmem_limit_bytes=40 << 20
            ),
            cost_estimate=pl.CostEstimate(
                flops=3 * flops, bytes_accessed=100 << 20, transcendentals=0
            ),
            name=name,
        )(*operands)
        pairs = [(outs[g], outs[groups + g]) for g in range(groups)]
        if with_rows:
            return pairs, outs[-2].reshape(base.shape), outs[-1].reshape(vector.shape)
        return pairs, None, None
    pairs = []
    shape = jax.ShapeDtypeStruct((count // groups, HDIM, HDIM), f32)
    for moment, total in zip(moments, totals):
        grams = whole_call(gram_kernel, "grams", shape, moment, total, flops=flops)
        full = whole_call(
            polynomial_kernel, "polynomials", shape, lax.psum(grams, "fsdp"), flops=flops
        )
        own = jax.ShapeDtypeStruct((rows, columns), bf16)
        ortho = whole_call(apply_kernel, "apply", own, moment, total, full, flops=flops)
        pairs.append((from_blocks(total), from_blocks(ortho)))
    if with_rows:
        return pairs, base + collect(part), lax.psum(vector, ("fsdp", "ctx", "tp"))
    return pairs, None, None


def pack(matrices):
    qkv, out, up, down = matrices
    count = lax.axis_size("ctx")
    rows = up.shape[0]
    low = lambda v: v.astype(bf16)
    four = jnp.concatenate([low(qkv), low(out).T[None]], axis=0)
    attn = four.reshape(4, rows, count, -1).transpose(2, 1, 0, 3).reshape(count, rows, -1)
    up_cut = low(up).reshape(rows, count, -1).transpose(1, 0, 2)
    down_cut = low(down).T.reshape(rows, count, -1).transpose(1, 0, 2)
    return attn, up_cut, down_cut


def finish(name, scale, grads, orthos, moments, weights):
    count, rows, columns = grads.shape
    three = [len(s.shape) == 3 for s in weights]
    tall = [len(s.shape) == 2 and s.shape[0] != rows for s in weights]
    number = len(weights)
    wide = columns // 4 if any(three) else columns
    specs = []
    for is_three, is_tall in zip(three, tall):
        if is_three:
            specs.append(pl.BlockSpec((3, rows, wide), lambda i: (0, 0, i)))
        elif is_tall:
            specs.append(pl.BlockSpec((wide, rows), lambda i: (i, 0)))
        else:
            specs.append(pl.BlockSpec((rows, wide), lambda i: (0, i)))

    def kernel(grad_ref, ortho_ref, *refs):
        for j in range(number):
            moment, weight = refs[j], refs[number + j]
            grad_out, state_out, master_out = refs[2 * number + 3 * j : 2 * number + 3 * j + 3]
            for w in range(3) if three[j] else (None,):
                start = (3 if w is None and any(three) else w or 0) * wide
                cut = lambda ref: ref[0, :, start : start + wide].astype(f32)
                grad, ortho = cut(grad_ref), cut(ortho_ref)
                if tall[j]:
                    grad, ortho = grad.T, ortho.T
                at = ... if w is None else w
                grad_out[at] = grad
                state_out[at] = decay_rate * moment[at] + grad
                master_out[at] = weight[at] - scale * ortho

    outs = pl.pallas_call(
        kernel,
        out_shape=[jax.ShapeDtypeStruct(s.shape, f32) for s in weights for _ in range(3)],
        grid=(count,),
        in_specs=[*[pl.BlockSpec((1, rows, columns), lambda i: (i, 0, 0))] * 2, *specs, *specs],
        out_specs=[spec for spec in specs for _ in range(3)],
        compiler_params=pltpu.CompilerParams(vmem_limit_bytes=32 << 20),
        cost_estimate=pl.CostEstimate(
            flops=4 * grads.size, bytes_accessed=24 * grads.size, transcendentals=0
        ),
        name=name,
    )(grads, orthos, *moments, *weights)
    return outs[0::3], outs[1::3], outs[2::3]


def over_ctx(stack):
    return lax.all_to_all(stack, "ctx", split_axis=0, concat_axis=0, tiled=True)


def to_blocks(stack):
    moved = over_ctx(stack)
    return moved.reshape(-1, moved.shape[-1])


def from_blocks(block):
    return over_ctx(block.reshape(lax.axis_size("ctx"), -1, block.shape[-1]))


def body(
    inputs,
    segment_ids,
    cotangent,
    w_qkv,
    w_out,
    w_up,
    w_down,
    bias_qv,
    bias_up,
    bias_res,
    norm_gain,
    norm_shift,
    moment_qkv,
    moment_out,
    moment_up,
    moment_down,
    moment_bqv,
    moment_bup,
    moment_bres,
    moment_gain,
    moment_shift,
):
    count_c = lax.axis_size("ctx")
    count_f = lax.axis_size("fsdp")
    c = lax.axis_index("ctx")
    t = lax.axis_index("tp")
    rows = inputs.shape[2]
    width = inputs.shape[3]
    length = rows * count_c
    token_total = inputs.shape[0] * inputs.shape[1] * count_f * length
    e = w_qkv.shape[2] // count_c
    u = w_up.shape[1] // count_c

    own_micro = lambda v: lax.dynamic_index_in_dim(v, t, 0, keepdims=False)[0]
    row_low = own_micro(inputs)
    upper = own_micro(cotangent)
    segments = own_micro(segment_ids)
    index = jnp.arange(count_c)
    order = index ^ c if count_c == 4 else index
    place = (segments * (length + HALF + 1) + jnp.arange(length, dtype=jnp.int32)).reshape(count_c, rows)
    place = jnp.take(place, order, axis=0).reshape(length)

    after = lambda value, *others: lax.optimization_barrier((value, *others))[0]
    attn_stack, up_stack, down_stack = pack((w_qkv, w_out, w_up, w_down))
    attn_block = to_blocks(attn_stack)
    gather_z = lambda v: lax.all_gather(v, "fsdp", axis=0, tiled=True)
    xs = jnp.concatenate(spread(after(row_low, attn_block)), axis=0)
    both_block = to_blocks(after(jnp.concatenate([up_stack, down_stack], axis=2), xs))
    up_block, down_block = both_block[:, :u], both_block[:, u:]
    attn_g, up_g, down_g = map(gather_z, (attn_block, up_block, down_block))
    moment_stack = jnp.concatenate(pack((moment_qkv, moment_out, moment_up, moment_down)), axis=2)
    moment_stack = after(moment_stack, both_block)
    attn_g = after(attn_g, moment_stack)
    attn_w = (attn_g, swap_core(attn_g))

    bias_q = lax.dynamic_slice_in_dim(bias_qv, c * e, e, 1)
    bias_u = lax.dynamic_slice_in_dim(bias_up, c * u, u, 0)
    small = jnp.concatenate([bias_q.reshape(-1), bias_u])
    small_pair = (small, swap_core(small))
    cores = range(2)

    qkv = []
    for i in cores:
        shift = jnp.concatenate([small_pair[i][:e], jnp.zeros((e,), f32), small_pair[i][e : 2 * e]])
        qkv.append((mm(xs, attn_w[i][:, : 3 * e], (1, 0)) + shift).astype(bf16))
    context = [attend_forward(qkv[i], place) for i in cores]
    part = sum(mm(context[i], attn_w[i][:, 3 * e :], (1, 1)) for i in cores).astype(bf16)
    row = lambda matrix, index: matrix[index : index + 1]
    first_all, (first_unit, first_inverse), _ = exchange(
        "first_rows",
        1,
        first_step,
        part,
        [row_low],
        [row(bias_res, 0), row(norm_gain, 0), row(norm_shift, 0)],
        [f32, f32],
        0,
    )
    moment_block = to_blocks(after(moment_stack, first_all))
    moments = [moment_block[:, : 4 * e], moment_block[:, 4 * e : 4 * e + u], moment_block[:, 4 * e + u :]]
    up_g = after(up_g, first_all)
    up_w = (up_g, swap_core(up_g))
    pre_act = [mm(first_all, up_w[i], (1, 0)) + small_pair[i][2 * e :] for i in cores]
    active = [gelu_tanh(p).astype(bf16) for p in pre_act]
    down_g = after(down_g, moment_block, *active)
    down_w = (down_g, swap_core(down_g))
    part = sum(mm(active[i], down_w[i], (1, 1)) for i in cores).astype(bf16)
    branch_all, (out_rows, grad_second), second_sums = exchange(
        "second_rows",
        2,
        second_step,
        part,
        [first_unit, upper],
        [row(bias_res, 1), row(norm_gain, 0), row(norm_shift, 0), row(norm_gain, 1), row(norm_shift, 1)],
        [bf16, f32],
        3,
    )

    def pair_sum(terms):
        return (terms[0] + swap_core(terms[1].astype(bf16)).astype(f32)).astype(bf16)

    scatter_z = lambda v: lax.psum_scatter(v, "fsdp", scatter_dimension=0, tiled=True)
    term_down = [None, mm(branch_all, active[1], (0, 0)).astype(bf16)]
    term_down[0] = mm(after(branch_all, term_down[1]), active[0], (0, 0))
    branch_all, *term_down = lax.optimization_barrier((branch_all, *term_down))
    down_sum = pair_sum(term_down)

    def before_gelu(i, rows):
        return jax.vjp(gelu_tanh, pre_act[i])[1](mm(rows, down_w[i], (1, 0)))[0].astype(bf16)

    grad_pre = [before_gelu(0, branch_all)]
    branch_all, down_sum, grad_pre[0] = lax.optimization_barrier((branch_all, down_sum, grad_pre[0]))
    grad_pre.append(before_gelu(1, branch_all))
    part = sum(mm(grad_pre[i], up_w[i], (1, 1)) for i in cores).astype(bf16)
    term_up = [None, mm(first_all, grad_pre[1], (0, 0)).astype(bf16)]
    term_up[0] = mm(after(first_all, term_up[1]), grad_pre[0], (0, 0))
    part, up_sum = lax.optimization_barrier((part, pair_sum(term_up)))
    attended_all, (grad_first,), first_sums = exchange(
        "third_rows",
        3,
        third_step,
        part,
        [first_unit, first_inverse, grad_second],
        [row(norm_gain, 0)],
        [f32],
        3,
    )
    grad_qkv_low, term_attn = [None, None], [None, None]
    rows_for = attended_all
    for i in (1, 0):
        grad_context = mm(rows_for, attn_w[i][:, 3 * e :], (1, 0)).astype(bf16)
        grad_qkv_low[i] = attend_backward(qkv[i], grad_context, place)
        term_attn[i] = jnp.concatenate(
            [mm(xs, grad_qkv_low[i], (0, 0)), mm(rows_for, context[i], (0, 0))], axis=1
        )
        if i:
            term_attn[i] = term_attn[i].astype(bf16)
            rows_for = after(attended_all, term_attn[i])
    attn_sum = pair_sum(term_attn)
    *lows, attn_sum = lax.optimization_barrier((*grad_qkv_low, attn_sum))
    part = sum(mm(lows[i], attn_w[i][:, : 3 * e], (1, 1)) for i in cores).astype(bf16)

    qv_sums = []
    for i in cores:
        sums_i = jnp.sum(grad_qkv_low[i].astype(f32), axis=0)
        qv_sums.append(jnp.stack([sums_i[:e], sums_i[2 * e :]]))
    up_sums = [jnp.sum(g.astype(f32), axis=0) for g in grad_pre]
    side = lambda pair: [jnp.where(t == m, pair[0], pair[1]) for m in range(2)]
    bqv_all = jnp.stack(
        [
            lax.dynamic_update_slice_in_dim(jnp.zeros((2, count_c * e), f32), v, c * e, 1)
            for v in side(qv_sums)
        ]
    )
    bup_all = jnp.stack(
        [
            lax.dynamic_update_slice_in_dim(jnp.zeros((count_c * u,), f32), v, c * u, 0)
            for v in side(up_sums)
        ]
    )
    rest = jnp.concatenate(
        [
            first_sums[2],
            second_sums[2],
            first_sums[0],
            second_sums[0],
            first_sums[1],
            second_sums[1],
        ],
        axis=0,
    )
    flat = jnp.concatenate([bqv_all.reshape(-1), bup_all.reshape(-1), rest.reshape(-1)])

    down_total, up_total, attn_total = map(scatter_z, (down_sum, up_sum, attn_sum))
    step_scale = matrix_rate * math.sqrt(width / HDIM)
    (up_blocks, down_blocks), input_rows, flat = gradients_and_orthogonal(
        "feed_forward_slabs",
        4,
        (moments[1], moments[2]),
        (up_total, down_total),
        part,
        grad_first,
        flat,
    )
    attn_total = after(attn_total, input_rows)
    (attn_blocks,), *_ = gradients_and_orthogonal("attention_slabs", 5, moments[:1], (attn_total,))
    up_done = finish("up_finish", step_scale, *up_blocks, (moment_up,), (w_up,))
    down_done = finish("down_finish", step_scale, *down_blocks, (moment_down,), (w_down,))
    attn_done = finish(
        "attention_finish", step_scale, *attn_blocks, (moment_qkv, moment_out), (w_qkv, w_out)
    )
    grads, states, masters = [
        [*attn_done[k], *up_done[k], *down_done[k]] for k in range(3)
    ]

    both = lambda own, other: jnp.stack([jnp.where(t == m, own, other) for m in range(2)])[:, None]
    layer_out = both(out_rows, swap_core(out_rows))
    input_grad = both(input_rows, swap_core(input_rows))

    cut = bqv_all.size
    cut_two = cut + bup_all.size
    grad_bqv = lax.dynamic_index_in_dim(flat[:cut].reshape(bqv_all.shape), t, 0, keepdims=False)
    grad_bup = lax.dynamic_index_in_dim(flat[cut:cut_two].reshape(bup_all.shape), t, 0, keepdims=False)
    rest = flat[cut_two:].reshape(3, 2, width)
    vector_grads = (grad_bqv, grad_bup, rest[0], rest[1], rest[2])
    vector_states = [
        decay_rate * m + g
        for m, g in zip(
            (moment_bqv, moment_bup, moment_bres, moment_gain, moment_shift), vector_grads
        )
    ]
    vector_step = 1.0 / math.sqrt(token_total)
    vector_masters = [
        v - vector_step * s
        for v, s in zip((bias_qv, bias_up, bias_res, norm_gain, norm_shift), vector_states)
    ]
    return (
        layer_out,
        input_grad,
        *grads,
        *vector_grads,
        *states,
        *vector_states,
        *masters,
        *vector_masters,
    )


def solution(mesh):
    rows = P(None, "fsdp", "ctx", None)
    matrices = (
        P(None, ("fsdp", "ctx"), "tp"),
        P("tp", ("fsdp", "ctx")),
        P(("fsdp", "ctx"), "tp"),
        P("tp", ("fsdp", "ctx")),
    )
    vectors = (P(None, "tp"), P("tp"), P(), P(), P())
    return jax.shard_map(
        body,
        mesh=mesh,
        in_specs=(rows, P(None, "fsdp", None), rows, *matrices, *vectors, *matrices, *vectors),
        out_specs=(rows, rows, *((*matrices, *vectors) * 3)),
        check_vma=False,
    )
```

```python
import math

import jax
import jax.numpy as jnp
from jax import lax
from jax.experimental import pallas as pl
from jax.experimental.pallas import tpu as pltpu
from jax.sharding import PartitionSpec as P

HDIM = 128
NS_STEPS = 5
HALF = 512

bf16 = jnp.bfloat16
f32 = jnp.float32
highest = lax.Precision.HIGHEST
norm_epsilon = 1e-05
ortho_epsilon = 1e-07
coef_first = 3.4445
coef_second = -4.775
coef_third = 2.0315
decay_rate = 0.5
matrix_rate = 0.25
masked_value = -1e30

CORE = [(0, 1), (1, 0)]


def xor_pairs(size, mask):
    return [(i, i ^ mask) for i in range(size)]


def swap_core(value):
    return lax.ppermute(value, "tp", CORE)


def swap_ctx(value, mask):
    return lax.ppermute(value, "ctx", xor_pairs(4, mask))


def swap_fsdp(value, mask):
    return lax.ppermute(value, "fsdp", xor_pairs(4, mask))


def mm(left, right, dims):
    return lax.dot_general(left, right, ((dims[:1], dims[1:]), ((), ())), preferred_element_type=f32)


def spread(own):
    if lax.axis_size("ctx") != 4:
        whole = lax.all_gather(own, "ctx", axis=0, tiled=False)
        return [whole[i] for i in range(whole.shape[0])]
    half = own.shape[0] // 2
    from_x = swap_ctx(own, 1)
    from_y = swap_ctx(own, 2)
    top = swap_ctx(from_x[:half], 2)
    low = swap_ctx(from_y[half:], 1)
    return [own, from_x, from_y, jnp.concatenate([top, low], axis=0)]


def collect(partial):
    count = lax.axis_size("ctx")
    rows = partial.shape[0] // count
    if count != 4:
        return lax.psum_scatter(partial, "ctx", scatter_dimension=0, tiled=True).astype(f32)
    half = rows // 2
    part = [partial[k * rows : (k + 1) * rows] for k in range(4)]
    over_x = swap_ctx(jnp.concatenate([part[1][:half], part[3][:half]], axis=0), 1).astype(f32)
    over_y = swap_ctx(jnp.concatenate([part[2][half:], part[3][half:]], axis=0), 2).astype(f32)
    then_y = swap_ctx((part[2][:half].astype(f32) + over_x[half:]).astype(bf16), 2)
    then_x = swap_ctx((part[1][half:].astype(f32) + over_y[half:]).astype(bf16), 1)
    own = part[0].astype(f32)
    return jnp.concatenate(
        [
            own[:half] + over_x[:half] + then_y.astype(f32),
            own[half:] + over_y[:half] + then_x.astype(f32),
        ],
        axis=0,
    )


def layer_norm(values, gain_row, shift_row):
    center = values - jnp.mean(values, axis=-1, keepdims=True)
    inverse = lax.rsqrt(jnp.mean(center * center, axis=-1, keepdims=True) + norm_epsilon)
    normed = center * inverse
    return (normed * gain_row + shift_row, normed, inverse)


def layer_norm_back(grad_upper, normed, inverse, gain_row):
    grad_normed = grad_upper * gain_row
    mean_grad = jnp.mean(grad_normed, axis=-1, keepdims=True)
    mean_dot = jnp.mean(grad_normed * normed, axis=-1, keepdims=True)
    return inverse * (grad_normed - mean_grad - normed * mean_dot)


def gelu_tanh(values):
    return jax.nn.gelu(values, approximate=True)


MESH = pl.DeviceIdType.MESH


def remote(source, target, send, receive, axis, index):
    return pltpu.make_async_remote_copy(
        src_ref=source,
        dst_ref=target,
        send_sem=send,
        recv_sem=receive,
        device_id={axis: index},
        device_id_type=MESH,
    )


def greet(axis_indices):
    barrier = pltpu.get_barrier_semaphore()
    for axis, index in axis_indices:
        pl.semaphore_signal(barrier, inc=1, device_id={axis: index}, device_id_type=MESH)
    pl.semaphore_wait(barrier, len(axis_indices))


def staged(kernel, count, n_in, n_out):
    def run(*refs):
        given, others, rest = refs[:count], refs[count : n_in + n_out], refs[n_in + n_out :]
        slots, sems, rest = rest[:count], rest[count], rest[count + 1 :]
        copies = [pltpu.make_async_copy(g, v, sems.at[k]) for k, (g, v) in enumerate(zip(given, slots))]
        for one in copies:
            one.start()

        def ready(first, last):
            for one in copies[first:last]:
                one.wait()

        kernel(given, ready, *slots, *others, *rest)

    return run


def slots_for(operands):
    return [
        *[pltpu.VMEM(o.shape, o.dtype) for o in operands],
        pltpu.SemaphoreType.DMA((len(operands),)),
    ]


class RowSums:
    def __init__(self, part, from_x, from_y, then_y, then_x, to_y, to_x, send, receive):
        self.part, self.send, self.receive = part, send, receive
        self.from_x, self.from_y, self.then_y, self.then_x = from_x, from_y, then_y, then_x
        self.to_y, self.to_x = to_y, to_x
        self.pieces, self.count = to_y.shape[:2]
        self.span = [pl.ds(j * self.count, self.count) for j in range(self.pieces)]
        c = lax.axis_index("ctx")
        self.x_side = c + 1 - 2 * (c % 2)
        self.y_side = c + 2 - 4 * (c // 2)
        self.one, self.two = [], []

    def copy(self, stage, j, source, target, side):
        copy = remote(source, target, self.send.at[stage, j], self.receive.at[stage, j], "ctx", side)
        copy.start()
        return copy

    def first(self, part):
        for j in range(self.pieces):
            self.one.append(
                (
                    self.copy(0, j, part.at[:, 1, 0, self.span[j]], self.from_x.at[j], self.x_side),
                    self.copy(1, j, part.at[1, :, 1, self.span[j]], self.from_y.at[j], self.y_side),
                )
            )

    def second(self):
        for j in range(self.pieces):
            at = self.span[j]
            self.one[j][0].wait_recv()
            value = self.part[1, 0, 0, at].astype(f32) + self.from_x[j, 1].astype(f32)
            self.to_y[j] = value.astype(bf16)
            over_y = self.copy(2, j, self.to_y.at[j], self.then_y.at[j], self.y_side)
            self.one[j][1].wait_recv()
            value = self.part[0, 1, 1, at].astype(f32) + self.from_y[j, 1].astype(f32)
            self.to_x[j] = value.astype(bf16)
            over_x = self.copy(3, j, self.to_x.at[j], self.then_x.at[j], self.x_side)
            self.two.append((over_y, over_x))

    def third(self, j):
        at = self.span[j]
        self.two[j][0].wait_recv()
        self.two[j][1].wait_recv()
        top = self.part[0, 0, 0, at].astype(f32) + self.from_x[j, 0].astype(f32)
        low = self.part[0, 0, 1, at].astype(f32) + self.from_y[j, 0].astype(f32)
        top = top + self.then_y[j].astype(f32)
        low = low + self.then_x[j].astype(f32)
        return at, jnp.concatenate([top, low], axis=0)

    def end(self):
        for pair in (*self.one, *self.two):
            for one in pair:
                one.wait_send()


def row_scratch(half, width, pieces=4):
    count = half // pieces
    return [
        pltpu.VMEM((pieces, 2, count, width), bf16),
        pltpu.VMEM((pieces, 2, count, width), bf16),
        *[pltpu.VMEM((pieces, count, width), bf16)] * 4,
        pltpu.SemaphoreType.DMA((4, pieces)),
        pltpu.SemaphoreType.DMA((4, pieces)),
    ]


def exchange_kernel(step, n_in, n_vec, n_out, n_sum, given, ready, *refs):
    part = refs[0]
    ins = refs[1 : 1 + n_in]
    vectors = refs[1 + n_in : 1 + n_in + n_vec]
    rest = refs[1 + n_in + n_vec :]
    whole = rest[0]
    outs = rest[1 : 1 + n_out]
    sums_ref = rest[1 + n_out]
    own, send, receive, local = rest[2 + n_out : 6 + n_out]
    row_sums = RowSums(part, *rest[6 + n_out :])
    x_side, y_side, span, count = row_sums.x_side, row_sums.y_side, row_sums.span, row_sums.count
    greet([("ctx", x_side), ("ctx", y_side)])

    def copy(stage, j, source, target, side):
        one = remote(source, target, send.at[stage, j], receive.at[stage, j], "ctx", side)
        one.start()
        return one

    row_sums.first(given[0])
    ready(0, 1)
    row_sums.second()
    ready(1, 1 + n_in)
    params = [v[...] for v in vectors]
    third, fourth, kept = [], [], []
    totals = None
    for j in range(row_sums.pieces):
        at, total = row_sums.third(j)
        both = lambda ref: jnp.concatenate([ref[0, at], ref[1, at]], axis=0)
        sent, rows, sums = step(total, [both(r) for r in ins], params)
        own[0, at] = sent[:count]
        own[1, at] = sent[count:]
        third.append(
            (
                copy(0, j, own.at[:, at], whole.at[1, :, at], x_side),
                copy(1, j, own.at[:, at], whole.at[2, :, at], y_side),
            )
        )
        keep = pltpu.make_async_copy(own.at[:, at], whole.at[0, :, at], local.at[j])
        keep.start()
        kept.append(keep)
        for out, value in zip(outs, rows):
            out[0, at] = value[:count]
            out[1, at] = value[count:]
        totals = sums if totals is None else [a + b for a, b in zip(totals, sums)]
    for k in range(n_sum):
        sums_ref[k : k + 1] = totals[k]
    for j, at in enumerate(span):
        third[j][0].wait_recv()
        over_y = copy(2, j, whole.at[1, 0, at], whole.at[3, 0, at], y_side)
        third[j][1].wait_recv()
        over_x = copy(3, j, whole.at[2, 1, at], whole.at[3, 1, at], x_side)
        fourth.append((over_y, over_x))
    row_sums.end()
    for pair in third:
        for one in pair:
            one.wait_send()
    for pair in fourth:
        for one in pair:
            one.wait()
    for one in kept:
        one.wait()


def exchange(name, number, step, part, ins, vectors, out_types, n_sum):
    rows, width = ins[0].shape
    if lax.axis_size("ctx") != 4 or rows % 128:
        sent, outs, sums = step(collect(part), ins, vectors)
        return jnp.concatenate(spread(sent), axis=0), outs, sums
    pieces = 4
    half = rows // 2
    vmem = pl.BlockSpec(memory_space=pltpu.VMEM)
    halves = lambda v: v.reshape(2, half, width)
    anywhere = pl.BlockSpec(memory_space=pl.ANY)
    operands = [part.reshape(2, 2, 2, half, width), *map(halves, ins)]
    n_in = len(operands) + len(vectors)

    def kernel(*refs):
        exchange_kernel(step, len(ins), len(vectors), len(out_types), n_sum, *refs)

    whole, *outs, sums = pl.pallas_call(
        staged(kernel, len(operands), n_in, 2 + len(out_types)),
        out_shape=[
            jax.ShapeDtypeStruct((4, 2, half, width), bf16),
            *[jax.ShapeDtypeStruct((2, half, width), d) for d in out_types],
            jax.ShapeDtypeStruct((8, width), f32),
        ],
        in_specs=[*[anywhere] * len(operands), *[vmem] * len(vectors)],
        out_specs=[anywhere, *[vmem] * (len(out_types) + 1)],
        scratch_shapes=[
            *slots_for(operands),
            pltpu.VMEM((2, half, width), bf16),
            pltpu.SemaphoreType.DMA((4, pieces)),
            pltpu.SemaphoreType.DMA((4, pieces)),
            pltpu.SemaphoreType.DMA((pieces,)),
            *row_scratch(half, width, pieces),
        ],
        compiler_params=pltpu.CompilerParams(
            collective_id=number, has_side_effects=True, vmem_limit_bytes=56 << 20
        ),
        cost_estimate=pl.CostEstimate(
            flops=60 * rows * width, bytes_accessed=130 << 20, transcendentals=0
        ),
        name=name,
    )(*operands, *vectors)
    return (
        whole.reshape(4 * rows, width),
        [o.reshape(rows, width) for o in outs],
        [sums[k : k + 1] for k in range(n_sum)],
    )


def column_sum(values):
    return jnp.sum(values, axis=0, keepdims=True)


def first_step(total, rows, vectors):
    bias, gain, shift = vectors
    first, unit, inverse = layer_norm(rows[0].astype(f32) + total + bias, gain, shift)
    return first.astype(bf16), [unit, jnp.broadcast_to(inverse, unit.shape)], []


def second_step(total, rows, vectors):
    bias, gain_one, shift_one, gain, shift = vectors
    first = rows[0] * gain_one + shift_one
    out, unit, inverse = layer_norm(first + total + bias, gain, shift)
    upper = rows[1].astype(f32)
    grad = layer_norm_back(upper, unit, inverse, gain)
    low = grad.astype(bf16)
    sums = [column_sum(upper * unit), column_sum(upper), column_sum(low.astype(f32))]
    return low, [out.astype(bf16), grad], sums


def third_step(total, rows, vectors):
    (gain,) = vectors
    unit, inverse, upper = rows
    upper = upper + total
    grad = layer_norm_back(upper, unit, inverse, gain)
    low = grad.astype(bf16)
    sums = [column_sum(upper * unit), column_sum(upper), column_sum(low.astype(f32))]
    return low, [grad], sums


def block_weights(query, keys, place_rows, place_cols):
    scores = mm(query, keys, (1, 1))
    scores = jnp.where(jnp.abs(place_rows - place_cols) <= HALF, scores, masked_value)
    top = jnp.max(scores, axis=-1, keepdims=True)
    weights = jnp.exp((scores - top) * HDIM**-0.5)
    return weights, 1.0 / jnp.sum(weights, axis=-1, keepdims=True)


def attend_kernel(block, q_ref, k_ref, v_ref, rows_ref, cols_ref, out_ref):
    for start in range(0, q_ref.shape[0], block):
        span = pl.ds(start, block)
        weights, inverse = block_weights(q_ref[span, :], k_ref[...], rows_ref[span, :], cols_ref[...])
        out_ref[span, :] = (mm(weights.astype(bf16), v_ref[...], (1, 0)) * inverse).astype(bf16)


def attend_forward(qkv, place):
    length = qkv.shape[0]
    heads = qkv.shape[1] // (3 * HDIM)
    piece = lambda which: pl.BlockSpec((length, HDIM), lambda h, w=which: (0, w * heads + h))
    return pl.pallas_call(
        lambda *refs: attend_kernel(256, *refs),
        out_shape=jax.ShapeDtypeStruct((length, heads * HDIM), bf16),
        grid=(heads,),
        in_specs=[
            piece(0),
            piece(1),
            piece(2),
            pl.BlockSpec((length, 1), lambda h: (0, 0)),
            pl.BlockSpec((1, length), lambda h: (0, 0)),
        ],
        out_specs=pl.BlockSpec((length, HDIM), lambda h: (0, h)),
        compiler_params=pltpu.CompilerParams(vmem_limit_bytes=40 << 20),
        cost_estimate=pl.CostEstimate(
            flops=4 * heads * length * length * HDIM,
            bytes_accessed=8 * heads * length * HDIM,
            transcendentals=heads * length * length,
        ),
        name="attend_forward",
    )(qkv, qkv, qkv, place[:, None], place[None, :])


def attend_back_kernel(
    block, heads, q_ref, k_ref, v_ref, up_ref, rows_ref, cols_ref, out_ref, sum_k, sum_v
):
    scale = HDIM**-0.5
    head = pl.program_id(0)
    column = lambda which: pl.ds(pl.multiple_of((which * heads + head) * HDIM, HDIM), HDIM)
    for start in range(0, q_ref.shape[0], block):
        span = pl.ds(start, block)
        query = q_ref[span, :]
        upper = up_ref[span, :]
        weights, inverse = block_weights(query, k_ref[...], rows_ref[span, :], cols_ref[...])
        probs = weights * inverse
        grad_probs = mm(upper, v_ref[...], (1, 1))
        inner = jnp.sum(probs * grad_probs, axis=-1, keepdims=True)
        grad_scores = (probs * (grad_probs - inner)).astype(bf16)
        out_ref[span, column(0)] = (mm(grad_scores, k_ref[...], (1, 0)) * scale).astype(bf16)
        add_k = mm(grad_scores, query, (0, 0))
        add_v = mm(probs.astype(bf16), upper, (0, 0))
        if start == 0:
            sum_k[...] = add_k
            sum_v[...] = add_v
        else:
            sum_k[...] += add_k
            sum_v[...] += add_v
    out_ref[:, column(1)] = (sum_k[...] * scale).astype(bf16)
    out_ref[:, column(2)] = sum_v[...].astype(bf16)


def attend_backward(qkv, upper, place):
    length = qkv.shape[0]
    heads = qkv.shape[1] // (3 * HDIM)
    piece = lambda which: pl.BlockSpec((length, HDIM), lambda h, w=which: (0, w * heads + h))
    return pl.pallas_call(
        lambda *refs: attend_back_kernel(256, heads, *refs),
        out_shape=jax.ShapeDtypeStruct(qkv.shape, bf16),
        grid=(heads,),
        in_specs=[
            piece(0),
            piece(1),
            piece(2),
            piece(0),
            pl.BlockSpec((length, 1), lambda h: (0, 0)),
            pl.BlockSpec((1, length), lambda h: (0, 0)),
        ],
        out_specs=pl.BlockSpec(qkv.shape, lambda h: (0, 0)),
        scratch_shapes=[pltpu.VMEM((length, HDIM), f32), pltpu.VMEM((length, HDIM), f32)],
        compiler_params=pltpu.CompilerParams(vmem_limit_bytes=48 << 20),
        cost_estimate=pl.CostEstimate(
            flops=10 * heads * length * length * HDIM,
            bytes_accessed=14 * heads * length * HDIM,
            transcendentals=heads * length * length,
        ),
        name="attend_backward",
    )(qkv, qkv, qkv, upper, place[:, None], place[None, :])


def gram_of(moment_ref, total_ref, n):
    span = pl.ds(n * HDIM, HDIM)
    state = decay_rate * moment_ref[:, span].astype(f32) + total_ref[:, span].astype(f32)
    return lax.dot_general(
        state, state, (((0,), (0,)), ((), ())), precision=highest, preferred_element_type=f32
    )


def gram_kernel(moment_ref, total_ref, out_ref):
    for n in range(out_ref.shape[0]):
        out_ref[n] = gram_of(moment_ref, total_ref, n)


def apply_kernel(moment_ref, total_ref, factor_ref, out_ref):
    for n in range(factor_ref.shape[0]):
        span = pl.ds(n * HDIM, HDIM)
        state = decay_rate * moment_ref[:, span].astype(f32) + total_ref[:, span].astype(f32)
        out_ref[:, span] = jnp.dot(
            state, factor_ref[n], precision=highest, preferred_element_type=f32
        ).astype(bf16)


def whole_call(kernel, name, out, *operands, flops):
    vmem = pl.BlockSpec(memory_space=pltpu.VMEM)
    return pl.pallas_call(
        kernel,
        out_shape=out,
        in_specs=[vmem] * len(operands),
        out_specs=vmem,
        compiler_params=pltpu.CompilerParams(vmem_limit_bytes=32 << 20),
        cost_estimate=pl.CostEstimate(
            flops=flops, bytes_accessed=sum(o.size * o.dtype.itemsize for o in operands), transcendentals=0
        ),
        name=name,
    )(*operands)


def polynomial(grams):
    width = grams[0].shape[0]
    same = lax.broadcasted_iota(jnp.int32, (width, width), 0) == lax.broadcasted_iota(
        jnp.int32, (width, width), 1
    )
    unit = same.astype(f32)
    dot = lambda a, b: jnp.dot(a, b, precision=highest, preferred_element_type=f32)
    scaled, totals = [], []
    for gram in grams:
        square = jnp.sum(jnp.sum(gram * unit, axis=1, keepdims=True), axis=0, keepdims=True)
        inverse = 1.0 / (jnp.sqrt(square) + ortho_epsilon)
        scaled.append(gram * (inverse * inverse))
        totals.append(unit * inverse)
    for step in range(NS_STEPS):
        squares = [dot(g, g) for g in scaled]
        polys = [
            coef_first * unit + coef_second * g + coef_third * s for g, s in zip(scaled, squares)
        ]
        totals = [dot(q, p) for q, p in zip(totals, polys)]
        if step + 1 < NS_STEPS:
            halves = [dot(g, p) for g, p in zip(scaled, polys)]
            scaled = [dot(p, h) for p, h in zip(polys, halves)]
    return totals


def polynomial_kernel(gram_ref, out_ref):
    for n, total in enumerate(polynomial([gram_ref[n] for n in range(gram_ref.shape[0])])):
        out_ref[n] = total


def summed_polynomials(moments, totals, grams, pieces, send, receive, keep, between):
    each_group = totals[0].shape[1] // HDIM
    count = grams.shape[0]
    size = min(each_group, count // 2)
    each = size // 4
    f = lax.axis_index("fsdp")
    planes = [(f + i) % 4 for i in range(4)]
    batches = range(count // size)
    copies = []
    for b in batches:
        first = b * size
        for n in range(first, first + size):
            g = n // each_group
            grams[n] = gram_of(moments[g], totals[g], n % each_group)
        copies.append([])
        for i in (1, 2, 3):
            one = remote(
                grams.at[pl.ds(first + planes[i] * each, each)],
                pieces.at[i - 1, pl.ds(b * each, each)],
                send.at[b, i - 1],
                receive.at[b, i - 1],
                "fsdp",
                planes[i],
            )
            one.start()
            copies[b].append(one)
    between()
    for b in batches:
        sums = [grams[b * size + f * each + n] for n in range(each)]
        for i in (1, 2, 3):
            copies[b][i - 1].wait()
            sums = [s + pieces[i - 1, b * each + n] for n, s in enumerate(sums)]
        for n, value in enumerate(polynomial(sums)):
            keep(b, n, value)
        yield b


def rows_to_owners(totals, targets, send, receive, local, first=0):
    rows = totals[0].shape[0] // 4
    c = lax.axis_index("ctx")
    copies = []
    for g, (total, target) in enumerate(zip(totals, targets)):
        for i in (3, 1, 2, 0):
            side = (c + i) % 4
            source = total.at[pl.ds(pl.multiple_of(side * rows, rows), rows)]
            if i:
                sems = send.at[first + g, i - 1], receive.at[first + g, i - 1]
                copies.append(remote(source, target.at[c], *sems, "ctx", side))
            else:
                copies.append(pltpu.make_async_copy(source, target.at[c], local.at[0, g]))
            copies[-1].start()
    return copies


class Chain:
    def __init__(self, b, size, factors, send, receive):
        self.b, self.size, self.factors, self.send, self.receive_sem = b, size, factors, send, receive
        self.f = lax.axis_index("fsdp")

    def copy(self, up, k, block, plane):
        each = self.size // 4
        ref = self.factors.at[pl.ds(self.b * self.size + block * each, each)]
        at = 2 * self.b + up, k
        return remote(ref, ref, self.send.at[at], self.receive_sem.at[at], "fsdp", plane)

    def leaving(self, up, k):
        f = self.f
        return self.copy(up, k, f - k, f + 1) if up else self.copy(up, k, f + k, f - 1)

    def coming(self, up, k):
        f = self.f
        return self.copy(up, k, f - 1 - k, f - 1) if up else self.copy(up, k, f + 1 + k, f + 1)

    def leaves(self, up, k):
        f = self.f
        return jnp.logical_and(f < 3, f >= k) if up else jnp.logical_and(f > 0, f + k <= 3)

    def comes(self, up, k):
        return self.f >= k + 1 if up else self.f <= 2 - k

    def start(self, k):
        for up in (1, 0):
            pl.when(self.leaves(up, k))(lambda up=up: self.leaving(up, k).start())

    def receive(self, k):
        for up in (1, 0):
            pl.when(self.comes(up, k))(lambda up=up: self.coming(up, k).wait_recv())

    def end(self):
        for k in range(3):
            for up in (1, 0):
                pl.when(self.leaves(up, k))(lambda up=up: self.leaving(up, k).wait_send())


def all_sides():
    c, f, t = (lax.axis_index(axis) for axis in ("ctx", "fsdp", "tp"))
    over = [(axis, (at + i) % 4) for axis, at in (("ctx", c), ("fsdp", f)) for i in (1, 2, 3)]
    return [*over, ("tp", 1 - t)]


def share_core(share, shared, send, receive, local):
    t = lax.axis_index("tp")
    copies = [
        remote(share, shared.at[t], send.at[0], receive.at[0], "tp", 1 - t),
        pltpu.make_async_copy(share, shared.at[t], local.at[0]),
    ]
    for one in copies:
        one.start()
    return copies


def feed_forward_kernel(given, ready, *refs):
    moments, totals, (part, base, vector), refs = refs[:2], refs[2:4], refs[4:7], refs[7:]
    share, refs = refs[0], refs[1:]
    (out, *grads), (shared, summed, vector_out), refs = refs[:3], refs[3:6], refs[6:]
    factors, send_c, receive_c, local, send_t, receive_t, local_t, send_f, receive_f = refs[:9]
    gram_refs, (sent_v, got_v, send_v, receive_v), row_refs = refs[9:13], refs[13:17], refs[17:]
    c, f, t = (lax.axis_index(axis) for axis in ("ctx", "fsdp", "tp"))
    partners = [
        ("tp", 1 - t),
        ("ctx", c + 1 - 2 * (c % 2)),
        ("ctx", c + 2 - 4 * (c // 2)),
        ("fsdp", f + 1 - 2 * (f % 2)),
        ("fsdp", f + 2 - 4 * (f // 2)),
    ]
    greet(all_sides())
    vector_copies = []

    def vector_start(k):
        one = remote(sent_v.at[k], got_v.at[k], send_v.at[k], receive_v.at[k], *partners[k])
        one.start()
        vector_copies.append(one)

    def vector_next(k):
        vector_copies[k].wait_recv()
        if k < 4:
            sent_v[k + 1] = sent_v[k] + got_v[k]
            vector_start(k + 1)
        else:
            vector_out[...] = sent_v[k] + got_v[k]

    sum_rows = RowSums(part, *row_refs)
    sum_rows.first(given[4])
    ready(0, 8)
    started = rows_to_owners(totals, grads, send_c, receive_c, local)
    started += share_core(share, shared, send_t, receive_t, local_t)
    sent_v[0] = vector[...]
    vector_start(0)
    size = totals[0].shape[1] // HDIM
    each = size // 4
    chains = [Chain(b, size, factors, send_f, receive_f) for b in range(2)]

    def keep(b, n, value):
        factors[b * size + f * each + n] = value

    def between():
        vector_next(0)
        sum_rows.second()
        vector_next(1)

    for b in summed_polynomials(moments, totals, *gram_refs, keep, between):
        chains[b].start(0)
    vector_next(2)
    for j in range(sum_rows.pieces):
        span, total = sum_rows.third(j)
        for h in range(2):
            value = total[h * sum_rows.count : (h + 1) * sum_rows.count]
            summed[h, span] = base[h, span] + value
    for k in range(3):
        for chain in chains:
            chain.receive(k)
            if k < 2:
                chain.start(k + 1)
        if k == 0:
            vector_next(3)
    out[...] = factors[...]
    vector_next(4)
    for chain in chains:
        chain.end()
    for one in vector_copies:
        one.wait_send()
    for one in started:
        one.wait()
    sum_rows.end()


def last_kernel(given, ready, *refs):
    moments, totals, (others, share), refs = refs[:3], refs[3:6], refs[6:8], refs[8:]
    orthos, (grads, shared), refs = refs[:3], refs[3:5], refs[5:]
    factors, stage, send_c, receive_c, local, send_t, receive_t, local_t, send_f, receive_f = refs[:10]
    gram_refs = refs[10:]
    rows = totals[0].shape[0] // 4
    count = totals[0].shape[1] // HDIM
    c, f = lax.axis_index("ctx"), lax.axis_index("fsdp")
    greet(all_sides())
    ready(0, 8)
    started = rows_to_owners(totals[:1], [grads], send_c, receive_c, local)
    started += share_core(share, shared, send_t, receive_t, local_t)

    def send_ortho(g, first, size, kind, factor):
        wide = pl.ds(first * HDIM, size * HDIM)
        for i in (3, 1, 2, 0):
            side = (c + i) % 4
            span = pl.ds(pl.multiple_of(side * rows, rows), rows)
            for n in range(first, first + size):
                column = pl.ds(n * HDIM, HDIM)
                state = decay_rate * moments[g][span, column].astype(f32)
                state = state + totals[g][span, column].astype(f32)
                stage[g, i, :, column] = jnp.dot(
                    state, factor(n), precision=highest, preferred_element_type=f32
                ).astype(bf16)
            source, target = stage.at[g, i, :, wide], orthos[g].at[c, :, wide]
            if i:
                sems = send_c.at[kind, i - 1], receive_c.at[kind, i - 1]
                copy = remote(source, target, *sems, "ctx", side)
            else:
                copy = pltpu.make_async_copy(source, target, local.at[0, kind])
            copy.start()
            started.append(copy)

    def between():
        for g in (1, 2):
            send_ortho(g, 0, count, g, lambda n: others[(g - 1) * count + n])

    size = count // 2
    each = size // 4
    chains = [Chain(b, size, factors, send_f, receive_f) for b in range(2)]

    def keep(b, n, value):
        factors[b * size + f * each + n] = value

    for b in summed_polynomials(moments[:1], totals[:1], *gram_refs, keep, between):
        chains[b].start(0)
    for k in range(2):
        for chain in chains:
            chain.receive(k)
            chain.start(k + 1)
    for b, chain in enumerate(chains):
        chain.receive(2)
        send_ortho(0, b * size, size, 3 + b, lambda n: factors[n])
    for chain in chains:
        chain.end()
    for one in started:
        one.wait()


def fits_planes(columns):
    return lax.axis_size("fsdp") == 4 and lax.axis_size("ctx") == 4 and columns == 8 * HDIM


def polynomials_over_planes(moment, total):
    count = total.shape[1] // HDIM
    flops = 12 * total.size * HDIM
    shape = jax.ShapeDtypeStruct((count, HDIM, HDIM), f32)
    grams = whole_call(gram_kernel, "grams", shape, moment, total, flops=flops)
    summed = lax.psum(grams, "fsdp")
    return whole_call(polynomial_kernel, "polynomials", shape, summed, flops=flops)


def shared_by_cores(share):
    other, t = swap_core(share), lax.axis_index("tp")
    return jnp.stack([jnp.where(t == m, share, other) for m in range(2)])


def feed_forward_slabs(moments, totals, share, part, base, vector):
    rows, columns = totals[0].shape
    if not fits_planes(columns):
        factors = [polynomials_over_planes(m, v) for m, v in zip(moments, totals)]
        summed = lax.psum(vector, ("fsdp", "ctx", "tp"))
        blocks = [from_blocks(v) for v in totals]
        return factors, blocks, shared_by_cores(share), base + collect(part), summed
    count = 2 * columns // HDIM
    vmem = pl.BlockSpec(memory_space=pltpu.VMEM)
    anywhere = pl.BlockSpec(memory_space=pl.ANY)
    block = jax.ShapeDtypeStruct((4, rows // 4, columns), bf16)
    half, width = base.shape[0] // 2, base.shape[1]
    lines = vector.size // HDIM
    dma = pltpu.SemaphoreType.DMA
    operands = [
        *moments,
        *totals,
        part.reshape(2, 2, 2, half, width),
        base.reshape(2, half, width),
        vector.reshape(lines, HDIM),
        share,
    ]
    factors, up, down, shared, summed, vector_sum = pl.pallas_call(
        staged(feed_forward_kernel, 8, 8, 6),
        out_shape=[
            jax.ShapeDtypeStruct((count, HDIM, HDIM), f32),
            block,
            block,
            jax.ShapeDtypeStruct((2, *share.shape), share.dtype),
            jax.ShapeDtypeStruct((2, half, width), f32),
            jax.ShapeDtypeStruct((lines, HDIM), f32),
        ],
        in_specs=[anywhere] * 8,
        out_specs=[vmem, anywhere, anywhere, anywhere, vmem, vmem],
        scratch_shapes=[
            *slots_for(operands),
            pltpu.VMEM((count, HDIM, HDIM), f32),
            *[dma((2, 3))] * 2,
            dma((1, 2)),
            *[dma((1,))] * 3,
            *[dma((4, 3))] * 2,
            pltpu.VMEM((count, HDIM, HDIM), f32),
            pltpu.VMEM((3, count // 4, HDIM, HDIM), f32),
            *[dma((2, 3))] * 2,
            *[pltpu.VMEM((5, lines, HDIM), f32)] * 2,
            *[dma((5,))] * 2,
            *row_scratch(half, width),
        ],
        compiler_params=pltpu.CompilerParams(
            collective_id=4, has_side_effects=True, vmem_limit_bytes=56 << 20
        ),
        cost_estimate=pl.CostEstimate(
            flops=24 * totals[0].size * HDIM, bytes_accessed=150 << 20, transcendentals=0
        ),
        name="feed_forward_slabs",
    )(*operands)
    return factors, [up, down], shared, summed.reshape(base.shape), vector_sum.reshape(vector.shape)


def last_slabs(moments, totals, factors, share):
    rows, columns = totals[0].shape
    own = jax.ShapeDtypeStruct((rows, columns), bf16)
    if not fits_planes(columns):
        factors = [polynomials_over_planes(moments[0], totals[0]), *factors]
        flops = 12 * totals[0].size * HDIM
        orthos = [
            from_blocks(whole_call(apply_kernel, "apply", own, m, v, p, flops=flops))
            for m, v, p in zip(moments, totals, factors)
        ]
        return orthos, from_blocks(totals[0]), shared_by_cores(share)
    count = columns // HDIM
    anywhere = pl.BlockSpec(memory_space=pl.ANY)
    block = jax.ShapeDtypeStruct((4, rows // 4, columns), bf16)
    dma = pltpu.SemaphoreType.DMA
    operands = [*moments, *totals, factors, share]
    *orthos, grads, shared = pl.pallas_call(
        staged(last_kernel, 8, 8, 5),
        out_shape=[*[block] * 4, jax.ShapeDtypeStruct((2, *share.shape), share.dtype)],
        in_specs=[anywhere] * 8,
        out_specs=[anywhere] * 5,
        scratch_shapes=[
            *slots_for(operands),
            pltpu.VMEM((count, HDIM, HDIM), f32),
            pltpu.VMEM((3, 4, rows // 4, columns), bf16),
            *[dma((5, 3))] * 2,
            dma((1, 5)),
            *[dma((1,))] * 3,
            *[dma((4, 3))] * 2,
            pltpu.VMEM((count, HDIM, HDIM), f32),
            pltpu.VMEM((3, count // 4, HDIM, HDIM), f32),
            *[dma((2, 3))] * 2,
        ],
        compiler_params=pltpu.CompilerParams(
            collective_id=5, has_side_effects=True, vmem_limit_bytes=56 << 20
        ),
        cost_estimate=pl.CostEstimate(
            flops=36 * totals[0].size * HDIM, bytes_accessed=100 << 20, transcendentals=0
        ),
        name="last_slabs",
    )(*operands)
    return orthos, grads, shared


def pack(matrices):
    qkv, out, up, down = matrices
    count = lax.axis_size("ctx")
    rows = up.shape[0]
    low = lambda v: v.astype(bf16)
    four = jnp.concatenate([low(qkv), low(out).T[None]], axis=0)
    attn = four.reshape(4, rows, count, -1).transpose(2, 1, 0, 3).reshape(count, rows, -1)
    up_cut = low(up).reshape(rows, count, -1).transpose(1, 0, 2)
    down_cut = low(down).T.reshape(rows, count, -1).transpose(1, 0, 2)
    return attn, up_cut, down_cut


def finish(name, scale, grads, orthos, moments, weights):
    count, rows, columns = grads.shape
    three = [len(s.shape) == 3 for s in weights]
    tall = [len(s.shape) == 2 and s.shape[0] != rows for s in weights]
    number = len(weights)
    wide = columns // 4 if any(three) else columns
    specs = []
    for is_three, is_tall in zip(three, tall):
        if is_three:
            specs.append(pl.BlockSpec((3, rows, wide), lambda i: (0, 0, i)))
        elif is_tall:
            specs.append(pl.BlockSpec((wide, rows), lambda i: (i, 0)))
        else:
            specs.append(pl.BlockSpec((rows, wide), lambda i: (0, i)))

    def kernel(grad_ref, ortho_ref, *refs):
        for j in range(number):
            moment, weight = refs[j], refs[number + j]
            grad_out, state_out, master_out = refs[2 * number + 3 * j : 2 * number + 3 * j + 3]
            for w in range(3) if three[j] else (None,):
                start = (3 if w is None and any(three) else w or 0) * wide
                cut = lambda ref: ref[0, :, start : start + wide].astype(f32)
                grad, ortho = cut(grad_ref), cut(ortho_ref)
                if tall[j]:
                    grad, ortho = grad.T, ortho.T
                at = ... if w is None else w
                grad_out[at] = grad
                state_out[at] = decay_rate * moment[at] + grad
                master_out[at] = weight[at] - scale * ortho

    outs = pl.pallas_call(
        kernel,
        out_shape=[jax.ShapeDtypeStruct(s.shape, f32) for s in weights for _ in range(3)],
        grid=(count,),
        in_specs=[*[pl.BlockSpec((1, rows, columns), lambda i: (i, 0, 0))] * 2, *specs, *specs],
        out_specs=[spec for spec in specs for _ in range(3)],
        compiler_params=pltpu.CompilerParams(vmem_limit_bytes=56 << 20),
        cost_estimate=pl.CostEstimate(
            flops=4 * grads.size, bytes_accessed=24 * grads.size, transcendentals=0
        ),
        name=name,
    )(grads, orthos, *moments, *weights)
    return outs[0::3], outs[1::3], outs[2::3]


def over_ctx(stack):
    return lax.all_to_all(stack, "ctx", split_axis=0, concat_axis=0, tiled=True)


def to_blocks(stack):
    moved = over_ctx(stack)
    return moved.reshape(-1, moved.shape[-1])


def from_blocks(block):
    return over_ctx(block.reshape(lax.axis_size("ctx"), -1, block.shape[-1]))


def body(
    inputs,
    segment_ids,
    cotangent,
    w_qkv,
    w_out,
    w_up,
    w_down,
    bias_qv,
    bias_up,
    bias_res,
    norm_gain,
    norm_shift,
    moment_qkv,
    moment_out,
    moment_up,
    moment_down,
    moment_bqv,
    moment_bup,
    moment_bres,
    moment_gain,
    moment_shift,
):
    count_c = lax.axis_size("ctx")
    count_f = lax.axis_size("fsdp")
    c = lax.axis_index("ctx")
    t = lax.axis_index("tp")
    rows = inputs.shape[2]
    width = inputs.shape[3]
    length = rows * count_c
    token_total = inputs.shape[0] * inputs.shape[1] * count_f * length
    e = w_qkv.shape[2] // count_c
    u = w_up.shape[1] // count_c

    own_micro = lambda v: lax.dynamic_index_in_dim(v, t, 0, keepdims=False)[0]
    row_low = own_micro(inputs)
    upper = own_micro(cotangent)
    segments = own_micro(segment_ids)
    index = jnp.arange(count_c)
    order = index ^ c if count_c == 4 else index
    place = (segments * (length + HALF + 1) + jnp.arange(length, dtype=jnp.int32)).reshape(count_c, rows)
    place = jnp.take(place, order, axis=0).reshape(length)

    after = lambda value, *others: lax.optimization_barrier((value, *others))[0]
    attn_stack, up_stack, down_stack = pack((w_qkv, w_out, w_up, w_down))
    attn_block = to_blocks(attn_stack)
    gather_z = lambda v: lax.all_gather(v, "fsdp", axis=0, tiled=True)
    xs = jnp.concatenate(spread(after(row_low, attn_block)), axis=0)
    both_block = to_blocks(after(jnp.concatenate([up_stack, down_stack], axis=2), xs))
    up_block, down_block = both_block[:, :u], both_block[:, u:]
    attn_g, up_g, down_g = map(gather_z, (attn_block, up_block, down_block))
    moment_stack = jnp.concatenate(pack((moment_qkv, moment_out, moment_up, moment_down)), axis=2)
    moment_stack = after(moment_stack, both_block)
    attn_g = after(attn_g, moment_stack)
    attn_w = (attn_g, swap_core(attn_g))

    bias_q = lax.dynamic_slice_in_dim(bias_qv, c * e, e, 1)
    bias_u = lax.dynamic_slice_in_dim(bias_up, c * u, u, 0)
    small = jnp.concatenate([bias_q.reshape(-1), bias_u])
    small_pair = (small, swap_core(small))
    cores = range(2)

    qkv = []
    for i in cores:
        shift = jnp.concatenate([small_pair[i][:e], jnp.zeros((e,), f32), small_pair[i][e : 2 * e]])
        qkv.append((mm(xs, attn_w[i][:, : 3 * e], (1, 0)) + shift).astype(bf16))
    context = [attend_forward(qkv[i], place) for i in cores]
    part = sum(mm(context[i], attn_w[i][:, 3 * e :], (1, 1)) for i in cores).astype(bf16)
    row = lambda matrix, index: matrix[index : index + 1]
    first_all, (first_unit, first_inverse), _ = exchange(
        "first_rows",
        1,
        first_step,
        part,
        [row_low],
        [row(bias_res, 0), row(norm_gain, 0), row(norm_shift, 0)],
        [f32, f32],
        0,
    )
    moment_block = to_blocks(after(moment_stack, first_all))
    moments = [moment_block[:, : 4 * e], moment_block[:, 4 * e : 4 * e + u], moment_block[:, 4 * e + u :]]
    up_g = after(up_g, first_all)
    up_w = (up_g, swap_core(up_g))
    pre_act = [mm(first_all, up_w[i], (1, 0)) + small_pair[i][2 * e :] for i in cores]
    active = [gelu_tanh(p).astype(bf16) for p in pre_act]
    down_g = after(down_g, moment_block, *active)
    down_w = (down_g, swap_core(down_g))
    part = sum(mm(active[i], down_w[i], (1, 1)) for i in cores).astype(bf16)
    branch_all, (out_rows, grad_second), second_sums = exchange(
        "second_rows",
        2,
        second_step,
        part,
        [first_unit, upper],
        [row(bias_res, 1), row(norm_gain, 0), row(norm_shift, 0), row(norm_gain, 1), row(norm_shift, 1)],
        [bf16, f32],
        3,
    )

    def pair_sum(terms):
        return (terms[0] + swap_core(terms[1].astype(bf16)).astype(f32)).astype(bf16)

    scatter_z = lambda v: lax.psum_scatter(v, "fsdp", scatter_dimension=0, tiled=True)
    term_down = [None, mm(branch_all, active[1], (0, 0)).astype(bf16)]
    term_down[0] = mm(after(branch_all, term_down[1]), active[0], (0, 0))
    branch_all, *term_down = lax.optimization_barrier((branch_all, *term_down))
    down_sum = pair_sum(term_down)

    def before_gelu(i, rows):
        return jax.vjp(gelu_tanh, pre_act[i])[1](mm(rows, down_w[i], (1, 0)))[0].astype(bf16)

    grad_pre = [before_gelu(0, branch_all)]
    branch_all, down_sum, grad_pre[0] = lax.optimization_barrier((branch_all, down_sum, grad_pre[0]))
    grad_pre.append(before_gelu(1, branch_all))
    part = sum(mm(grad_pre[i], up_w[i], (1, 1)) for i in cores).astype(bf16)
    term_up = [None, mm(first_all, grad_pre[1], (0, 0)).astype(bf16)]
    term_up[0] = mm(after(first_all, term_up[1]), grad_pre[0], (0, 0))
    part, up_sum = lax.optimization_barrier((part, pair_sum(term_up)))
    attended_all, (grad_first,), first_sums = exchange(
        "third_rows",
        3,
        third_step,
        part,
        [first_unit, first_inverse, grad_second],
        [row(norm_gain, 0)],
        [f32],
        3,
    )
    grad_qkv_low, term_qkv, term_out = [None, None], [None, None], [None, None]
    rows_for = attended_all
    for i in (1, 0):
        grad_context = mm(rows_for, attn_w[i][:, 3 * e :], (1, 0)).astype(bf16)
        grad_qkv_low[i] = attend_backward(qkv[i], grad_context, place)
        term_qkv[i] = mm(xs, grad_qkv_low[i], (0, 0))
        term_out[i] = mm(rows_for, context[i], (0, 0))
        if i:
            term_qkv[i], term_out[i] = term_qkv[i].astype(bf16), term_out[i].astype(bf16)
            rows_for = after(attended_all, term_qkv[i], term_out[i])
    attn_sum = jnp.concatenate([pair_sum(term_qkv), pair_sum(term_out)], axis=1)
    down_total, up_total = map(scatter_z, (down_sum, up_sum))
    *lows, attn_sum = lax.optimization_barrier((*grad_qkv_low, attn_sum))
    part = sum(mm(lows[i], attn_w[i][:, : 3 * e], (1, 1)) for i in cores).astype(bf16)

    qv_sums = []
    for i in cores:
        sums_i = jnp.sum(grad_qkv_low[i].astype(f32), axis=0)
        qv_sums.append(jnp.stack([sums_i[:e], sums_i[2 * e :]]))
    up_sums = [jnp.sum(g.astype(f32), axis=0) for g in grad_pre]
    side = lambda pair: [jnp.where(t == m, pair[0], pair[1]) for m in range(2)]
    bqv_all = jnp.stack(
        [
            lax.dynamic_update_slice_in_dim(jnp.zeros((2, count_c * e), f32), v, c * e, 1)
            for v in side(qv_sums)
        ]
    )
    bup_all = jnp.stack(
        [
            lax.dynamic_update_slice_in_dim(jnp.zeros((count_c * u,), f32), v, c * u, 0)
            for v in side(up_sums)
        ]
    )
    rest = jnp.concatenate(
        [
            first_sums[2],
            second_sums[2],
            first_sums[0],
            second_sums[0],
            first_sums[1],
            second_sums[1],
        ],
        axis=0,
    )
    flat = jnp.concatenate([bqv_all.reshape(-1), bup_all.reshape(-1), rest.reshape(-1)])

    attn_total = scatter_z(attn_sum)
    step_scale = matrix_rate * math.sqrt(width / HDIM)
    factors, gradient_blocks, layer_out, input_rows, flat = feed_forward_slabs(
        moments[1:], (up_total, down_total), after(out_rows, attn_sum), part, grad_first, flat
    )
    orthos, attn_gradients, input_grad = last_slabs(
        moments, (attn_total, up_total, down_total), factors, input_rows
    )
    gradient_blocks, flat, orthos = lax.optimization_barrier((gradient_blocks, flat, orthos))
    up_done, down_done = [
        finish(name, step_scale, *operands)
        for name, *operands in (
            ("up_finish", gradient_blocks[0], orthos[1], (moment_up,), (w_up,)),
            ("down_finish", gradient_blocks[1], orthos[2], (moment_down,), (w_down,)),
        )
    ]
    attn_done = finish(
        "attention_finish",
        step_scale,
        attn_gradients,
        orthos[0],
        (moment_qkv, moment_out),
        (w_qkv, w_out),
    )
    grads, states, masters = [
        [*attn_done[k], *up_done[k], *down_done[k]] for k in range(3)
    ]

    cut = bqv_all.size
    cut_two = cut + bup_all.size
    grad_bqv = lax.dynamic_index_in_dim(flat[:cut].reshape(bqv_all.shape), t, 0, keepdims=False)
    grad_bup = lax.dynamic_index_in_dim(flat[cut:cut_two].reshape(bup_all.shape), t, 0, keepdims=False)
    rest = flat[cut_two:].reshape(3, 2, width)
    vector_grads = (grad_bqv, grad_bup, rest[0], rest[1], rest[2])
    vector_states = [
        decay_rate * m + g
        for m, g in zip(
            (moment_bqv, moment_bup, moment_bres, moment_gain, moment_shift), vector_grads
        )
    ]
    vector_step = 1.0 / math.sqrt(token_total)
    vector_masters = [
        v - vector_step * s
        for v, s in zip((bias_qv, bias_up, bias_res, norm_gain, norm_shift), vector_states)
    ]
    return (
        layer_out[:, None],
        input_grad[:, None],
        *grads,
        *vector_grads,
        *states,
        *vector_states,
        *masters,
        *vector_masters,
    )


def solution(mesh):
    rows = P(None, "fsdp", "ctx", None)
    matrices = (
        P(None, ("fsdp", "ctx"), "tp"),
        P("tp", ("fsdp", "ctx")),
        P(("fsdp", "ctx"), "tp"),
        P("tp", ("fsdp", "ctx")),
    )
    vectors = (P(None, "tp"), P("tp"), P(), P(), P())
    return jax.shard_map(
        body,
        mesh=mesh,
        in_specs=(rows, P(None, "fsdp", None), rows, *matrices, *vectors, *matrices, *vectors),
        out_specs=(rows, rows, *((*matrices, *vectors) * 3)),
        check_vma=False,
    )
```

```python
import math

import jax
import jax.numpy as jnp
from jax import lax
from jax.experimental import pallas as pl
from jax.experimental.pallas import tpu as pltpu
from jax.sharding import PartitionSpec as P

HDIM = 128
NS_STEPS = 5
HALF = 512

bf16 = jnp.bfloat16
f32 = jnp.float32
highest = lax.Precision.HIGHEST
norm_epsilon = 1e-05
ortho_epsilon = 1e-07
coef_first = 3.4445
coef_second = -4.775
coef_third = 2.0315
decay_rate = 0.5
matrix_rate = 0.25
masked_value = -1e30

CORE = [(0, 1), (1, 0)]


def xor_pairs(size, mask):
    return [(i, i ^ mask) for i in range(size)]


def swap_core(value):
    return lax.ppermute(value, "tp", CORE)


def swap_ctx(value, mask):
    return lax.ppermute(value, "ctx", xor_pairs(4, mask))


def swap_fsdp(value, mask):
    return lax.ppermute(value, "fsdp", xor_pairs(4, mask))


def mm(left, right, dims):
    return lax.dot_general(left, right, ((dims[:1], dims[1:]), ((), ())), preferred_element_type=f32)


def spread(own):
    if lax.axis_size("ctx") != 4:
        whole = lax.all_gather(own, "ctx", axis=0, tiled=False)
        return [whole[i] for i in range(whole.shape[0])]
    half = own.shape[0] // 2
    from_x = swap_ctx(own, 1)
    from_y = swap_ctx(own, 2)
    top = swap_ctx(from_x[:half], 2)
    low = swap_ctx(from_y[half:], 1)
    return [own, from_x, from_y, jnp.concatenate([top, low], axis=0)]


def collect(partial):
    count = lax.axis_size("ctx")
    rows = partial.shape[0] // count
    if count != 4:
        return lax.psum_scatter(partial, "ctx", scatter_dimension=0, tiled=True).astype(f32)
    half = rows // 2
    part = [partial[k * rows : (k + 1) * rows] for k in range(4)]
    over_x = swap_ctx(jnp.concatenate([part[1][:half], part[3][:half]], axis=0), 1).astype(f32)
    over_y = swap_ctx(jnp.concatenate([part[2][half:], part[3][half:]], axis=0), 2).astype(f32)
    then_y = swap_ctx((part[2][:half].astype(f32) + over_x[half:]).astype(bf16), 2)
    then_x = swap_ctx((part[1][half:].astype(f32) + over_y[half:]).astype(bf16), 1)
    own = part[0].astype(f32)
    return jnp.concatenate(
        [
            own[:half] + over_x[:half] + then_y.astype(f32),
            own[half:] + over_y[:half] + then_x.astype(f32),
        ],
        axis=0,
    )


def layer_norm(values, gain_row, shift_row):
    center = values - jnp.mean(values, axis=-1, keepdims=True)
    inverse = lax.rsqrt(jnp.mean(center * center, axis=-1, keepdims=True) + norm_epsilon)
    normed = center * inverse
    return (normed * gain_row + shift_row, normed, inverse)


def layer_norm_back(grad_upper, normed, inverse, gain_row):
    grad_normed = grad_upper * gain_row
    mean_grad = jnp.mean(grad_normed, axis=-1, keepdims=True)
    mean_dot = jnp.mean(grad_normed * normed, axis=-1, keepdims=True)
    return inverse * (grad_normed - mean_grad - normed * mean_dot)


def gelu_tanh(values):
    return jax.nn.gelu(values, approximate=True)


MESH = pl.DeviceIdType.MESH


def remote(source, target, send, receive, axis, index):
    return pltpu.make_async_remote_copy(
        src_ref=source,
        dst_ref=target,
        send_sem=send,
        recv_sem=receive,
        device_id={axis: index},
        device_id_type=MESH,
    )


def greet(axis_indices):
    barrier = pltpu.get_barrier_semaphore()
    for axis, index in axis_indices:
        pl.semaphore_signal(barrier, inc=1, device_id={axis: index}, device_id_type=MESH)
    pl.semaphore_wait(barrier, len(axis_indices))


def staged(kernel, count, n_in, n_out):
    def run(*refs):
        given, others, rest = refs[:count], refs[count : n_in + n_out], refs[n_in + n_out :]
        slots, sems, rest = rest[:count], rest[count], rest[count + 1 :]
        copies = [pltpu.make_async_copy(g, v, sems.at[k]) for k, (g, v) in enumerate(zip(given, slots))]
        for one in copies:
            one.start()

        def ready(first, last):
            for one in copies[first:last]:
                one.wait()

        kernel(given, ready, *slots, *others, *rest)

    return run


def slots_for(operands):
    return [
        *[pltpu.VMEM(o.shape, o.dtype) for o in operands],
        pltpu.SemaphoreType.DMA((len(operands),)),
    ]


class RowSums:
    def __init__(self, part, from_x, from_y, then_y, then_x, to_y, to_x, send, receive):
        self.part, self.send, self.receive = part, send, receive
        self.from_x, self.from_y, self.then_y, self.then_x = from_x, from_y, then_y, then_x
        self.to_y, self.to_x = to_y, to_x
        self.pieces, self.count = to_y.shape[:2]
        self.span = [pl.ds(j * self.count, self.count) for j in range(self.pieces)]
        c = lax.axis_index("ctx")
        self.x_side = c + 1 - 2 * (c % 2)
        self.y_side = c + 2 - 4 * (c // 2)
        self.one, self.two = [], []

    def copy(self, stage, j, source, target, side):
        copy = remote(source, target, self.send.at[stage, j], self.receive.at[stage, j], "ctx", side)
        copy.start()
        return copy

    def first(self, part):
        for j in range(self.pieces):
            self.one.append(
                (
                    self.copy(0, j, part.at[:, 1, 0, self.span[j]], self.from_x.at[j], self.x_side),
                    self.copy(1, j, part.at[1, :, 1, self.span[j]], self.from_y.at[j], self.y_side),
                )
            )

    def second(self):
        for j in range(self.pieces):
            at = self.span[j]
            self.one[j][0].wait_recv()
            value = self.part[1, 0, 0, at].astype(f32) + self.from_x[j, 1].astype(f32)
            self.to_y[j] = value.astype(bf16)
            over_y = self.copy(2, j, self.to_y.at[j], self.then_y.at[j], self.y_side)
            self.one[j][1].wait_recv()
            value = self.part[0, 1, 1, at].astype(f32) + self.from_y[j, 1].astype(f32)
            self.to_x[j] = value.astype(bf16)
            over_x = self.copy(3, j, self.to_x.at[j], self.then_x.at[j], self.x_side)
            self.two.append((over_y, over_x))

    def third(self, j):
        at = self.span[j]
        self.two[j][0].wait_recv()
        self.two[j][1].wait_recv()
        top = self.part[0, 0, 0, at].astype(f32) + self.from_x[j, 0].astype(f32)
        low = self.part[0, 0, 1, at].astype(f32) + self.from_y[j, 0].astype(f32)
        top = top + self.then_y[j].astype(f32)
        low = low + self.then_x[j].astype(f32)
        return at, jnp.concatenate([top, low], axis=0)

    def end(self):
        for pair in (*self.one, *self.two):
            for one in pair:
                one.wait_send()


def row_scratch(half, width, pieces=4):
    count = half // pieces
    return [
        pltpu.VMEM((pieces, 2, count, width), bf16),
        pltpu.VMEM((pieces, 2, count, width), bf16),
        *[pltpu.VMEM((pieces, count, width), bf16)] * 4,
        pltpu.SemaphoreType.DMA((4, pieces)),
        pltpu.SemaphoreType.DMA((4, pieces)),
    ]


def exchange_kernel(step, n_in, n_vec, n_out, n_sum, given, ready, *refs):
    part = refs[0]
    ins = refs[1 : 1 + n_in]
    vectors = refs[1 + n_in : 1 + n_in + n_vec]
    rest = refs[1 + n_in + n_vec :]
    whole = rest[0]
    outs = rest[1 : 1 + n_out]
    sums_ref = rest[1 + n_out]
    own, send, receive, local = rest[2 + n_out : 6 + n_out]
    row_sums = RowSums(part, *rest[6 + n_out :])
    x_side, y_side, span, count = row_sums.x_side, row_sums.y_side, row_sums.span, row_sums.count
    greet([("ctx", x_side), ("ctx", y_side)])

    def copy(stage, j, source, target, side):
        one = remote(source, target, send.at[stage, j], receive.at[stage, j], "ctx", side)
        one.start()
        return one

    row_sums.first(given[0])
    ready(0, 1)
    row_sums.second()
    ready(1, 1 + n_in)
    params = [v[...] for v in vectors]
    third, fourth, kept = [], [], []
    totals = None
    for j in range(row_sums.pieces):
        at, total = row_sums.third(j)
        both = lambda ref: jnp.concatenate([ref[0, at], ref[1, at]], axis=0)
        sent, rows, sums = step(total, [both(r) for r in ins], params)
        own[0, at] = sent[:count]
        own[1, at] = sent[count:]
        third.append(
            (
                copy(0, j, own.at[:, at], whole.at[1, :, at], x_side),
                copy(1, j, own.at[:, at], whole.at[2, :, at], y_side),
            )
        )
        keep = pltpu.make_async_copy(own.at[:, at], whole.at[0, :, at], local.at[j])
        keep.start()
        kept.append(keep)
        for out, value in zip(outs, rows):
            out[0, at] = value[:count]
            out[1, at] = value[count:]
        totals = sums if totals is None else [a + b for a, b in zip(totals, sums)]
    for k in range(n_sum):
        sums_ref[k : k + 1] = totals[k]
    for j, at in enumerate(span):
        third[j][0].wait_recv()
        over_y = copy(2, j, whole.at[1, 0, at], whole.at[3, 0, at], y_side)
        third[j][1].wait_recv()
        over_x = copy(3, j, whole.at[2, 1, at], whole.at[3, 1, at], x_side)
        fourth.append((over_y, over_x))
    row_sums.end()
    for pair in third:
        for one in pair:
            one.wait_send()
    for pair in fourth:
        for one in pair:
            one.wait()
    for one in kept:
        one.wait()


def exchange(name, number, step, part, ins, vectors, out_types, n_sum):
    rows, width = ins[0].shape
    if lax.axis_size("ctx") != 4 or rows % 128:
        sent, outs, sums = step(collect(part), ins, vectors)
        return jnp.concatenate(spread(sent), axis=0), outs, sums
    pieces = 4
    half = rows // 2
    vmem = pl.BlockSpec(memory_space=pltpu.VMEM)
    halves = lambda v: v.reshape(2, half, width)
    anywhere = pl.BlockSpec(memory_space=pl.ANY)
    operands = [part.reshape(2, 2, 2, half, width), *map(halves, ins)]
    n_in = len(operands) + len(vectors)

    def kernel(*refs):
        exchange_kernel(step, len(ins), len(vectors), len(out_types), n_sum, *refs)

    whole, *outs, sums = pl.pallas_call(
        staged(kernel, len(operands), n_in, 2 + len(out_types)),
        out_shape=[
            jax.ShapeDtypeStruct((4, 2, half, width), bf16),
            *[jax.ShapeDtypeStruct((2, half, width), d) for d in out_types],
            jax.ShapeDtypeStruct((8, width), f32),
        ],
        in_specs=[*[anywhere] * len(operands), *[vmem] * len(vectors)],
        out_specs=[anywhere, *[vmem] * (len(out_types) + 1)],
        scratch_shapes=[
            *slots_for(operands),
            pltpu.VMEM((2, half, width), bf16),
            pltpu.SemaphoreType.DMA((4, pieces)),
            pltpu.SemaphoreType.DMA((4, pieces)),
            pltpu.SemaphoreType.DMA((pieces,)),
            *row_scratch(half, width, pieces),
        ],
        compiler_params=pltpu.CompilerParams(
            collective_id=number, has_side_effects=True, vmem_limit_bytes=56 << 20
        ),
        cost_estimate=pl.CostEstimate(
            flops=60 * rows * width, bytes_accessed=130 << 20, transcendentals=0
        ),
        name=name,
    )(*operands, *vectors)
    return (
        whole.reshape(4 * rows, width),
        [o.reshape(rows, width) for o in outs],
        [sums[k : k + 1] for k in range(n_sum)],
    )


def column_sum(values):
    return jnp.sum(values, axis=0, keepdims=True)


def first_step(total, rows, vectors):
    bias, gain, shift = vectors
    first, unit, inverse = layer_norm(rows[0].astype(f32) + total + bias, gain, shift)
    return first.astype(bf16), [unit, jnp.broadcast_to(inverse, unit.shape)], []


def second_step(total, rows, vectors):
    bias, gain_one, shift_one, gain, shift = vectors
    first = rows[0] * gain_one + shift_one
    out, unit, inverse = layer_norm(first + total + bias, gain, shift)
    upper = rows[1].astype(f32)
    grad = layer_norm_back(upper, unit, inverse, gain)
    low = grad.astype(bf16)
    sums = [column_sum(upper * unit), column_sum(upper), column_sum(low.astype(f32))]
    return low, [out.astype(bf16), grad], sums


def third_step(total, rows, vectors):
    (gain,) = vectors
    unit, inverse, upper = rows
    upper = upper + total
    grad = layer_norm_back(upper, unit, inverse, gain)
    low = grad.astype(bf16)
    sums = [column_sum(upper * unit), column_sum(upper), column_sum(low.astype(f32))]
    return low, [grad], sums


def block_weights(query, keys, place_rows, place_cols):
    scores = mm(query, keys, (1, 1))
    scores = jnp.where(jnp.abs(place_rows - place_cols) <= HALF, scores, masked_value)
    top = jnp.max(scores, axis=-1, keepdims=True)
    weights = jnp.exp((scores - top) * HDIM**-0.5)
    return weights, 1.0 / jnp.sum(weights, axis=-1, keepdims=True)


def attend_kernel(block, q_ref, k_ref, v_ref, rows_ref, cols_ref, out_ref):
    for start in range(0, q_ref.shape[0], block):
        span = pl.ds(start, block)
        weights, inverse = block_weights(q_ref[span, :], k_ref[...], rows_ref[span, :], cols_ref[...])
        out_ref[span, :] = (mm(weights.astype(bf16), v_ref[...], (1, 0)) * inverse).astype(bf16)


def attend_forward(qkv, place):
    length = qkv.shape[0]
    heads = qkv.shape[1] // (3 * HDIM)
    piece = lambda which: pl.BlockSpec((length, HDIM), lambda h, w=which: (0, w * heads + h))
    return pl.pallas_call(
        lambda *refs: attend_kernel(256, *refs),
        out_shape=jax.ShapeDtypeStruct((length, heads * HDIM), bf16),
        grid=(heads,),
        in_specs=[
            piece(0),
            piece(1),
            piece(2),
            pl.BlockSpec((length, 1), lambda h: (0, 0)),
            pl.BlockSpec((1, length), lambda h: (0, 0)),
        ],
        out_specs=pl.BlockSpec((length, HDIM), lambda h: (0, h)),
        compiler_params=pltpu.CompilerParams(vmem_limit_bytes=40 << 20),
        cost_estimate=pl.CostEstimate(
            flops=4 * heads * length * length * HDIM,
            bytes_accessed=8 * heads * length * HDIM,
            transcendentals=heads * length * length,
        ),
        name="attend_forward",
    )(qkv, qkv, qkv, place[:, None], place[None, :])


def attend_back_kernel(
    block, heads, q_ref, k_ref, v_ref, up_ref, rows_ref, cols_ref, out_ref, sum_k, sum_v
):
    scale = HDIM**-0.5
    head = pl.program_id(0)
    column = lambda which: pl.ds(pl.multiple_of((which * heads + head) * HDIM, HDIM), HDIM)
    for start in range(0, q_ref.shape[0], block):
        span = pl.ds(start, block)
        query = q_ref[span, :]
        upper = up_ref[span, :]
        weights, inverse = block_weights(query, k_ref[...], rows_ref[span, :], cols_ref[...])
        probs = weights * inverse
        grad_probs = mm(upper, v_ref[...], (1, 1))
        inner = jnp.sum(probs * grad_probs, axis=-1, keepdims=True)
        grad_scores = (probs * (grad_probs - inner)).astype(bf16)
        out_ref[span, column(0)] = (mm(grad_scores, k_ref[...], (1, 0)) * scale).astype(bf16)
        add_k = mm(grad_scores, query, (0, 0))
        add_v = mm(probs.astype(bf16), upper, (0, 0))
        if start == 0:
            sum_k[...] = add_k
            sum_v[...] = add_v
        else:
            sum_k[...] += add_k
            sum_v[...] += add_v
    out_ref[:, column(1)] = (sum_k[...] * scale).astype(bf16)
    out_ref[:, column(2)] = sum_v[...].astype(bf16)


def attend_backward(qkv, upper, place):
    length = qkv.shape[0]
    heads = qkv.shape[1] // (3 * HDIM)
    piece = lambda which: pl.BlockSpec((length, HDIM), lambda h, w=which: (0, w * heads + h))
    return pl.pallas_call(
        lambda *refs: attend_back_kernel(256, heads, *refs),
        out_shape=jax.ShapeDtypeStruct(qkv.shape, bf16),
        grid=(heads,),
        in_specs=[
            piece(0),
            piece(1),
            piece(2),
            piece(0),
            pl.BlockSpec((length, 1), lambda h: (0, 0)),
            pl.BlockSpec((1, length), lambda h: (0, 0)),
        ],
        out_specs=pl.BlockSpec(qkv.shape, lambda h: (0, 0)),
        scratch_shapes=[pltpu.VMEM((length, HDIM), f32), pltpu.VMEM((length, HDIM), f32)],
        compiler_params=pltpu.CompilerParams(vmem_limit_bytes=48 << 20),
        cost_estimate=pl.CostEstimate(
            flops=10 * heads * length * length * HDIM,
            bytes_accessed=14 * heads * length * HDIM,
            transcendentals=heads * length * length,
        ),
        name="attend_backward",
    )(qkv, qkv, qkv, upper, place[:, None], place[None, :])


def gram_of(moment_ref, total_ref, n):
    span = pl.ds(n * HDIM, HDIM)
    state = decay_rate * moment_ref[:, span].astype(f32) + total_ref[:, span].astype(f32)
    return lax.dot_general(
        state, state, (((0,), (0,)), ((), ())), precision=highest, preferred_element_type=f32
    )


def gram_kernel(moment_ref, total_ref, out_ref):
    for n in range(out_ref.shape[0]):
        out_ref[n] = gram_of(moment_ref, total_ref, n)


def apply_kernel(moment_ref, total_ref, factor_ref, out_ref):
    for n in range(factor_ref.shape[0]):
        span = pl.ds(n * HDIM, HDIM)
        state = decay_rate * moment_ref[:, span].astype(f32) + total_ref[:, span].astype(f32)
        out_ref[:, span] = jnp.dot(
            state, factor_ref[n], precision=highest, preferred_element_type=f32
        ).astype(bf16)


def whole_call(kernel, name, out, *operands, flops):
    vmem = pl.BlockSpec(memory_space=pltpu.VMEM)
    return pl.pallas_call(
        kernel,
        out_shape=out,
        in_specs=[vmem] * len(operands),
        out_specs=vmem,
        compiler_params=pltpu.CompilerParams(vmem_limit_bytes=32 << 20),
        cost_estimate=pl.CostEstimate(
            flops=flops, bytes_accessed=sum(o.size * o.dtype.itemsize for o in operands), transcendentals=0
        ),
        name=name,
    )(*operands)


def polynomial(grams):
    width = grams[0].shape[0]
    same = lax.broadcasted_iota(jnp.int32, (width, width), 0) == lax.broadcasted_iota(
        jnp.int32, (width, width), 1
    )
    unit = same.astype(f32)
    dot = lambda a, b: jnp.dot(a, b, precision=highest, preferred_element_type=f32)
    scaled, totals = [], []
    for gram in grams:
        square = jnp.sum(jnp.sum(gram * unit, axis=1, keepdims=True), axis=0, keepdims=True)
        inverse = 1.0 / (jnp.sqrt(square) + ortho_epsilon)
        scaled.append(gram * (inverse * inverse))
        totals.append(unit * inverse)
    for step in range(NS_STEPS):
        squares = [dot(g, g) for g in scaled]
        polys = [
            coef_first * unit + coef_second * g + coef_third * s for g, s in zip(scaled, squares)
        ]
        totals = [dot(q, p) for q, p in zip(totals, polys)]
        if step + 1 < NS_STEPS:
            halves = [dot(g, p) for g, p in zip(scaled, polys)]
            scaled = [dot(p, h) for p, h in zip(polys, halves)]
    return totals


def polynomial_kernel(gram_ref, out_ref):
    for n, total in enumerate(polynomial([gram_ref[n] for n in range(gram_ref.shape[0])])):
        out_ref[n] = total


def fold(symmetric):
    half = symmetric.shape[0] // 2
    last = symmetric[half:, half:]
    sides = jnp.concatenate([last[: half // 2], last[half // 2 :]], axis=1)
    return jnp.concatenate([symmetric[:half], sides], axis=0)


def unfold(folded):
    half = folded.shape[1] // 2
    top, sides = folded[:half], folded[half:]
    last = jnp.concatenate([sides[:, :half], sides[:, half:]], axis=0)
    return jnp.concatenate([top, jnp.concatenate([top[:, half:].T, last], axis=1)], axis=0)


FOLDED = 3 * HDIM // 4


def summed_polynomials(moments, totals, grams, pieces, send, receive, keep, between):
    each_group = totals[0].shape[1] // HDIM
    count = grams.shape[0]
    size = min(each_group, count // 2)
    each = size // 4
    f = lax.axis_index("fsdp")
    planes = [(f + i) % 4 for i in range(4)]
    batches = range(count // size)
    copies = []
    for b in batches:
        first = b * size
        for n in range(first, first + size):
            g = n // each_group
            grams[n] = fold(gram_of(moments[g], totals[g], n % each_group))
        copies.append([])
        for i in (1, 2, 3):
            one = remote(
                grams.at[pl.ds(first + planes[i] * each, each)],
                pieces.at[i - 1, pl.ds(b * each, each)],
                send.at[b, i - 1],
                receive.at[b, i - 1],
                "fsdp",
                planes[i],
            )
            one.start()
            copies[b].append(one)
    between()
    for b in batches:
        sums = [grams[b * size + f * each + n] for n in range(each)]
        for i in (1, 2, 3):
            copies[b][i - 1].wait()
            sums = [s + pieces[i - 1, b * each + n] for n, s in enumerate(sums)]
        for n, value in enumerate(polynomial([unfold(v) for v in sums])):
            keep(b, n, fold(value))
        yield b


def rows_to_owners(totals, targets, send, receive, local, first=0):
    rows = totals[0].shape[0] // 4
    c = lax.axis_index("ctx")
    copies = []
    for g, (total, target) in enumerate(zip(totals, targets)):
        for i in (3, 1, 2, 0):
            side = (c + i) % 4
            source = total.at[pl.ds(pl.multiple_of(side * rows, rows), rows)]
            if i:
                sems = send.at[first + g, i - 1], receive.at[first + g, i - 1]
                copies.append(remote(source, target.at[c], *sems, "ctx", side))
            else:
                copies.append(pltpu.make_async_copy(source, target.at[c], local.at[0, g]))
            copies[-1].start()
    return copies


class Chain:
    def __init__(self, b, size, factors, send, receive):
        self.b, self.size, self.factors, self.send, self.receive_sem = b, size, factors, send, receive
        self.f = lax.axis_index("fsdp")

    def copy(self, up, k, block, plane):
        each = self.size // 4
        ref = self.factors.at[pl.ds(self.b * self.size + block * each, each)]
        at = 2 * self.b + up, k
        return remote(ref, ref, self.send.at[at], self.receive_sem.at[at], "fsdp", plane)

    def leaving(self, up, k):
        f = self.f
        return self.copy(up, k, f - k, f + 1) if up else self.copy(up, k, f + k, f - 1)

    def coming(self, up, k):
        f = self.f
        return self.copy(up, k, f - 1 - k, f - 1) if up else self.copy(up, k, f + 1 + k, f + 1)

    def leaves(self, up, k):
        f = self.f
        return jnp.logical_and(f < 3, f >= k) if up else jnp.logical_and(f > 0, f + k <= 3)

    def comes(self, up, k):
        return self.f >= k + 1 if up else self.f <= 2 - k

    def start(self, k):
        for up in (1, 0):
            pl.when(self.leaves(up, k))(lambda up=up: self.leaving(up, k).start())

    def receive(self, k):
        for up in (1, 0):
            pl.when(self.comes(up, k))(lambda up=up: self.coming(up, k).wait_recv())

    def end(self):
        for k in range(3):
            for up in (1, 0):
                pl.when(self.leaves(up, k))(lambda up=up: self.leaving(up, k).wait_send())


def all_sides():
    c, f, t = (lax.axis_index(axis) for axis in ("ctx", "fsdp", "tp"))
    over = [(axis, (at + i) % 4) for axis, at in (("ctx", c), ("fsdp", f)) for i in (1, 2, 3)]
    return [*over, ("tp", 1 - t)]


def share_core(share, shared, send, receive, local):
    t = lax.axis_index("tp")
    copies = [
        remote(share, shared.at[t], send.at[0], receive.at[0], "tp", 1 - t),
        pltpu.make_async_copy(share, shared.at[t], local.at[0]),
    ]
    for one in copies:
        one.start()
    return copies


def feed_forward_kernel(given, ready, *refs):
    moments, totals, (base, vector, share), refs = refs[:2], refs[2:4], refs[4:7], refs[7:]
    grads_low, weights, refs = refs[:2], refs[2:4], refs[4:]
    (out, *grads), (shared, summed, vector_out), refs = refs[:3], refs[3:6], refs[6:]
    factors, send_c, receive_c, local, send_t, receive_t, local_t, send_f, receive_f = refs[:9]
    gram_refs, (sent_v, got_v, send_v, receive_v) = refs[9:13], refs[13:17]
    part, row_refs = refs[17], refs[18:]
    c, f, t = (lax.axis_index(axis) for axis in ("ctx", "fsdp", "tp"))
    partners = [
        ("tp", 1 - t),
        ("ctx", c + 1 - 2 * (c % 2)),
        ("ctx", c + 2 - 4 * (c // 2)),
        ("fsdp", f + 1 - 2 * (f % 2)),
        ("fsdp", f + 2 - 4 * (f // 2)),
    ]
    greet(all_sides())
    vector_copies = []

    def vector_start(k):
        one = remote(sent_v.at[k], got_v.at[k], send_v.at[k], receive_v.at[k], *partners[k])
        one.start()
        vector_copies.append(one)

    def vector_next(k):
        vector_copies[k].wait_recv()
        if k < 4:
            sent_v[k + 1] = sent_v[k] + got_v[k]
            vector_start(k + 1)
        else:
            vector_out[...] = sent_v[k] + got_v[k]

    sum_rows = RowSums(part, *row_refs)
    half, width = part.shape[3:]
    depth = grads_low[0].shape[1]
    block = width // 4

    def make_part(k, carry):
        rows = pl.ds(pl.multiple_of(k * 2 * half, 2 * half), 2 * half)
        for n in range(4):
            column = pl.ds(n * block, block)
            value = sum(mm(grads_low[i][rows, :], weights[i][column, :depth], (1, 1)) for i in range(2))
            value = value.astype(bf16)
            part[k // 2, k % 2, 0, :, column] = value[:half]
            part[k // 2, k % 2, 1, :, column] = value[half:]
        return carry

    ready(0, 7)
    started = rows_to_owners(totals, grads, send_c, receive_c, local)
    started += share_core(share, shared, send_t, receive_t, local_t)
    sent_v[0] = vector[...]
    vector_start(0)
    size = totals[0].shape[1] // HDIM
    each = size // 4
    chains = [Chain(b, size, factors, send_f, receive_f) for b in range(2)]

    def keep(b, n, value):
        factors[b * size + f * each + n] = value

    def between():
        ready(7, 11)
        lax.fori_loop(0, 4, make_part, 0)
        sum_rows.first(part)
        vector_next(0)

    for b in summed_polynomials(moments, totals, *gram_refs, keep, between):
        chains[b].start(0)
        if b == 0:
            vector_next(1)
            sum_rows.second()
    vector_next(2)
    for j in range(sum_rows.pieces):
        span, total = sum_rows.third(j)
        for h in range(2):
            value = total[h * sum_rows.count : (h + 1) * sum_rows.count]
            summed[h, span] = base[h, span] + value
    for k in range(3):
        for chain in chains:
            chain.receive(k)
            if k < 2:
                chain.start(k + 1)
        if k == 0:
            vector_next(3)
    out[...] = factors[...]
    vector_next(4)
    for chain in chains:
        chain.end()
    for one in vector_copies:
        one.wait_send()
    for one in started:
        one.wait()
    sum_rows.end()


def last_kernel(given, ready, *refs):
    moments, totals, (others, share), refs = refs[:3], refs[3:6], refs[6:8], refs[8:]
    orthos, (grads, shared), refs = refs[:3], refs[3:5], refs[5:]
    factors, stage, send_c, receive_c, local, send_t, receive_t, local_t, send_f, receive_f = refs[:10]
    gram_refs = refs[10:]
    rows = totals[0].shape[0] // 4
    count = totals[0].shape[1] // HDIM
    c, f = lax.axis_index("ctx"), lax.axis_index("fsdp")
    greet(all_sides())
    ready(0, 8)
    started = rows_to_owners(totals[:1], [grads], send_c, receive_c, local)
    started += share_core(share, shared, send_t, receive_t, local_t)

    def send_ortho(g, first, size, kind, factor):
        made = {n: unfold(factor(n)) for n in range(first, first + size)}
        wide = pl.ds(first * HDIM, size * HDIM)
        for i in (3, 1, 2, 0):
            side = (c + i) % 4
            span = pl.ds(pl.multiple_of(side * rows, rows), rows)
            for n in range(first, first + size):
                column = pl.ds(n * HDIM, HDIM)
                state = decay_rate * moments[g][span, column].astype(f32)
                state = state + totals[g][span, column].astype(f32)
                stage[g, i, :, column] = jnp.dot(
                    state, made[n], precision=highest, preferred_element_type=f32
                ).astype(bf16)
            source, target = stage.at[g, i, :, wide], orthos[g].at[c, :, wide]
            if i:
                sems = send_c.at[kind, i - 1], receive_c.at[kind, i - 1]
                copy = remote(source, target, *sems, "ctx", side)
            else:
                copy = pltpu.make_async_copy(source, target, local.at[0, kind])
            copy.start()
            started.append(copy)

    def between():
        for g in (1, 2):
            send_ortho(g, 0, count, g, lambda n: others[(g - 1) * count + n])

    size = count // 2
    each = size // 4
    chains = [Chain(b, size, factors, send_f, receive_f) for b in range(2)]

    def keep(b, n, value):
        factors[b * size + f * each + n] = value

    for b in summed_polynomials(moments[:1], totals[:1], *gram_refs, keep, between):
        chains[b].start(0)
    for k in range(2):
        for chain in chains:
            chain.receive(k)
            chain.start(k + 1)
    for b, chain in enumerate(chains):
        chain.receive(2)
        send_ortho(0, b * size, size, 3 + b, lambda n: factors[n])
    for chain in chains:
        chain.end()
    for one in started:
        one.wait()


def fits_planes(columns):
    return lax.axis_size("fsdp") == 4 and lax.axis_size("ctx") == 4 and columns == 8 * HDIM


def polynomials_over_planes(moment, total):
    count = total.shape[1] // HDIM
    flops = 12 * total.size * HDIM
    shape = jax.ShapeDtypeStruct((count, HDIM, HDIM), f32)
    grams = whole_call(gram_kernel, "grams", shape, moment, total, flops=flops)
    summed = lax.psum(grams, "fsdp")
    return whole_call(polynomial_kernel, "polynomials", shape, summed, flops=flops)


def shared_by_cores(share):
    other, t = swap_core(share), lax.axis_index("tp")
    return jnp.stack([jnp.where(t == m, share, other) for m in range(2)])


def feed_forward_slabs(moments, totals, share, grads_low, weights, base, vector):
    rows, columns = totals[0].shape
    if not fits_planes(columns):
        factors = [polynomials_over_planes(m, v) for m, v in zip(moments, totals)]
        summed = lax.psum(vector, ("fsdp", "ctx", "tp"))
        blocks = [from_blocks(v) for v in totals]
        depth = grads_low[0].shape[1]
        part = sum(mm(g, w[:, :depth], (1, 1)) for g, w in zip(grads_low, weights)).astype(bf16)
        return factors, blocks, shared_by_cores(share), base + collect(part), summed
    count = 2 * columns // HDIM
    vmem = pl.BlockSpec(memory_space=pltpu.VMEM)
    anywhere = pl.BlockSpec(memory_space=pl.ANY)
    block = jax.ShapeDtypeStruct((4, rows // 4, columns), bf16)
    half, width = base.shape[0] // 2, base.shape[1]
    lines = vector.size // HDIM
    dma = pltpu.SemaphoreType.DMA
    operands = [
        *moments,
        *totals,
        base.reshape(2, half, width),
        vector.reshape(lines, HDIM),
        share,
        *grads_low,
        *weights,
    ]
    factors, up, down, shared, summed, vector_sum = pl.pallas_call(
        staged(feed_forward_kernel, 11, 11, 6),
        out_shape=[
            jax.ShapeDtypeStruct((count, FOLDED, HDIM), f32),
            block,
            block,
            jax.ShapeDtypeStruct((2, *share.shape), share.dtype),
            jax.ShapeDtypeStruct((2, half, width), f32),
            jax.ShapeDtypeStruct((lines, HDIM), f32),
        ],
        in_specs=[anywhere] * 11,
        out_specs=[vmem, anywhere, anywhere, anywhere, vmem, vmem],
        scratch_shapes=[
            *slots_for(operands),
            pltpu.VMEM((count, FOLDED, HDIM), f32),
            *[dma((2, 3))] * 2,
            dma((1, 2)),
            *[dma((1,))] * 3,
            *[dma((4, 3))] * 2,
            pltpu.VMEM((count, FOLDED, HDIM), f32),
            pltpu.VMEM((3, count // 4, FOLDED, HDIM), f32),
            *[dma((2, 3))] * 2,
            *[pltpu.VMEM((5, lines, HDIM), f32)] * 2,
            *[dma((5,))] * 2,
            pltpu.VMEM((2, 2, 2, half, width), bf16),
            *row_scratch(half, width),
        ],
        compiler_params=pltpu.CompilerParams(
            collective_id=4, has_side_effects=True, vmem_limit_bytes=56 << 20
        ),
        cost_estimate=pl.CostEstimate(
            flops=24 * totals[0].size * HDIM, bytes_accessed=150 << 20, transcendentals=0
        ),
        name="feed_forward_slabs",
    )(*operands)
    return factors, [up, down], shared, summed.reshape(base.shape), vector_sum.reshape(vector.shape)


def last_slabs(moments, totals, factors, share):
    rows, columns = totals[0].shape
    own = jax.ShapeDtypeStruct((rows, columns), bf16)
    if not fits_planes(columns):
        factors = [polynomials_over_planes(moments[0], totals[0]), *factors]
        flops = 12 * totals[0].size * HDIM
        orthos = [
            from_blocks(whole_call(apply_kernel, "apply", own, m, v, p, flops=flops))
            for m, v, p in zip(moments, totals, factors)
        ]
        return orthos, from_blocks(totals[0]), shared_by_cores(share)
    count = columns // HDIM
    anywhere = pl.BlockSpec(memory_space=pl.ANY)
    block = jax.ShapeDtypeStruct((4, rows // 4, columns), bf16)
    dma = pltpu.SemaphoreType.DMA
    operands = [*moments, *totals, factors, share]
    *orthos, grads, shared = pl.pallas_call(
        staged(last_kernel, 8, 8, 5),
        out_shape=[*[block] * 4, jax.ShapeDtypeStruct((2, *share.shape), share.dtype)],
        in_specs=[anywhere] * 8,
        out_specs=[anywhere] * 5,
        scratch_shapes=[
            *slots_for(operands),
            pltpu.VMEM((count, FOLDED, HDIM), f32),
            pltpu.VMEM((3, 4, rows // 4, columns), bf16),
            *[dma((5, 3))] * 2,
            dma((1, 5)),
            *[dma((1,))] * 3,
            *[dma((4, 3))] * 2,
            pltpu.VMEM((count, FOLDED, HDIM), f32),
            pltpu.VMEM((3, count // 4, FOLDED, HDIM), f32),
            *[dma((2, 3))] * 2,
        ],
        compiler_params=pltpu.CompilerParams(
            collective_id=5, has_side_effects=True, vmem_limit_bytes=56 << 20
        ),
        cost_estimate=pl.CostEstimate(
            flops=36 * totals[0].size * HDIM, bytes_accessed=100 << 20, transcendentals=0
        ),
        name="last_slabs",
    )(*operands)
    return orthos, grads, shared


def pack_attention_kernel(qkv_ref, out_ref, stack_ref):
    wide = qkv_ref.shape[2]
    for which in range(3):
        stack_ref[0, :, which * wide : (which + 1) * wide] = qkv_ref[which].astype(bf16)
    stack_ref[0, :, 3 * wide :] = out_ref[...].T.astype(bf16)


def pack_attention(qkv, out):
    count = lax.axis_size("ctx")
    _, rows, columns = qkv.shape
    wide = columns // count
    return pl.pallas_call(
        pack_attention_kernel,
        out_shape=jax.ShapeDtypeStruct((count, rows, 4 * wide), bf16),
        grid=(count,),
        in_specs=[
            pl.BlockSpec((3, rows, wide), lambda i: (0, 0, i)),
            pl.BlockSpec((wide, rows), lambda i: (i, 0)),
        ],
        out_specs=pl.BlockSpec((1, rows, 4 * wide), lambda i: (i, 0, 0)),
        compiler_params=pltpu.CompilerParams(vmem_limit_bytes=56 << 20),
        cost_estimate=pl.CostEstimate(
            flops=qkv.size, bytes_accessed=8 * qkv.size, transcendentals=0
        ),
        name="pack_attention",
    )(qkv, out)


def pack_feed_forward(up, down):
    count = lax.axis_size("ctx")
    rows = up.shape[0]
    low = lambda v: v.astype(bf16)
    up_cut = low(up).reshape(rows, count, -1).transpose(1, 0, 2)
    down_cut = low(down).T.reshape(rows, count, -1).transpose(1, 0, 2)
    return up_cut, down_cut


def finish(name, scale, grads, orthos, moments, weights):
    count, rows, columns = grads.shape
    three = [len(s.shape) == 3 for s in weights]
    tall = [len(s.shape) == 2 and s.shape[0] != rows for s in weights]
    number = len(weights)
    wide = columns // 4 if any(three) else columns
    specs = []
    for is_three, is_tall in zip(three, tall):
        if is_three:
            specs.append(pl.BlockSpec((3, rows, wide), lambda i: (0, 0, i)))
        elif is_tall:
            specs.append(pl.BlockSpec((wide, rows), lambda i: (i, 0)))
        else:
            specs.append(pl.BlockSpec((rows, wide), lambda i: (0, i)))

    def kernel(grad_ref, ortho_ref, *refs):
        for j in range(number):
            moment, weight = refs[j], refs[number + j]
            grad_out, state_out, master_out = refs[2 * number + 3 * j : 2 * number + 3 * j + 3]
            for w in range(3) if three[j] else (None,):
                start = (3 if w is None and any(three) else w or 0) * wide
                cut = lambda ref: ref[0, :, start : start + wide].astype(f32)
                grad, ortho = cut(grad_ref), cut(ortho_ref)
                if tall[j]:
                    grad, ortho = grad.T, ortho.T
                at = ... if w is None else w
                grad_out[at] = grad
                state_out[at] = decay_rate * moment[at] + grad
                master_out[at] = weight[at] - scale * ortho

    outs = pl.pallas_call(
        kernel,
        out_shape=[jax.ShapeDtypeStruct(s.shape, f32) for s in weights for _ in range(3)],
        grid=(count,),
        in_specs=[*[pl.BlockSpec((1, rows, columns), lambda i: (i, 0, 0))] * 2, *specs, *specs],
        out_specs=[spec for spec in specs for _ in range(3)],
        compiler_params=pltpu.CompilerParams(vmem_limit_bytes=56 << 20),
        cost_estimate=pl.CostEstimate(
            flops=4 * grads.size, bytes_accessed=24 * grads.size, transcendentals=0
        ),
        name=name,
    )(grads, orthos, *moments, *weights)
    return outs[0::3], outs[1::3], outs[2::3]


def over_ctx(stack):
    return lax.all_to_all(stack, "ctx", split_axis=0, concat_axis=0, tiled=True)


def to_blocks(stack):
    moved = over_ctx(stack)
    return moved.reshape(-1, moved.shape[-1])


def from_blocks(block):
    return over_ctx(block.reshape(lax.axis_size("ctx"), -1, block.shape[-1]))


def body(
    inputs,
    segment_ids,
    cotangent,
    w_qkv,
    w_out,
    w_up,
    w_down,
    bias_qv,
    bias_up,
    bias_res,
    norm_gain,
    norm_shift,
    moment_qkv,
    moment_out,
    moment_up,
    moment_down,
    moment_bqv,
    moment_bup,
    moment_bres,
    moment_gain,
    moment_shift,
):
    count_c = lax.axis_size("ctx")
    count_f = lax.axis_size("fsdp")
    c = lax.axis_index("ctx")
    t = lax.axis_index("tp")
    rows = inputs.shape[2]
    width = inputs.shape[3]
    length = rows * count_c
    token_total = inputs.shape[0] * inputs.shape[1] * count_f * length
    e = w_qkv.shape[2] // count_c
    u = w_up.shape[1] // count_c

    own_micro = lambda v: lax.dynamic_index_in_dim(v, t, 0, keepdims=False)[0]
    row_low = own_micro(inputs)
    upper = own_micro(cotangent)
    segments = own_micro(segment_ids)
    index = jnp.arange(count_c)
    order = index ^ c if count_c == 4 else index
    place = (segments * (length + HALF + 1) + jnp.arange(length, dtype=jnp.int32)).reshape(count_c, rows)
    place = jnp.take(place, order, axis=0).reshape(length)

    after = lambda value, *others: lax.optimization_barrier((value, *others))[0]
    attn_block = to_blocks(pack_attention(w_qkv, w_out))
    up_late, down_late, *moments_late, _ = lax.optimization_barrier(
        (w_up, w_down, moment_qkv, moment_out, moment_up, moment_down, attn_block)
    )
    up_stack, down_stack = pack_feed_forward(up_late, down_late)
    gather_z = lambda v: lax.all_gather(v, "fsdp", axis=0, tiled=True)
    row_first, upper, _ = lax.optimization_barrier((row_low, upper, attn_block))
    xs = jnp.concatenate(spread(row_first), axis=0)
    both_block = to_blocks(after(jnp.concatenate([up_stack, down_stack], axis=2), xs))
    up_block, down_block = both_block[:, :u], both_block[:, u:]
    attn_g, up_g, down_g = map(gather_z, (attn_block, up_block, down_block))
    moment_stack = jnp.concatenate(
        [pack_attention(*moments_late[:2]), *pack_feed_forward(*moments_late[2:])], axis=2
    )
    moment_stack = after(moment_stack, both_block)
    attn_g = after(attn_g, moment_stack)
    attn_w = (attn_g, swap_core(attn_g))

    bias_q = lax.dynamic_slice_in_dim(bias_qv, c * e, e, 1)
    bias_u = lax.dynamic_slice_in_dim(bias_up, c * u, u, 0)
    small = jnp.concatenate([bias_q.reshape(-1), bias_u])
    small_pair = (small, swap_core(small))
    cores = range(2)

    qkv = []
    for i in cores:
        shift = jnp.concatenate([small_pair[i][:e], jnp.zeros((e,), f32), small_pair[i][e : 2 * e]])
        qkv.append((mm(xs, attn_w[i][:, : 3 * e], (1, 0)) + shift).astype(bf16))
    context = [attend_forward(qkv[i], place) for i in cores]
    part = sum(mm(context[i], attn_w[i][:, 3 * e :], (1, 1)) for i in cores).astype(bf16)
    row = lambda matrix, index: matrix[index : index + 1]
    first_all, (first_unit, first_inverse), _ = exchange(
        "first_rows",
        1,
        first_step,
        part,
        [row_low],
        [row(bias_res, 0), row(norm_gain, 0), row(norm_shift, 0)],
        [f32, f32],
        0,
    )
    moment_block = to_blocks(after(moment_stack, first_all))
    moments = [moment_block[:, : 4 * e], moment_block[:, 4 * e : 4 * e + u], moment_block[:, 4 * e + u :]]
    up_g = after(up_g, first_all)
    up_w = (up_g, swap_core(up_g))
    pre_act = [mm(first_all, up_w[i], (1, 0)) + small_pair[i][2 * e :] for i in cores]
    active = [gelu_tanh(p).astype(bf16) for p in pre_act]
    down_g = after(down_g, moment_block, *active)
    down_w = (down_g, swap_core(down_g))
    part = sum(mm(active[i], down_w[i], (1, 1)) for i in cores).astype(bf16)
    branch_all, (out_rows, grad_second), second_sums = exchange(
        "second_rows",
        2,
        second_step,
        part,
        [first_unit, upper],
        [row(bias_res, 1), row(norm_gain, 0), row(norm_shift, 0), row(norm_gain, 1), row(norm_shift, 1)],
        [bf16, f32],
        3,
    )

    def pair_sum(terms):
        return (terms[0] + swap_core(terms[1].astype(bf16)).astype(f32)).astype(bf16)

    scatter_z = lambda v: lax.psum_scatter(v, "fsdp", scatter_dimension=0, tiled=True)
    term_down = [None, mm(branch_all, active[1], (0, 0)).astype(bf16)]
    term_down[0] = mm(after(branch_all, term_down[1]), active[0], (0, 0))
    branch_all, *term_down = lax.optimization_barrier((branch_all, *term_down))
    down_sum = pair_sum(term_down)

    def before_gelu(i, rows):
        return jax.vjp(gelu_tanh, pre_act[i])[1](mm(rows, down_w[i], (1, 0)))[0].astype(bf16)

    grad_pre = [before_gelu(0, branch_all)]
    branch_all, down_sum, grad_pre[0] = lax.optimization_barrier((branch_all, down_sum, grad_pre[0]))
    grad_pre.append(before_gelu(1, branch_all))
    part = sum(mm(grad_pre[i], up_w[i], (1, 1)) for i in cores).astype(bf16)
    term_up = [None, mm(first_all, grad_pre[1], (0, 0)).astype(bf16)]
    term_up[0] = mm(after(first_all, term_up[1]), grad_pre[0], (0, 0))
    part, up_sum = lax.optimization_barrier((part, pair_sum(term_up)))
    attended_all, (grad_first,), first_sums = exchange(
        "third_rows",
        3,
        third_step,
        part,
        [first_unit, first_inverse, grad_second],
        [row(norm_gain, 0)],
        [f32],
        3,
    )
    grad_qkv_low, term_qkv, term_out = [None, None], [None, None], [None, None]
    rows_for = attended_all
    for i in (1, 0):
        grad_context = mm(rows_for, attn_w[i][:, 3 * e :], (1, 0)).astype(bf16)
        grad_qkv_low[i] = attend_backward(qkv[i], grad_context, place)
        term_qkv[i] = mm(xs, grad_qkv_low[i], (0, 0))
        term_out[i] = mm(rows_for, context[i], (0, 0))
        if i:
            term_qkv[i], term_out[i] = term_qkv[i].astype(bf16), term_out[i].astype(bf16)
            rows_for = after(attended_all, term_qkv[i], term_out[i])
    attn_sum = jnp.concatenate([pair_sum(term_qkv), pair_sum(term_out)], axis=1)
    down_total, up_total = map(scatter_z, (down_sum, up_sum))
    *lows, attn_sum = lax.optimization_barrier((*grad_qkv_low, attn_sum))

    qv_sums = []
    for i in cores:
        sums_i = jnp.sum(grad_qkv_low[i].astype(f32), axis=0)
        qv_sums.append(jnp.stack([sums_i[:e], sums_i[2 * e :]]))
    up_sums = [jnp.sum(g.astype(f32), axis=0) for g in grad_pre]
    side = lambda pair: [jnp.where(t == m, pair[0], pair[1]) for m in range(2)]
    bqv_all = jnp.stack(
        [
            lax.dynamic_update_slice_in_dim(jnp.zeros((2, count_c * e), f32), v, c * e, 1)
            for v in side(qv_sums)
        ]
    )
    bup_all = jnp.stack(
        [
            lax.dynamic_update_slice_in_dim(jnp.zeros((count_c * u,), f32), v, c * u, 0)
            for v in side(up_sums)
        ]
    )
    rest = jnp.concatenate(
        [
            first_sums[2],
            second_sums[2],
            first_sums[0],
            second_sums[0],
            first_sums[1],
            second_sums[1],
        ],
        axis=0,
    )
    flat = jnp.concatenate([bqv_all.reshape(-1), bup_all.reshape(-1), rest.reshape(-1)])

    attn_total = scatter_z(attn_sum)
    step_scale = matrix_rate * math.sqrt(width / HDIM)
    factors, gradient_blocks, layer_out, input_rows, flat = feed_forward_slabs(
        moments[1:], (up_total, down_total), after(out_rows, attn_sum), lows, attn_w, grad_first, flat
    )
    orthos, attn_gradients, input_grad = last_slabs(
        moments, (attn_total, up_total, down_total), factors, input_rows
    )
    gradient_blocks, flat, orthos = lax.optimization_barrier((gradient_blocks, flat, orthos))
    up_done, down_done = [
        finish(name, step_scale, *operands)
        for name, *operands in (
            ("up_finish", gradient_blocks[0], orthos[1], (moment_up,), (w_up,)),
            ("down_finish", gradient_blocks[1], orthos[2], (moment_down,), (w_down,)),
        )
    ]
    attn_done = finish(
        "attention_finish",
        step_scale,
        attn_gradients,
        orthos[0],
        (moment_qkv, moment_out),
        (w_qkv, w_out),
    )
    grads, states, masters = [
        [*attn_done[k], *up_done[k], *down_done[k]] for k in range(3)
    ]

    cut = bqv_all.size
    cut_two = cut + bup_all.size
    grad_bqv = lax.dynamic_index_in_dim(flat[:cut].reshape(bqv_all.shape), t, 0, keepdims=False)
    grad_bup = lax.dynamic_index_in_dim(flat[cut:cut_two].reshape(bup_all.shape), t, 0, keepdims=False)
    rest = flat[cut_two:].reshape(3, 2, width)
    vector_grads = (grad_bqv, grad_bup, rest[0], rest[1], rest[2])
    vector_states = [
        decay_rate * m + g
        for m, g in zip(
            (moment_bqv, moment_bup, moment_bres, moment_gain, moment_shift), vector_grads
        )
    ]
    vector_step = 1.0 / math.sqrt(token_total)
    vector_masters = [
        v - vector_step * s
        for v, s in zip((bias_qv, bias_up, bias_res, norm_gain, norm_shift), vector_states)
    ]
    return (
        layer_out[:, None],
        input_grad[:, None],
        *grads,
        *vector_grads,
        *states,
        *vector_states,
        *masters,
        *vector_masters,
    )


def solution(mesh):
    rows = P(None, "fsdp", "ctx", None)
    matrices = (
        P(None, ("fsdp", "ctx"), "tp"),
        P("tp", ("fsdp", "ctx")),
        P(("fsdp", "ctx"), "tp"),
        P("tp", ("fsdp", "ctx")),
    )
    vectors = (P(None, "tp"), P("tp"), P(), P(), P())
    return jax.shard_map(
        body,
        mesh=mesh,
        in_specs=(rows, P(None, "fsdp", None), rows, *matrices, *vectors, *matrices, *vectors),
        out_specs=(rows, rows, *((*matrices, *vectors) * 3)),
        check_vma=False,
    )
```

```python
import math

import jax
import jax.numpy as jnp
from jax import lax
from jax.experimental import pallas as pl
from jax.experimental.pallas import tpu as pltpu
from jax.sharding import PartitionSpec as P

HDIM = 128
NS_STEPS = 5
HALF = 512

bf16 = jnp.bfloat16
f32 = jnp.float32
highest = lax.Precision.HIGHEST
norm_epsilon = 1e-05
ortho_epsilon = 1e-07
coef_first = 3.4445
coef_second = -4.775
coef_third = 2.0315
decay_rate = 0.5
matrix_rate = 0.25
masked_value = -1e30

CORE = [(0, 1), (1, 0)]


def xor_pairs(size, mask):
    return [(i, i ^ mask) for i in range(size)]


def swap_core(value):
    return lax.ppermute(value, "tp", CORE)


def swap_ctx(value, mask):
    return lax.ppermute(value, "ctx", xor_pairs(4, mask))


def swap_fsdp(value, mask):
    return lax.ppermute(value, "fsdp", xor_pairs(4, mask))


def mm(left, right, dims):
    return lax.dot_general(left, right, ((dims[:1], dims[1:]), ((), ())), preferred_element_type=f32)


def spread(own):
    if lax.axis_size("ctx") != 4:
        whole = lax.all_gather(own, "ctx", axis=0, tiled=False)
        return [whole[i] for i in range(whole.shape[0])]
    half = own.shape[0] // 2
    from_x = swap_ctx(own, 1)
    from_y = swap_ctx(own, 2)
    top = swap_ctx(from_x[:half], 2)
    low = swap_ctx(from_y[half:], 1)
    return [own, from_x, from_y, jnp.concatenate([top, low], axis=0)]


def collect(partial):
    count = lax.axis_size("ctx")
    rows = partial.shape[0] // count
    if count != 4:
        return lax.psum_scatter(partial, "ctx", scatter_dimension=0, tiled=True).astype(f32)
    half = rows // 2
    part = [partial[k * rows : (k + 1) * rows] for k in range(4)]
    over_x = swap_ctx(jnp.concatenate([part[1][:half], part[3][:half]], axis=0), 1).astype(f32)
    over_y = swap_ctx(jnp.concatenate([part[2][half:], part[3][half:]], axis=0), 2).astype(f32)
    then_y = swap_ctx((part[2][:half].astype(f32) + over_x[half:]).astype(bf16), 2)
    then_x = swap_ctx((part[1][half:].astype(f32) + over_y[half:]).astype(bf16), 1)
    own = part[0].astype(f32)
    return jnp.concatenate(
        [
            own[:half] + over_x[:half] + then_y.astype(f32),
            own[half:] + over_y[:half] + then_x.astype(f32),
        ],
        axis=0,
    )


def layer_norm(values, gain_row, shift_row):
    center = values - jnp.mean(values, axis=-1, keepdims=True)
    inverse = lax.rsqrt(jnp.mean(center * center, axis=-1, keepdims=True) + norm_epsilon)
    normed = center * inverse
    return (normed * gain_row + shift_row, normed, inverse)


def layer_norm_back(grad_upper, normed, inverse, gain_row):
    grad_normed = grad_upper * gain_row
    mean_grad = jnp.mean(grad_normed, axis=-1, keepdims=True)
    mean_dot = jnp.mean(grad_normed * normed, axis=-1, keepdims=True)
    return inverse * (grad_normed - mean_grad - normed * mean_dot)


def gelu_tanh(values):
    return jax.nn.gelu(values, approximate=True)


MESH = pl.DeviceIdType.MESH


def remote(source, target, send, receive, axis, index):
    return pltpu.make_async_remote_copy(
        src_ref=source,
        dst_ref=target,
        send_sem=send,
        recv_sem=receive,
        device_id={axis: index},
        device_id_type=MESH,
    )


def greet(axis_indices):
    barrier = pltpu.get_barrier_semaphore()
    for axis, index in axis_indices:
        pl.semaphore_signal(barrier, inc=1, device_id={axis: index}, device_id_type=MESH)
    pl.semaphore_wait(barrier, len(axis_indices))


def staged(kernel, count, n_in, n_out):
    def run(*refs):
        given, others, rest = refs[:count], refs[count : n_in + n_out], refs[n_in + n_out :]
        slots, sems, rest = rest[:count], rest[count], rest[count + 1 :]
        copies = [pltpu.make_async_copy(g, v, sems.at[k]) for k, (g, v) in enumerate(zip(given, slots))]
        for one in copies:
            one.start()

        def ready(first, last):
            for one in copies[first:last]:
                one.wait()

        kernel(given, ready, *slots, *others, *rest)

    return run


def slots_for(operands):
    return [
        *[pltpu.VMEM(o.shape, o.dtype) for o in operands],
        pltpu.SemaphoreType.DMA((len(operands),)),
    ]


class RowSums:
    def __init__(self, part, from_x, from_y, then_y, then_x, to_y, to_x, send, receive):
        self.part, self.send, self.receive = part, send, receive
        self.from_x, self.from_y, self.then_y, self.then_x = from_x, from_y, then_y, then_x
        self.to_y, self.to_x = to_y, to_x
        self.pieces, self.count = to_y.shape[:2]
        self.span = [pl.ds(j * self.count, self.count) for j in range(self.pieces)]
        c = lax.axis_index("ctx")
        self.x_side = c + 1 - 2 * (c % 2)
        self.y_side = c + 2 - 4 * (c // 2)
        self.one, self.two = [], []

    def copy(self, stage, j, source, target, side):
        copy = remote(source, target, self.send.at[stage, j], self.receive.at[stage, j], "ctx", side)
        copy.start()
        return copy

    def first(self, part):
        for j in range(self.pieces):
            self.one.append(
                (
                    self.copy(0, j, part.at[:, 1, 0, self.span[j]], self.from_x.at[j], self.x_side),
                    self.copy(1, j, part.at[1, :, 1, self.span[j]], self.from_y.at[j], self.y_side),
                )
            )

    def second(self):
        for j in range(self.pieces):
            at = self.span[j]
            self.one[j][0].wait_recv()
            value = self.part[1, 0, 0, at].astype(f32) + self.from_x[j, 1].astype(f32)
            self.to_y[j] = value.astype(bf16)
            over_y = self.copy(2, j, self.to_y.at[j], self.then_y.at[j], self.y_side)
            self.one[j][1].wait_recv()
            value = self.part[0, 1, 1, at].astype(f32) + self.from_y[j, 1].astype(f32)
            self.to_x[j] = value.astype(bf16)
            over_x = self.copy(3, j, self.to_x.at[j], self.then_x.at[j], self.x_side)
            self.two.append((over_y, over_x))

    def third(self, j):
        at = self.span[j]
        self.two[j][0].wait_recv()
        self.two[j][1].wait_recv()
        top = self.part[0, 0, 0, at].astype(f32) + self.from_x[j, 0].astype(f32)
        low = self.part[0, 0, 1, at].astype(f32) + self.from_y[j, 0].astype(f32)
        top = top + self.then_y[j].astype(f32)
        low = low + self.then_x[j].astype(f32)
        return at, jnp.concatenate([top, low], axis=0)

    def end(self):
        for pair in (*self.one, *self.two):
            for one in pair:
                one.wait_send()


def row_scratch(half, width, pieces=4):
    count = half // pieces
    return [
        pltpu.VMEM((pieces, 2, count, width), bf16),
        pltpu.VMEM((pieces, 2, count, width), bf16),
        *[pltpu.VMEM((pieces, count, width), bf16)] * 4,
        pltpu.SemaphoreType.DMA((4, pieces)),
        pltpu.SemaphoreType.DMA((4, pieces)),
    ]


def exchange_kernel(step, n_in, n_vec, n_out, n_sum, given, ready, *refs):
    part = refs[0]
    ins = refs[1 : 1 + n_in]
    vectors = refs[1 + n_in : 1 + n_in + n_vec]
    rest = refs[1 + n_in + n_vec :]
    whole = rest[0]
    outs = rest[1 : 1 + n_out]
    sums_ref = rest[1 + n_out]
    own, send, receive, local = rest[2 + n_out : 6 + n_out]
    row_sums = RowSums(part, *rest[6 + n_out :])
    x_side, y_side, span, count = row_sums.x_side, row_sums.y_side, row_sums.span, row_sums.count
    greet([("ctx", x_side), ("ctx", y_side)])

    def copy(stage, j, source, target, side):
        one = remote(source, target, send.at[stage, j], receive.at[stage, j], "ctx", side)
        one.start()
        return one

    row_sums.first(given[0])
    ready(0, 1)
    row_sums.second()
    ready(1, 1 + n_in)
    params = [v[...] for v in vectors]
    third, fourth, kept = [], [], []
    totals = None
    for j in range(row_sums.pieces):
        at, total = row_sums.third(j)
        both = lambda ref: jnp.concatenate([ref[0, at], ref[1, at]], axis=0)
        sent, rows, sums = step(total, [both(r) for r in ins], params)
        own[0, at] = sent[:count]
        own[1, at] = sent[count:]
        third.append(
            (
                copy(0, j, own.at[:, at], whole.at[1, :, at], x_side),
                copy(1, j, own.at[:, at], whole.at[2, :, at], y_side),
            )
        )
        keep = pltpu.make_async_copy(own.at[:, at], whole.at[0, :, at], local.at[j])
        keep.start()
        kept.append(keep)
        for out, value in zip(outs, rows):
            out[0, at] = value[:count]
            out[1, at] = value[count:]
        totals = sums if totals is None else [a + b for a, b in zip(totals, sums)]
    for k in range(n_sum):
        sums_ref[k : k + 1] = totals[k]
    for j, at in enumerate(span):
        third[j][0].wait_recv()
        over_y = copy(2, j, whole.at[1, 0, at], whole.at[3, 0, at], y_side)
        third[j][1].wait_recv()
        over_x = copy(3, j, whole.at[2, 1, at], whole.at[3, 1, at], x_side)
        fourth.append((over_y, over_x))
    row_sums.end()
    for pair in third:
        for one in pair:
            one.wait_send()
    for pair in fourth:
        for one in pair:
            one.wait()
    for one in kept:
        one.wait()


def exchange(name, number, step, part, ins, vectors, out_types, n_sum):
    rows, width = ins[0].shape
    if lax.axis_size("ctx") != 4 or rows % 128:
        sent, outs, sums = step(collect(part), ins, vectors)
        return jnp.concatenate(spread(sent), axis=0), outs, sums
    pieces = 4
    half = rows // 2
    vmem = pl.BlockSpec(memory_space=pltpu.VMEM)
    halves = lambda v: v.reshape(2, half, width)
    anywhere = pl.BlockSpec(memory_space=pl.ANY)
    operands = [part.reshape(2, 2, 2, half, width), *map(halves, ins)]
    n_in = len(operands) + len(vectors)

    def kernel(*refs):
        exchange_kernel(step, len(ins), len(vectors), len(out_types), n_sum, *refs)

    whole, *outs, sums = pl.pallas_call(
        staged(kernel, len(operands), n_in, 2 + len(out_types)),
        out_shape=[
            jax.ShapeDtypeStruct((4, 2, half, width), bf16),
            *[jax.ShapeDtypeStruct((2, half, width), d) for d in out_types],
            jax.ShapeDtypeStruct((8, width), f32),
        ],
        in_specs=[*[anywhere] * len(operands), *[vmem] * len(vectors)],
        out_specs=[anywhere, *[vmem] * (len(out_types) + 1)],
        scratch_shapes=[
            *slots_for(operands),
            pltpu.VMEM((2, half, width), bf16),
            pltpu.SemaphoreType.DMA((4, pieces)),
            pltpu.SemaphoreType.DMA((4, pieces)),
            pltpu.SemaphoreType.DMA((pieces,)),
            *row_scratch(half, width, pieces),
        ],
        compiler_params=pltpu.CompilerParams(
            collective_id=number, has_side_effects=True, vmem_limit_bytes=56 << 20
        ),
        cost_estimate=pl.CostEstimate(
            flops=60 * rows * width, bytes_accessed=130 << 20, transcendentals=0
        ),
        name=name,
    )(*operands, *vectors)
    return (
        whole.reshape(4 * rows, width),
        [o.reshape(rows, width) for o in outs],
        [sums[k : k + 1] for k in range(n_sum)],
    )


def column_sum(values):
    return jnp.sum(values, axis=0, keepdims=True)


def first_step(total, rows, vectors):
    bias, gain, shift = vectors
    first, unit, inverse = layer_norm(rows[0].astype(f32) + total + bias, gain, shift)
    return first.astype(bf16), [unit, jnp.broadcast_to(inverse, unit.shape)], []


def second_step(total, rows, vectors):
    bias, gain_one, shift_one, gain, shift = vectors
    first = rows[0] * gain_one + shift_one
    out, unit, inverse = layer_norm(first + total + bias, gain, shift)
    upper = rows[1].astype(f32)
    grad = layer_norm_back(upper, unit, inverse, gain)
    low = grad.astype(bf16)
    sums = [column_sum(upper * unit), column_sum(upper), column_sum(low.astype(f32))]
    return low, [out.astype(bf16), grad], sums


def third_step(total, rows, vectors):
    (gain,) = vectors
    unit, inverse, upper = rows
    upper = upper + total
    grad = layer_norm_back(upper, unit, inverse, gain)
    low = grad.astype(bf16)
    sums = [column_sum(upper * unit), column_sum(upper), column_sum(low.astype(f32))]
    return low, [grad], sums


def block_weights(query, keys, place_rows, place_cols):
    scores = mm(query, keys, (1, 1))
    scores = jnp.where(jnp.abs(place_rows - place_cols) <= HALF, scores, masked_value)
    top = jnp.max(scores, axis=-1, keepdims=True)
    weights = jnp.exp((scores - top) * HDIM**-0.5)
    return weights, 1.0 / jnp.sum(weights, axis=-1, keepdims=True)


def attend_kernel(block, q_ref, k_ref, v_ref, rows_ref, cols_ref, out_ref):
    for start in range(0, q_ref.shape[0], block):
        span = pl.ds(start, block)
        weights, inverse = block_weights(q_ref[span, :], k_ref[...], rows_ref[span, :], cols_ref[...])
        out_ref[span, :] = (mm(weights.astype(bf16), v_ref[...], (1, 0)) * inverse).astype(bf16)


def attend_forward(qkv, place):
    length = qkv.shape[0]
    heads = qkv.shape[1] // (3 * HDIM)
    piece = lambda which: pl.BlockSpec((length, HDIM), lambda h, w=which: (0, w * heads + h))
    return pl.pallas_call(
        lambda *refs: attend_kernel(256, *refs),
        out_shape=jax.ShapeDtypeStruct((length, heads * HDIM), bf16),
        grid=(heads,),
        in_specs=[
            piece(0),
            piece(1),
            piece(2),
            pl.BlockSpec((length, 1), lambda h: (0, 0)),
            pl.BlockSpec((1, length), lambda h: (0, 0)),
        ],
        out_specs=pl.BlockSpec((length, HDIM), lambda h: (0, h)),
        compiler_params=pltpu.CompilerParams(vmem_limit_bytes=40 << 20),
        cost_estimate=pl.CostEstimate(
            flops=4 * heads * length * length * HDIM,
            bytes_accessed=8 * heads * length * HDIM,
            transcendentals=heads * length * length,
        ),
        name="attend_forward",
    )(qkv, qkv, qkv, place[:, None], place[None, :])


def attend_back_kernel(
    block, heads, q_ref, k_ref, v_ref, up_ref, rows_ref, cols_ref, out_ref, sum_k, sum_v
):
    scale = HDIM**-0.5
    head = pl.program_id(0)
    column = lambda which: pl.ds(pl.multiple_of((which * heads + head) * HDIM, HDIM), HDIM)
    for start in range(0, q_ref.shape[0], block):
        span = pl.ds(start, block)
        query = q_ref[span, :]
        upper = up_ref[span, :]
        weights, inverse = block_weights(query, k_ref[...], rows_ref[span, :], cols_ref[...])
        probs = weights * inverse
        grad_probs = mm(upper, v_ref[...], (1, 1))
        inner = jnp.sum(probs * grad_probs, axis=-1, keepdims=True)
        grad_scores = (probs * (grad_probs - inner)).astype(bf16)
        out_ref[span, column(0)] = (mm(grad_scores, k_ref[...], (1, 0)) * scale).astype(bf16)
        add_k = mm(grad_scores, query, (0, 0))
        add_v = mm(probs.astype(bf16), upper, (0, 0))
        if start == 0:
            sum_k[...] = add_k
            sum_v[...] = add_v
        else:
            sum_k[...] += add_k
            sum_v[...] += add_v
    out_ref[:, column(1)] = (sum_k[...] * scale).astype(bf16)
    out_ref[:, column(2)] = sum_v[...].astype(bf16)


def attend_backward(qkv, upper, place):
    length = qkv.shape[0]
    heads = qkv.shape[1] // (3 * HDIM)
    piece = lambda which: pl.BlockSpec((length, HDIM), lambda h, w=which: (0, w * heads + h))
    return pl.pallas_call(
        lambda *refs: attend_back_kernel(256, heads, *refs),
        out_shape=jax.ShapeDtypeStruct(qkv.shape, bf16),
        grid=(heads,),
        in_specs=[
            piece(0),
            piece(1),
            piece(2),
            piece(0),
            pl.BlockSpec((length, 1), lambda h: (0, 0)),
            pl.BlockSpec((1, length), lambda h: (0, 0)),
        ],
        out_specs=pl.BlockSpec(qkv.shape, lambda h: (0, 0)),
        scratch_shapes=[pltpu.VMEM((length, HDIM), f32), pltpu.VMEM((length, HDIM), f32)],
        compiler_params=pltpu.CompilerParams(vmem_limit_bytes=48 << 20),
        cost_estimate=pl.CostEstimate(
            flops=10 * heads * length * length * HDIM,
            bytes_accessed=14 * heads * length * HDIM,
            transcendentals=heads * length * length,
        ),
        name="attend_backward",
    )(qkv, qkv, qkv, upper, place[:, None], place[None, :])


def gram_of(moment_ref, total_ref, n):
    span = pl.ds(n * HDIM, HDIM)
    state = decay_rate * moment_ref[:, span].astype(f32) + total_ref[:, span].astype(f32)
    return lax.dot_general(
        state, state, (((0,), (0,)), ((), ())), precision=highest, preferred_element_type=f32
    )


def gram_kernel(moment_ref, total_ref, out_ref):
    for n in range(out_ref.shape[0]):
        out_ref[n] = gram_of(moment_ref, total_ref, n)


def apply_kernel(moment_ref, total_ref, factor_ref, out_ref):
    for n in range(factor_ref.shape[0]):
        span = pl.ds(n * HDIM, HDIM)
        state = decay_rate * moment_ref[:, span].astype(f32) + total_ref[:, span].astype(f32)
        out_ref[:, span] = jnp.dot(
            state, factor_ref[n], precision=highest, preferred_element_type=f32
        ).astype(bf16)


def whole_call(kernel, name, out, *operands, flops):
    vmem = pl.BlockSpec(memory_space=pltpu.VMEM)
    return pl.pallas_call(
        kernel,
        out_shape=out,
        in_specs=[vmem] * len(operands),
        out_specs=vmem,
        compiler_params=pltpu.CompilerParams(vmem_limit_bytes=32 << 20),
        cost_estimate=pl.CostEstimate(
            flops=flops, bytes_accessed=sum(o.size * o.dtype.itemsize for o in operands), transcendentals=0
        ),
        name=name,
    )(*operands)


def polynomial(grams):
    width = grams[0].shape[0]
    same = lax.broadcasted_iota(jnp.int32, (width, width), 0) == lax.broadcasted_iota(
        jnp.int32, (width, width), 1
    )
    unit = same.astype(f32)
    dot = lambda a, b: jnp.dot(a, b, precision=highest, preferred_element_type=f32)
    scaled, totals = [], []
    for gram in grams:
        square = jnp.sum(jnp.sum(gram * unit, axis=1, keepdims=True), axis=0, keepdims=True)
        inverse = 1.0 / (jnp.sqrt(square) + ortho_epsilon)
        scaled.append(gram * (inverse * inverse))
        totals.append(unit * inverse)
    for step in range(NS_STEPS):
        squares = [dot(g, g) for g in scaled]
        polys = [
            coef_first * unit + coef_second * g + coef_third * s for g, s in zip(scaled, squares)
        ]
        totals = [dot(q, p) for q, p in zip(totals, polys)]
        if step + 1 < NS_STEPS:
            halves = [dot(g, p) for g, p in zip(scaled, polys)]
            scaled = [dot(p, h) for p, h in zip(polys, halves)]
    return totals


def polynomial_kernel(gram_ref, out_ref):
    for n, total in enumerate(polynomial([gram_ref[n] for n in range(gram_ref.shape[0])])):
        out_ref[n] = total


def fold(symmetric):
    half = symmetric.shape[0] // 2
    last = symmetric[half:, half:]
    sides = jnp.concatenate([last[: half // 2], last[half // 2 :]], axis=1)
    return jnp.concatenate([symmetric[:half], sides], axis=0)


def unfold(folded):
    half = folded.shape[1] // 2
    top, sides = folded[:half], folded[half:]
    last = jnp.concatenate([sides[:, :half], sides[:, half:]], axis=0)
    return jnp.concatenate([top, jnp.concatenate([top[:, half:].T, last], axis=1)], axis=0)


FOLDED = 3 * HDIM // 4


def summed_polynomials(moments, totals, grams, pieces, send, receive, keep, between):
    each_group = totals[0].shape[1] // HDIM
    count = grams.shape[0]
    size = min(each_group, count // 2)
    each = size // 4
    f = lax.axis_index("fsdp")
    planes = [(f + i) % 4 for i in range(4)]
    batches = range(count // size)
    copies = []
    for b in batches:
        first = b * size
        for n in range(first, first + size):
            g = n // each_group
            grams[n] = fold(gram_of(moments[g], totals[g], n % each_group))
        copies.append([])
        for i in (1, 2, 3):
            one = remote(
                grams.at[pl.ds(first + planes[i] * each, each)],
                pieces.at[i - 1, pl.ds(b * each, each)],
                send.at[b, i - 1],
                receive.at[b, i - 1],
                "fsdp",
                planes[i],
            )
            one.start()
            copies[b].append(one)
    between()
    for b in batches:
        sums = [grams[b * size + f * each + n] for n in range(each)]
        for i in (1, 2, 3):
            copies[b][i - 1].wait()
            sums = [s + pieces[i - 1, b * each + n] for n, s in enumerate(sums)]
        for n, value in enumerate(polynomial([unfold(v) for v in sums])):
            keep(b, n, fold(value))
        yield b


def rows_to_owners(totals, targets, send, receive, local, first=0):
    rows = totals[0].shape[0] // 4
    c = lax.axis_index("ctx")
    copies = []
    for g, (total, target) in enumerate(zip(totals, targets)):
        for i in (3, 1, 2, 0):
            side = (c + i) % 4
            source = total.at[pl.ds(pl.multiple_of(side * rows, rows), rows)]
            if i:
                sems = send.at[first + g, i - 1], receive.at[first + g, i - 1]
                copies.append(remote(source, target.at[c], *sems, "ctx", side))
            else:
                copies.append(pltpu.make_async_copy(source, target.at[c], local.at[0, g]))
            copies[-1].start()
    return copies


class Chain:
    def __init__(self, b, size, factors, send, receive):
        self.b, self.size, self.factors, self.send, self.receive_sem = b, size, factors, send, receive
        self.f = lax.axis_index("fsdp")

    def copy(self, up, k, block, plane):
        each = self.size // 4
        ref = self.factors.at[pl.ds(self.b * self.size + block * each, each)]
        at = 2 * self.b + up, k
        return remote(ref, ref, self.send.at[at], self.receive_sem.at[at], "fsdp", plane)

    def leaving(self, up, k):
        f = self.f
        return self.copy(up, k, f - k, f + 1) if up else self.copy(up, k, f + k, f - 1)

    def coming(self, up, k):
        f = self.f
        return self.copy(up, k, f - 1 - k, f - 1) if up else self.copy(up, k, f + 1 + k, f + 1)

    def leaves(self, up, k):
        f = self.f
        return jnp.logical_and(f < 3, f >= k) if up else jnp.logical_and(f > 0, f + k <= 3)

    def comes(self, up, k):
        return self.f >= k + 1 if up else self.f <= 2 - k

    def start(self, k):
        for up in (1, 0):
            pl.when(self.leaves(up, k))(lambda up=up: self.leaving(up, k).start())

    def receive(self, k):
        for up in (1, 0):
            pl.when(self.comes(up, k))(lambda up=up: self.coming(up, k).wait_recv())

    def end(self):
        for k in range(3):
            for up in (1, 0):
                pl.when(self.leaves(up, k))(lambda up=up: self.leaving(up, k).wait_send())


def all_sides():
    c, f, t = (lax.axis_index(axis) for axis in ("ctx", "fsdp", "tp"))
    over = [(axis, (at + i) % 4) for axis, at in (("ctx", c), ("fsdp", f)) for i in (1, 2, 3)]
    return [*over, ("tp", 1 - t)]


def share_core(share, shared, send, receive, local):
    t = lax.axis_index("tp")
    copies = [
        remote(share, shared.at[t], send.at[0], receive.at[0], "tp", 1 - t),
        pltpu.make_async_copy(share, shared.at[t], local.at[0]),
    ]
    for one in copies:
        one.start()
    return copies


def feed_forward_kernel(given, ready, *refs):
    moments, totals, (base, vector, share), refs = refs[:2], refs[2:4], refs[4:7], refs[7:]
    grads_low, weights, refs = refs[:2], refs[2:4], refs[4:]
    (out, *grads), (shared, summed, vector_out), refs = refs[:3], refs[3:6], refs[6:]
    factors, send_c, receive_c, local, send_t, receive_t, local_t, send_f, receive_f = refs[:9]
    gram_refs, (sent_v, got_v, send_v, receive_v) = refs[9:13], refs[13:17]
    part, row_refs = refs[17], refs[18:]
    c, f, t = (lax.axis_index(axis) for axis in ("ctx", "fsdp", "tp"))
    partners = [
        ("tp", 1 - t),
        ("ctx", c + 1 - 2 * (c % 2)),
        ("ctx", c + 2 - 4 * (c // 2)),
        ("fsdp", f + 1 - 2 * (f % 2)),
        ("fsdp", f + 2 - 4 * (f // 2)),
    ]
    greet(all_sides())
    vector_copies = []

    def vector_start(k):
        one = remote(sent_v.at[k], got_v.at[k], send_v.at[k], receive_v.at[k], *partners[k])
        one.start()
        vector_copies.append(one)

    def vector_next(k):
        vector_copies[k].wait_recv()
        if k < 4:
            sent_v[k + 1] = sent_v[k] + got_v[k]
            vector_start(k + 1)
        else:
            vector_out[...] = sent_v[k] + got_v[k]

    sum_rows = RowSums(part, *row_refs)
    half, width = part.shape[3:]
    depth = grads_low[0].shape[1]
    block = width // 4

    def make_part(k, carry):
        rows = pl.ds(pl.multiple_of(k * 2 * half, 2 * half), 2 * half)
        for n in range(4):
            column = pl.ds(n * block, block)
            value = sum(mm(grads_low[i][rows, :], weights[i][column, :depth], (1, 1)) for i in range(2))
            value = value.astype(bf16)
            part[k // 2, k % 2, 0, :, column] = value[:half]
            part[k // 2, k % 2, 1, :, column] = value[half:]
        return carry

    ready(0, 7)
    started = rows_to_owners(totals, grads, send_c, receive_c, local)
    started += share_core(share, shared, send_t, receive_t, local_t)
    sent_v[0] = vector[...]
    vector_start(0)
    size = totals[0].shape[1] // HDIM
    each = size // 4
    chains = [Chain(b, size, factors, send_f, receive_f) for b in range(2)]

    def keep(b, n, value):
        factors[b * size + f * each + n] = value

    def between():
        ready(7, 11)
        lax.fori_loop(0, 4, make_part, 0)
        sum_rows.first(part)
        vector_next(0)

    for b in summed_polynomials(moments, totals, *gram_refs, keep, between):
        chains[b].start(0)
        if b == 0:
            vector_next(1)
            sum_rows.second()
    vector_next(2)
    for j in range(sum_rows.pieces):
        span, total = sum_rows.third(j)
        for h in range(2):
            value = total[h * sum_rows.count : (h + 1) * sum_rows.count]
            summed[h, span] = base[h, span] + value
    for k in range(3):
        for chain in chains:
            chain.receive(k)
            if k < 2:
                chain.start(k + 1)
        if k == 0:
            vector_next(3)
    out[...] = factors[...]
    vector_next(4)
    for chain in chains:
        chain.end()
    for one in vector_copies:
        one.wait_send()
    for one in started:
        one.wait()
    sum_rows.end()


def last_kernel(given, ready, *refs):
    moments, totals, (others, share), refs = refs[:3], refs[3:6], refs[6:8], refs[8:]
    orthos, (grads, shared), refs = refs[:3], refs[3:5], refs[5:]
    factors, stage, send_c, receive_c, local, send_t, receive_t, local_t, send_f, receive_f = refs[:10]
    gram_refs = refs[10:]
    rows = totals[0].shape[0] // 4
    count = totals[0].shape[1] // HDIM
    c, f = lax.axis_index("ctx"), lax.axis_index("fsdp")
    greet(all_sides())
    ready(0, 8)
    started = rows_to_owners(totals[:1], [grads], send_c, receive_c, local)
    started += share_core(share, shared, send_t, receive_t, local_t)

    def send_ortho(g, first, size, kind, factor):
        made = {n: unfold(factor(n)) for n in range(first, first + size)}
        wide = pl.ds(first * HDIM, size * HDIM)
        for i in (3, 1, 2, 0):
            side = (c + i) % 4
            span = pl.ds(pl.multiple_of(side * rows, rows), rows)
            for n in range(first, first + size):
                column = pl.ds(n * HDIM, HDIM)
                state = decay_rate * moments[g][span, column].astype(f32)
                state = state + totals[g][span, column].astype(f32)
                stage[g, i, :, column] = jnp.dot(
                    state, made[n], precision=highest, preferred_element_type=f32
                ).astype(bf16)
            source, target = stage.at[g, i, :, wide], orthos[g].at[c, :, wide]
            if i:
                sems = send_c.at[kind, i - 1], receive_c.at[kind, i - 1]
                copy = remote(source, target, *sems, "ctx", side)
            else:
                copy = pltpu.make_async_copy(source, target, local.at[0, kind])
            copy.start()
            started.append(copy)

    def between():
        for g in (1, 2):
            send_ortho(g, 0, count, g, lambda n: others[(g - 1) * count + n])

    size = count // 2
    each = size // 4
    chains = [Chain(b, size, factors, send_f, receive_f) for b in range(2)]

    def keep(b, n, value):
        factors[b * size + f * each + n] = value

    for b in summed_polynomials(moments[:1], totals[:1], *gram_refs, keep, between):
        chains[b].start(0)
    for k in range(2):
        for chain in chains:
            chain.receive(k)
            chain.start(k + 1)
    for b, chain in enumerate(chains):
        chain.receive(2)
        send_ortho(0, b * size, size, 3 + b, lambda n: factors[n])
    for chain in chains:
        chain.end()
    for one in started:
        one.wait()


def fits_planes(columns):
    return lax.axis_size("fsdp") == 4 and lax.axis_size("ctx") == 4 and columns == 8 * HDIM


def polynomials_over_planes(moment, total):
    count = total.shape[1] // HDIM
    flops = 12 * total.size * HDIM
    shape = jax.ShapeDtypeStruct((count, HDIM, HDIM), f32)
    grams = whole_call(gram_kernel, "grams", shape, moment, total, flops=flops)
    summed = lax.psum(grams, "fsdp")
    return whole_call(polynomial_kernel, "polynomials", shape, summed, flops=flops)


def shared_by_cores(share):
    other, t = swap_core(share), lax.axis_index("tp")
    return jnp.stack([jnp.where(t == m, share, other) for m in range(2)])


def feed_forward_slabs(moments, totals, share, grads_low, weights, base, vector):
    rows, columns = totals[0].shape
    if not fits_planes(columns):
        factors = [polynomials_over_planes(m, v) for m, v in zip(moments, totals)]
        summed = lax.psum(vector, ("fsdp", "ctx", "tp"))
        blocks = [from_blocks(v) for v in totals]
        depth = grads_low[0].shape[1]
        part = sum(mm(g, w[:, :depth], (1, 1)) for g, w in zip(grads_low, weights)).astype(bf16)
        return factors, blocks, shared_by_cores(share), base + collect(part), summed
    count = 2 * columns // HDIM
    vmem = pl.BlockSpec(memory_space=pltpu.VMEM)
    anywhere = pl.BlockSpec(memory_space=pl.ANY)
    block = jax.ShapeDtypeStruct((4, rows // 4, columns), bf16)
    half, width = base.shape[0] // 2, base.shape[1]
    lines = vector.size // HDIM
    dma = pltpu.SemaphoreType.DMA
    operands = [
        *moments,
        *totals,
        base.reshape(2, half, width),
        vector.reshape(lines, HDIM),
        share,
        *grads_low,
        *weights,
    ]
    factors, up, down, shared, summed, vector_sum = pl.pallas_call(
        staged(feed_forward_kernel, 11, 11, 6),
        out_shape=[
            jax.ShapeDtypeStruct((count, FOLDED, HDIM), f32),
            block,
            block,
            jax.ShapeDtypeStruct((2, *share.shape), share.dtype),
            jax.ShapeDtypeStruct((2, half, width), f32),
            jax.ShapeDtypeStruct((lines, HDIM), f32),
        ],
        in_specs=[anywhere] * 11,
        out_specs=[vmem, anywhere, anywhere, anywhere, vmem, vmem],
        scratch_shapes=[
            *slots_for(operands),
            pltpu.VMEM((count, FOLDED, HDIM), f32),
            *[dma((2, 3))] * 2,
            dma((1, 2)),
            *[dma((1,))] * 3,
            *[dma((4, 3))] * 2,
            pltpu.VMEM((count, FOLDED, HDIM), f32),
            pltpu.VMEM((3, count // 4, FOLDED, HDIM), f32),
            *[dma((2, 3))] * 2,
            *[pltpu.VMEM((5, lines, HDIM), f32)] * 2,
            *[dma((5,))] * 2,
            pltpu.VMEM((2, 2, 2, half, width), bf16),
            *row_scratch(half, width),
        ],
        compiler_params=pltpu.CompilerParams(
            collective_id=4, has_side_effects=True, vmem_limit_bytes=56 << 20
        ),
        cost_estimate=pl.CostEstimate(
            flops=24 * totals[0].size * HDIM, bytes_accessed=150 << 20, transcendentals=0
        ),
        name="feed_forward_slabs",
    )(*operands)
    return factors, [up, down], shared, summed.reshape(base.shape), vector_sum.reshape(vector.shape)


def last_slabs(moments, totals, factors, share):
    rows, columns = totals[0].shape
    own = jax.ShapeDtypeStruct((rows, columns), bf16)
    if not fits_planes(columns):
        factors = [polynomials_over_planes(moments[0], totals[0]), *factors]
        flops = 12 * totals[0].size * HDIM
        orthos = [
            from_blocks(whole_call(apply_kernel, "apply", own, m, v, p, flops=flops))
            for m, v, p in zip(moments, totals, factors)
        ]
        return orthos, from_blocks(totals[0]), shared_by_cores(share)
    count = columns // HDIM
    anywhere = pl.BlockSpec(memory_space=pl.ANY)
    block = jax.ShapeDtypeStruct((4, rows // 4, columns), bf16)
    dma = pltpu.SemaphoreType.DMA
    operands = [*moments, *totals, factors, share]
    *orthos, grads, shared = pl.pallas_call(
        staged(last_kernel, 8, 8, 5),
        out_shape=[*[block] * 4, jax.ShapeDtypeStruct((2, *share.shape), share.dtype)],
        in_specs=[anywhere] * 8,
        out_specs=[anywhere] * 5,
        scratch_shapes=[
            *slots_for(operands),
            pltpu.VMEM((count, FOLDED, HDIM), f32),
            pltpu.VMEM((3, 4, rows // 4, columns), bf16),
            *[dma((5, 3))] * 2,
            dma((1, 5)),
            *[dma((1,))] * 3,
            *[dma((4, 3))] * 2,
            pltpu.VMEM((count, FOLDED, HDIM), f32),
            pltpu.VMEM((3, count // 4, FOLDED, HDIM), f32),
            *[dma((2, 3))] * 2,
        ],
        compiler_params=pltpu.CompilerParams(
            collective_id=5, has_side_effects=True, vmem_limit_bytes=56 << 20
        ),
        cost_estimate=pl.CostEstimate(
            flops=36 * totals[0].size * HDIM, bytes_accessed=100 << 20, transcendentals=0
        ),
        name="last_slabs",
    )(*operands)
    return orthos, grads, shared


def pack_attention_kernel(qkv_ref, out_ref, stack_ref):
    wide = qkv_ref.shape[2]
    for which in range(3):
        stack_ref[0, :, which * wide : (which + 1) * wide] = qkv_ref[which].astype(bf16)
    stack_ref[0, :, 3 * wide :] = out_ref[...].T.astype(bf16)


def pack_attention(qkv, out):
    count = lax.axis_size("ctx")
    _, rows, columns = qkv.shape
    wide = columns // count
    return pl.pallas_call(
        pack_attention_kernel,
        out_shape=jax.ShapeDtypeStruct((count, rows, 4 * wide), bf16),
        grid=(count,),
        in_specs=[
            pl.BlockSpec((3, rows, wide), lambda i: (0, 0, i)),
            pl.BlockSpec((wide, rows), lambda i: (i, 0)),
        ],
        out_specs=pl.BlockSpec((1, rows, 4 * wide), lambda i: (i, 0, 0)),
        compiler_params=pltpu.CompilerParams(vmem_limit_bytes=56 << 20),
        cost_estimate=pl.CostEstimate(
            flops=qkv.size, bytes_accessed=8 * qkv.size, transcendentals=0
        ),
        name="pack_attention",
    )(qkv, out)


def attention_block_kernel(given, ready, qkv_ref, out_ref, block_ref, stage, send, receive, local):
    wide = stage.shape[2] // 4
    c = lax.axis_index("ctx")
    greet([("ctx", (c + i) % 4) for i in (1, 2, 3)])
    ready(0, 2)
    copies = []
    for i in (3, 1, 2, 0):
        side = (c + i) % 4
        span = pl.ds(pl.multiple_of(side * wide, wide), wide)
        for which in range(3):
            stage[i, :, which * wide : (which + 1) * wide] = qkv_ref[which, :, span].astype(bf16)
        stage[i, :, 3 * wide :] = out_ref[span, :].T.astype(bf16)
        if i:
            sems = send.at[i - 1], receive.at[i - 1]
            copies.append(remote(stage.at[i], block_ref.at[c], *sems, "ctx", side))
        else:
            copies.append(pltpu.make_async_copy(stage.at[i], block_ref.at[c], local.at[0]))
        copies[-1].start()
    for one in copies:
        one.wait()


def attention_block(qkv, out):
    _, rows, columns = qkv.shape
    if lax.axis_size("ctx") != 4 or columns % 512 or rows % 16:
        return to_blocks(pack_attention(qkv, out))
    shape = (4, rows, columns)
    anywhere = pl.BlockSpec(memory_space=pl.ANY)
    block = pl.pallas_call(
        staged(attention_block_kernel, 2, 2, 1),
        out_shape=jax.ShapeDtypeStruct(shape, bf16),
        in_specs=[anywhere] * 2,
        out_specs=anywhere,
        scratch_shapes=[
            *slots_for([qkv, out]),
            pltpu.VMEM(shape, bf16),
            *[pltpu.SemaphoreType.DMA((3,))] * 2,
            pltpu.SemaphoreType.DMA((1,)),
        ],
        compiler_params=pltpu.CompilerParams(
            collective_id=6, has_side_effects=True, vmem_limit_bytes=56 << 20
        ),
        cost_estimate=pl.CostEstimate(flops=qkv.size, bytes_accessed=30 << 20, transcendentals=0),
        name="attention_block",
    )(qkv, out)
    return block.reshape(4 * rows, columns)


def pack_feed_forward(up, down):
    count = lax.axis_size("ctx")
    rows = up.shape[0]
    low = lambda v: v.astype(bf16)
    up_cut = low(up).reshape(rows, count, -1).transpose(1, 0, 2)
    down_cut = low(down).T.reshape(rows, count, -1).transpose(1, 0, 2)
    return up_cut, down_cut


def finish(name, scale, grads, orthos, moments, weights):
    count, rows, columns = grads.shape
    three = [len(s.shape) == 3 for s in weights]
    tall = [len(s.shape) == 2 and s.shape[0] != rows for s in weights]
    number = len(weights)
    wide = columns // 4 if any(three) else columns
    specs = []
    for is_three, is_tall in zip(three, tall):
        if is_three:
            specs.append(pl.BlockSpec((3, rows, wide), lambda i: (0, 0, i)))
        elif is_tall:
            specs.append(pl.BlockSpec((wide, rows), lambda i: (i, 0)))
        else:
            specs.append(pl.BlockSpec((rows, wide), lambda i: (0, i)))

    def kernel(grad_ref, ortho_ref, *refs):
        for j in range(number):
            moment, weight = refs[j], refs[number + j]
            grad_out, state_out, master_out = refs[2 * number + 3 * j : 2 * number + 3 * j + 3]
            for w in range(3) if three[j] else (None,):
                start = (3 if w is None and any(three) else w or 0) * wide
                cut = lambda ref: ref[0, :, start : start + wide].astype(f32)
                grad, ortho = cut(grad_ref), cut(ortho_ref)
                if tall[j]:
                    grad, ortho = grad.T, ortho.T
                at = ... if w is None else w
                grad_out[at] = grad
                state_out[at] = decay_rate * moment[at] + grad
                master_out[at] = weight[at] - scale * ortho

    outs = pl.pallas_call(
        kernel,
        out_shape=[jax.ShapeDtypeStruct(s.shape, f32) for s in weights for _ in range(3)],
        grid=(count,),
        in_specs=[*[pl.BlockSpec((1, rows, columns), lambda i: (i, 0, 0))] * 2, *specs, *specs],
        out_specs=[spec for spec in specs for _ in range(3)],
        compiler_params=pltpu.CompilerParams(vmem_limit_bytes=56 << 20),
        cost_estimate=pl.CostEstimate(
            flops=4 * grads.size, bytes_accessed=24 * grads.size, transcendentals=0
        ),
        name=name,
    )(grads, orthos, *moments, *weights)
    return outs[0::3], outs[1::3], outs[2::3]


def over_ctx(stack):
    return lax.all_to_all(stack, "ctx", split_axis=0, concat_axis=0, tiled=True)


def to_blocks(stack):
    moved = over_ctx(stack)
    return moved.reshape(-1, moved.shape[-1])


def from_blocks(block):
    return over_ctx(block.reshape(lax.axis_size("ctx"), -1, block.shape[-1]))


def body(
    inputs,
    segment_ids,
    cotangent,
    w_qkv,
    w_out,
    w_up,
    w_down,
    bias_qv,
    bias_up,
    bias_res,
    norm_gain,
    norm_shift,
    moment_qkv,
    moment_out,
    moment_up,
    moment_down,
    moment_bqv,
    moment_bup,
    moment_bres,
    moment_gain,
    moment_shift,
):
    count_c = lax.axis_size("ctx")
    count_f = lax.axis_size("fsdp")
    c = lax.axis_index("ctx")
    t = lax.axis_index("tp")
    rows = inputs.shape[2]
    width = inputs.shape[3]
    length = rows * count_c
    token_total = inputs.shape[0] * inputs.shape[1] * count_f * length
    e = w_qkv.shape[2] // count_c
    u = w_up.shape[1] // count_c

    own_micro = lambda v: lax.dynamic_index_in_dim(v, t, 0, keepdims=False)[0]
    row_low = own_micro(inputs)
    upper = own_micro(cotangent)
    segments = own_micro(segment_ids)
    index = jnp.arange(count_c)
    order = index ^ c if count_c == 4 else index
    place = (segments * (length + HALF + 1) + jnp.arange(length, dtype=jnp.int32)).reshape(count_c, rows)
    place = jnp.take(place, order, axis=0).reshape(length)

    after = lambda value, *others: lax.optimization_barrier((value, *others))[0]
    attn_block = attention_block(w_qkv, w_out)
    up_late, down_late, *moments_late, _ = lax.optimization_barrier(
        (w_up, w_down, moment_qkv, moment_out, moment_up, moment_down, attn_block)
    )
    up_stack, down_stack = pack_feed_forward(up_late, down_late)
    gather_z = lambda v: lax.all_gather(v, "fsdp", axis=0, tiled=True)
    row_first, upper, _ = lax.optimization_barrier((row_low, upper, attn_block))
    xs = jnp.concatenate(spread(row_first), axis=0)
    both_block = to_blocks(after(jnp.concatenate([up_stack, down_stack], axis=2), xs))
    up_block, down_block = both_block[:, :u], both_block[:, u:]
    attn_g, up_g, down_g = map(gather_z, (attn_block, up_block, down_block))
    attn_moments = to_blocks(after(pack_attention(*moments_late[:2]), both_block))
    moment_stack = jnp.concatenate(pack_feed_forward(*moments_late[2:]), axis=2)
    moment_stack = after(moment_stack, both_block)
    attn_g = after(attn_g, moment_stack)
    attn_w = (attn_g, swap_core(attn_g))

    bias_q = lax.dynamic_slice_in_dim(bias_qv, c * e, e, 1)
    bias_u = lax.dynamic_slice_in_dim(bias_up, c * u, u, 0)
    small = jnp.concatenate([bias_q.reshape(-1), bias_u])
    small_pair = (small, swap_core(small))
    cores = range(2)

    qkv = []
    for i in cores:
        shift = jnp.concatenate([small_pair[i][:e], jnp.zeros((e,), f32), small_pair[i][e : 2 * e]])
        qkv.append((mm(xs, attn_w[i][:, : 3 * e], (1, 0)) + shift).astype(bf16))
    context = [attend_forward(qkv[i], place) for i in cores]
    part = sum(mm(context[i], attn_w[i][:, 3 * e :], (1, 1)) for i in cores).astype(bf16)
    row = lambda matrix, index: matrix[index : index + 1]
    part = after(part, attn_moments)
    first_all, (first_unit, first_inverse), _ = exchange(
        "first_rows",
        1,
        first_step,
        part,
        [row_low],
        [row(bias_res, 0), row(norm_gain, 0), row(norm_shift, 0)],
        [f32, f32],
        0,
    )
    moment_block = to_blocks(after(moment_stack, first_all))
    moments = [attn_moments, moment_block[:, :u], moment_block[:, u:]]
    up_g = after(up_g, first_all)
    up_w = (up_g, swap_core(up_g))
    pre_act = [mm(first_all, up_w[i], (1, 0)) + small_pair[i][2 * e :] for i in cores]
    active = [gelu_tanh(p).astype(bf16) for p in pre_act]
    down_g = after(down_g, moment_block, *active)
    down_w = (down_g, swap_core(down_g))
    part = sum(mm(active[i], down_w[i], (1, 1)) for i in cores).astype(bf16)
    branch_all, (out_rows, grad_second), second_sums = exchange(
        "second_rows",
        2,
        second_step,
        part,
        [first_unit, upper],
        [row(bias_res, 1), row(norm_gain, 0), row(norm_shift, 0), row(norm_gain, 1), row(norm_shift, 1)],
        [bf16, f32],
        3,
    )

    def pair_sum(terms):
        return (terms[0] + swap_core(terms[1].astype(bf16)).astype(f32)).astype(bf16)

    scatter_z = lambda v: lax.psum_scatter(v, "fsdp", scatter_dimension=0, tiled=True)
    term_down = [None, mm(branch_all, active[1], (0, 0)).astype(bf16)]
    term_down[0] = mm(after(branch_all, term_down[1]), active[0], (0, 0))
    branch_all, *term_down = lax.optimization_barrier((branch_all, *term_down))
    down_sum = pair_sum(term_down)

    def before_gelu(i, rows):
        return jax.vjp(gelu_tanh, pre_act[i])[1](mm(rows, down_w[i], (1, 0)))[0].astype(bf16)

    grad_pre = [before_gelu(0, branch_all)]
    branch_all, down_sum, grad_pre[0] = lax.optimization_barrier((branch_all, down_sum, grad_pre[0]))
    grad_pre.append(before_gelu(1, branch_all))
    part = sum(mm(grad_pre[i], up_w[i], (1, 1)) for i in cores).astype(bf16)
    term_up = [None, mm(first_all, grad_pre[1], (0, 0)).astype(bf16)]
    term_up[0] = mm(after(first_all, term_up[1]), grad_pre[0], (0, 0))
    part, up_sum = lax.optimization_barrier((part, pair_sum(term_up)))
    attended_all, (grad_first,), first_sums = exchange(
        "third_rows",
        3,
        third_step,
        part,
        [first_unit, first_inverse, grad_second],
        [row(norm_gain, 0)],
        [f32],
        3,
    )
    grad_qkv_low, term_qkv, term_out = [None, None], [None, None], [None, None]
    rows_for = attended_all
    for i in (1, 0):
        grad_context = mm(rows_for, attn_w[i][:, 3 * e :], (1, 0)).astype(bf16)
        grad_qkv_low[i] = attend_backward(qkv[i], grad_context, place)
        term_qkv[i] = mm(xs, grad_qkv_low[i], (0, 0))
        term_out[i] = mm(rows_for, context[i], (0, 0))
        if i:
            term_qkv[i], term_out[i] = term_qkv[i].astype(bf16), term_out[i].astype(bf16)
            rows_for = after(attended_all, term_qkv[i], term_out[i])
    attn_sum = jnp.concatenate([pair_sum(term_qkv), pair_sum(term_out)], axis=1)
    down_total, up_total = map(scatter_z, (down_sum, up_sum))
    *lows, attn_sum = lax.optimization_barrier((*grad_qkv_low, attn_sum))

    qv_sums = []
    for i in cores:
        sums_i = jnp.sum(grad_qkv_low[i].astype(f32), axis=0)
        qv_sums.append(jnp.stack([sums_i[:e], sums_i[2 * e :]]))
    up_sums = [jnp.sum(g.astype(f32), axis=0) for g in grad_pre]
    side = lambda pair: [jnp.where(t == m, pair[0], pair[1]) for m in range(2)]
    bqv_all = jnp.stack(
        [
            lax.dynamic_update_slice_in_dim(jnp.zeros((2, count_c * e), f32), v, c * e, 1)
            for v in side(qv_sums)
        ]
    )
    bup_all = jnp.stack(
        [
            lax.dynamic_update_slice_in_dim(jnp.zeros((count_c * u,), f32), v, c * u, 0)
            for v in side(up_sums)
        ]
    )
    rest = jnp.concatenate(
        [
            first_sums[2],
            second_sums[2],
            first_sums[0],
            second_sums[0],
            first_sums[1],
            second_sums[1],
        ],
        axis=0,
    )
    flat = jnp.concatenate([bqv_all.reshape(-1), bup_all.reshape(-1), rest.reshape(-1)])

    attn_total = scatter_z(attn_sum)
    step_scale = matrix_rate * math.sqrt(width / HDIM)
    factors, gradient_blocks, layer_out, input_rows, flat = feed_forward_slabs(
        moments[1:], (up_total, down_total), after(out_rows, attn_sum), lows, attn_w, grad_first, flat
    )
    orthos, attn_gradients, input_grad = last_slabs(
        moments, (attn_total, up_total, down_total), factors, input_rows
    )
    gradient_blocks, flat, orthos = lax.optimization_barrier((gradient_blocks, flat, orthos))
    up_done, down_done = [
        finish(name, step_scale, *operands)
        for name, *operands in (
            ("up_finish", gradient_blocks[0], orthos[1], (moment_up,), (w_up,)),
            ("down_finish", gradient_blocks[1], orthos[2], (moment_down,), (w_down,)),
        )
    ]
    attn_done = finish(
        "attention_finish",
        step_scale,
        attn_gradients,
        orthos[0],
        (moment_qkv, moment_out),
        (w_qkv, w_out),
    )
    grads, states, masters = [
        [*attn_done[k], *up_done[k], *down_done[k]] for k in range(3)
    ]

    cut = bqv_all.size
    cut_two = cut + bup_all.size
    grad_bqv = lax.dynamic_index_in_dim(flat[:cut].reshape(bqv_all.shape), t, 0, keepdims=False)
    grad_bup = lax.dynamic_index_in_dim(flat[cut:cut_two].reshape(bup_all.shape), t, 0, keepdims=False)
    rest = flat[cut_two:].reshape(3, 2, width)
    vector_grads = (grad_bqv, grad_bup, rest[0], rest[1], rest[2])
    vector_states = [
        decay_rate * m + g
        for m, g in zip(
            (moment_bqv, moment_bup, moment_bres, moment_gain, moment_shift), vector_grads
        )
    ]
    vector_step = 1.0 / math.sqrt(token_total)
    vector_masters = [
        v - vector_step * s
        for v, s in zip((bias_qv, bias_up, bias_res, norm_gain, norm_shift), vector_states)
    ]
    return (
        layer_out[:, None],
        input_grad[:, None],
        *grads,
        *vector_grads,
        *states,
        *vector_states,
        *masters,
        *vector_masters,
    )


def solution(mesh):
    rows = P(None, "fsdp", "ctx", None)
    matrices = (
        P(None, ("fsdp", "ctx"), "tp"),
        P("tp", ("fsdp", "ctx")),
        P(("fsdp", "ctx"), "tp"),
        P("tp", ("fsdp", "ctx")),
    )
    vectors = (P(None, "tp"), P("tp"), P(), P(), P())
    return jax.shard_map(
        body,
        mesh=mesh,
        in_specs=(rows, P(None, "fsdp", None), rows, *matrices, *vectors, *matrices, *vectors),
        out_specs=(rows, rows, *((*matrices, *vectors) * 3)),
        check_vma=False,
    )
```

```python
import math

import jax
import jax.numpy as jnp
from jax import lax
from jax.experimental import pallas as pl
from jax.experimental.pallas import tpu as pltpu
from jax.sharding import PartitionSpec as P

HDIM = 128
NS_STEPS = 5
HALF = 512

bf16 = jnp.bfloat16
f32 = jnp.float32
highest = lax.Precision.HIGHEST
norm_epsilon = 1e-05
ortho_epsilon = 1e-07
coef_first = 3.4445
coef_second = -4.775
coef_third = 2.0315
decay_rate = 0.5
matrix_rate = 0.25
masked_value = -1e30

CORE = [(0, 1), (1, 0)]


def xor_pairs(size, mask):
    return [(i, i ^ mask) for i in range(size)]


def swap_core(value):
    return lax.ppermute(value, "tp", CORE)


def swap_ctx(value, mask):
    return lax.ppermute(value, "ctx", xor_pairs(4, mask))


def swap_fsdp(value, mask):
    return lax.ppermute(value, "fsdp", xor_pairs(4, mask))


def mm(left, right, dims):
    return lax.dot_general(left, right, ((dims[:1], dims[1:]), ((), ())), preferred_element_type=f32)


def spread(own):
    if lax.axis_size("ctx") != 4:
        whole = lax.all_gather(own, "ctx", axis=0, tiled=False)
        return [whole[i] for i in range(whole.shape[0])]
    half = own.shape[0] // 2
    from_x = swap_ctx(own, 1)
    from_y = swap_ctx(own, 2)
    top = swap_ctx(from_x[:half], 2)
    low = swap_ctx(from_y[half:], 1)
    return [own, from_x, from_y, jnp.concatenate([top, low], axis=0)]


def collect(partial):
    count = lax.axis_size("ctx")
    rows = partial.shape[0] // count
    if count != 4:
        return lax.psum_scatter(partial, "ctx", scatter_dimension=0, tiled=True).astype(f32)
    half = rows // 2
    part = [partial[k * rows : (k + 1) * rows] for k in range(4)]
    over_x = swap_ctx(jnp.concatenate([part[1][:half], part[3][:half]], axis=0), 1).astype(f32)
    over_y = swap_ctx(jnp.concatenate([part[2][half:], part[3][half:]], axis=0), 2).astype(f32)
    then_y = swap_ctx((part[2][:half].astype(f32) + over_x[half:]).astype(bf16), 2)
    then_x = swap_ctx((part[1][half:].astype(f32) + over_y[half:]).astype(bf16), 1)
    own = part[0].astype(f32)
    return jnp.concatenate(
        [
            own[:half] + over_x[:half] + then_y.astype(f32),
            own[half:] + over_y[:half] + then_x.astype(f32),
        ],
        axis=0,
    )


def layer_norm(values, gain_row, shift_row):
    center = values - jnp.mean(values, axis=-1, keepdims=True)
    inverse = lax.rsqrt(jnp.mean(center * center, axis=-1, keepdims=True) + norm_epsilon)
    normed = center * inverse
    return (normed * gain_row + shift_row, normed, inverse)


def layer_norm_back(grad_upper, normed, inverse, gain_row):
    grad_normed = grad_upper * gain_row
    mean_grad = jnp.mean(grad_normed, axis=-1, keepdims=True)
    mean_dot = jnp.mean(grad_normed * normed, axis=-1, keepdims=True)
    return inverse * (grad_normed - mean_grad - normed * mean_dot)


def gelu_tanh(values):
    return jax.nn.gelu(values, approximate=True)


MESH = pl.DeviceIdType.MESH


def remote(source, target, send, receive, axis, index):
    return pltpu.make_async_remote_copy(
        src_ref=source,
        dst_ref=target,
        send_sem=send,
        recv_sem=receive,
        device_id={axis: index},
        device_id_type=MESH,
    )


def greet(axis_indices):
    barrier = pltpu.get_barrier_semaphore()
    for axis, index in axis_indices:
        pl.semaphore_signal(barrier, inc=1, device_id={axis: index}, device_id_type=MESH)
    pl.semaphore_wait(barrier, len(axis_indices))


def staged(kernel, count, n_in, n_out):
    def run(*refs):
        given, others, rest = refs[:count], refs[count : n_in + n_out], refs[n_in + n_out :]
        slots, sems, rest = rest[:count], rest[count], rest[count + 1 :]
        copies = [pltpu.make_async_copy(g, v, sems.at[k]) for k, (g, v) in enumerate(zip(given, slots))]
        for one in copies:
            one.start()

        def ready(first, last):
            for one in copies[first:last]:
                one.wait()

        kernel(given, ready, *slots, *others, *rest)

    return run


def slots_for(operands):
    return [
        *[pltpu.VMEM(o.shape, o.dtype) for o in operands],
        pltpu.SemaphoreType.DMA((len(operands),)),
    ]


class RowSums:
    def __init__(self, part, from_x, from_y, then_y, then_x, to_y, to_x, send, receive):
        self.part, self.send, self.receive = part, send, receive
        self.from_x, self.from_y, self.then_y, self.then_x = from_x, from_y, then_y, then_x
        self.to_y, self.to_x = to_y, to_x
        self.pieces, self.count = to_y.shape[:2]
        self.span = [pl.ds(j * self.count, self.count) for j in range(self.pieces)]
        c = lax.axis_index("ctx")
        self.x_side = c + 1 - 2 * (c % 2)
        self.y_side = c + 2 - 4 * (c // 2)
        self.one, self.two = [], []

    def copy(self, stage, j, source, target, side):
        copy = remote(source, target, self.send.at[stage, j], self.receive.at[stage, j], "ctx", side)
        copy.start()
        return copy

    def first(self, part):
        for j in range(self.pieces):
            self.one.append(
                (
                    self.copy(0, j, part.at[:, 1, 0, self.span[j]], self.from_x.at[j], self.x_side),
                    self.copy(1, j, part.at[1, :, 1, self.span[j]], self.from_y.at[j], self.y_side),
                )
            )

    def second(self):
        for j in range(self.pieces):
            at = self.span[j]
            self.one[j][0].wait_recv()
            value = self.part[1, 0, 0, at].astype(f32) + self.from_x[j, 1].astype(f32)
            self.to_y[j] = value.astype(bf16)
            over_y = self.copy(2, j, self.to_y.at[j], self.then_y.at[j], self.y_side)
            self.one[j][1].wait_recv()
            value = self.part[0, 1, 1, at].astype(f32) + self.from_y[j, 1].astype(f32)
            self.to_x[j] = value.astype(bf16)
            over_x = self.copy(3, j, self.to_x.at[j], self.then_x.at[j], self.x_side)
            self.two.append((over_y, over_x))

    def third(self, j):
        at = self.span[j]
        self.two[j][0].wait_recv()
        self.two[j][1].wait_recv()
        top = self.part[0, 0, 0, at].astype(f32) + self.from_x[j, 0].astype(f32)
        low = self.part[0, 0, 1, at].astype(f32) + self.from_y[j, 0].astype(f32)
        top = top + self.then_y[j].astype(f32)
        low = low + self.then_x[j].astype(f32)
        return at, jnp.concatenate([top, low], axis=0)

    def end(self):
        for pair in (*self.one, *self.two):
            for one in pair:
                one.wait_send()


def row_scratch(half, width, pieces=4):
    count = half // pieces
    return [
        pltpu.VMEM((pieces, 2, count, width), bf16),
        pltpu.VMEM((pieces, 2, count, width), bf16),
        *[pltpu.VMEM((pieces, count, width), bf16)] * 4,
        pltpu.SemaphoreType.DMA((4, pieces)),
        pltpu.SemaphoreType.DMA((4, pieces)),
    ]


def exchange_kernel(step, n_in, n_vec, n_out, n_sum, given, ready, *refs):
    part = refs[0]
    ins = refs[1 : 1 + n_in]
    vectors = refs[1 + n_in : 1 + n_in + n_vec]
    rest = refs[1 + n_in + n_vec :]
    whole = rest[0]
    outs = rest[1 : 1 + n_out]
    sums_ref = rest[1 + n_out]
    own, send, receive, local = rest[2 + n_out : 6 + n_out]
    row_sums = RowSums(part, *rest[6 + n_out :])
    x_side, y_side, span, count = row_sums.x_side, row_sums.y_side, row_sums.span, row_sums.count
    greet([("ctx", x_side), ("ctx", y_side)])

    def copy(stage, j, source, target, side):
        one = remote(source, target, send.at[stage, j], receive.at[stage, j], "ctx", side)
        one.start()
        return one

    row_sums.first(given[0])
    ready(0, 1)
    row_sums.second()
    ready(1, 1 + n_in)
    params = [v[...] for v in vectors]
    third, fourth, kept = [], [], []
    totals = None
    for j in range(row_sums.pieces):
        at, total = row_sums.third(j)
        both = lambda ref: jnp.concatenate([ref[0, at], ref[1, at]], axis=0)
        sent, rows, sums = step(total, [both(r) for r in ins], params)
        own[0, at] = sent[:count]
        own[1, at] = sent[count:]
        third.append(
            (
                copy(0, j, own.at[:, at], whole.at[1, :, at], x_side),
                copy(1, j, own.at[:, at], whole.at[2, :, at], y_side),
            )
        )
        keep = pltpu.make_async_copy(own.at[:, at], whole.at[0, :, at], local.at[j])
        keep.start()
        kept.append(keep)
        for out, value in zip(outs, rows):
            out[0, at] = value[:count]
            out[1, at] = value[count:]
        totals = sums if totals is None else [a + b for a, b in zip(totals, sums)]
    for k in range(n_sum):
        sums_ref[k : k + 1] = totals[k]
    for j, at in enumerate(span):
        third[j][0].wait_recv()
        over_y = copy(2, j, whole.at[1, 0, at], whole.at[3, 0, at], y_side)
        third[j][1].wait_recv()
        over_x = copy(3, j, whole.at[2, 1, at], whole.at[3, 1, at], x_side)
        fourth.append((over_y, over_x))
    row_sums.end()
    for pair in third:
        for one in pair:
            one.wait_send()
    for pair in fourth:
        for one in pair:
            one.wait()
    for one in kept:
        one.wait()


def exchange(name, number, step, part, ins, vectors, out_types, n_sum):
    rows, width = ins[0].shape
    if lax.axis_size("ctx") != 4 or rows % 128:
        sent, outs, sums = step(collect(part), ins, vectors)
        return jnp.concatenate(spread(sent), axis=0), outs, sums
    pieces = 4
    half = rows // 2
    vmem = pl.BlockSpec(memory_space=pltpu.VMEM)
    halves = lambda v: v.reshape(2, half, width)
    anywhere = pl.BlockSpec(memory_space=pl.ANY)
    operands = [part.reshape(2, 2, 2, half, width), *map(halves, ins)]
    n_in = len(operands) + len(vectors)

    def kernel(*refs):
        exchange_kernel(step, len(ins), len(vectors), len(out_types), n_sum, *refs)

    whole, *outs, sums = pl.pallas_call(
        staged(kernel, len(operands), n_in, 2 + len(out_types)),
        out_shape=[
            jax.ShapeDtypeStruct((4, 2, half, width), bf16),
            *[jax.ShapeDtypeStruct((2, half, width), d) for d in out_types],
            jax.ShapeDtypeStruct((8, width), f32),
        ],
        in_specs=[*[anywhere] * len(operands), *[vmem] * len(vectors)],
        out_specs=[anywhere, *[vmem] * (len(out_types) + 1)],
        scratch_shapes=[
            *slots_for(operands),
            pltpu.VMEM((2, half, width), bf16),
            pltpu.SemaphoreType.DMA((4, pieces)),
            pltpu.SemaphoreType.DMA((4, pieces)),
            pltpu.SemaphoreType.DMA((pieces,)),
            *row_scratch(half, width, pieces),
        ],
        compiler_params=pltpu.CompilerParams(
            collective_id=number, has_side_effects=True, vmem_limit_bytes=56 << 20
        ),
        cost_estimate=pl.CostEstimate(
            flops=60 * rows * width, bytes_accessed=130 << 20, transcendentals=0
        ),
        name=name,
    )(*operands, *vectors)
    return (
        whole.reshape(4 * rows, width),
        [o.reshape(rows, width) for o in outs],
        [sums[k : k + 1] for k in range(n_sum)],
    )


def column_sum(values):
    return jnp.sum(values, axis=0, keepdims=True)


def first_step(total, rows, vectors):
    bias, gain, shift = vectors
    first, unit, inverse = layer_norm(rows[0].astype(f32) + total + bias, gain, shift)
    return first.astype(bf16), [unit, jnp.broadcast_to(inverse, unit.shape)], []


def second_step(total, rows, vectors):
    bias, gain_one, shift_one, gain, shift = vectors
    first = rows[0] * gain_one + shift_one
    out, unit, inverse = layer_norm(first + total + bias, gain, shift)
    upper = rows[1].astype(f32)
    grad = layer_norm_back(upper, unit, inverse, gain)
    low = grad.astype(bf16)
    sums = [column_sum(upper * unit), column_sum(upper), column_sum(low.astype(f32))]
    return low, [out.astype(bf16), grad], sums


def third_step(total, rows, vectors):
    (gain,) = vectors
    unit, inverse, upper = rows
    upper = upper + total
    grad = layer_norm_back(upper, unit, inverse, gain)
    low = grad.astype(bf16)
    sums = [column_sum(upper * unit), column_sum(upper), column_sum(low.astype(f32))]
    return low, [grad], sums


def block_weights(query, keys, place_rows, place_cols):
    scores = mm(query, keys, (1, 1))
    scores = jnp.where(jnp.abs(place_rows - place_cols) <= HALF, scores, masked_value)
    top = jnp.max(scores, axis=-1, keepdims=True)
    weights = jnp.exp((scores - top) * HDIM**-0.5)
    return weights, 1.0 / jnp.sum(weights, axis=-1, keepdims=True)


def attend_kernel(block, q_ref, k_ref, v_ref, rows_ref, cols_ref, out_ref):
    for start in range(0, q_ref.shape[0], block):
        span = pl.ds(start, block)
        weights, inverse = block_weights(q_ref[span, :], k_ref[...], rows_ref[span, :], cols_ref[...])
        out_ref[span, :] = (mm(weights.astype(bf16), v_ref[...], (1, 0)) * inverse).astype(bf16)


def attend_forward(qkv, place):
    length = qkv.shape[0]
    heads = qkv.shape[1] // (3 * HDIM)
    piece = lambda which: pl.BlockSpec((length, HDIM), lambda h, w=which: (0, w * heads + h))
    return pl.pallas_call(
        lambda *refs: attend_kernel(256, *refs),
        out_shape=jax.ShapeDtypeStruct((length, heads * HDIM), bf16),
        grid=(heads,),
        in_specs=[
            piece(0),
            piece(1),
            piece(2),
            pl.BlockSpec((length, 1), lambda h: (0, 0)),
            pl.BlockSpec((1, length), lambda h: (0, 0)),
        ],
        out_specs=pl.BlockSpec((length, HDIM), lambda h: (0, h)),
        compiler_params=pltpu.CompilerParams(vmem_limit_bytes=40 << 20),
        cost_estimate=pl.CostEstimate(
            flops=4 * heads * length * length * HDIM,
            bytes_accessed=8 * heads * length * HDIM,
            transcendentals=heads * length * length,
        ),
        name="attend_forward",
    )(qkv, qkv, qkv, place[:, None], place[None, :])


def attend_back_kernel(
    block, heads, q_ref, k_ref, v_ref, up_ref, rows_ref, cols_ref, out_ref, sum_k, sum_v
):
    scale = HDIM**-0.5
    head = pl.program_id(0)
    column = lambda which: pl.ds(pl.multiple_of((which * heads + head) * HDIM, HDIM), HDIM)
    for start in range(0, q_ref.shape[0], block):
        span = pl.ds(start, block)
        query = q_ref[span, :]
        upper = up_ref[span, :]
        weights, inverse = block_weights(query, k_ref[...], rows_ref[span, :], cols_ref[...])
        probs = weights * inverse
        grad_probs = mm(upper, v_ref[...], (1, 1))
        inner = jnp.sum(probs * grad_probs, axis=-1, keepdims=True)
        grad_scores = (probs * (grad_probs - inner)).astype(bf16)
        out_ref[span, column(0)] = (mm(grad_scores, k_ref[...], (1, 0)) * scale).astype(bf16)
        add_k = mm(grad_scores, query, (0, 0))
        add_v = mm(probs.astype(bf16), upper, (0, 0))
        if start == 0:
            sum_k[...] = add_k
            sum_v[...] = add_v
        else:
            sum_k[...] += add_k
            sum_v[...] += add_v
    out_ref[:, column(1)] = (sum_k[...] * scale).astype(bf16)
    out_ref[:, column(2)] = sum_v[...].astype(bf16)


def attend_backward(qkv, upper, place):
    length = qkv.shape[0]
    heads = qkv.shape[1] // (3 * HDIM)
    piece = lambda which: pl.BlockSpec((length, HDIM), lambda h, w=which: (0, w * heads + h))
    return pl.pallas_call(
        lambda *refs: attend_back_kernel(256, heads, *refs),
        out_shape=jax.ShapeDtypeStruct(qkv.shape, bf16),
        grid=(heads,),
        in_specs=[
            piece(0),
            piece(1),
            piece(2),
            piece(0),
            pl.BlockSpec((length, 1), lambda h: (0, 0)),
            pl.BlockSpec((1, length), lambda h: (0, 0)),
        ],
        out_specs=pl.BlockSpec(qkv.shape, lambda h: (0, 0)),
        scratch_shapes=[pltpu.VMEM((length, HDIM), f32), pltpu.VMEM((length, HDIM), f32)],
        compiler_params=pltpu.CompilerParams(vmem_limit_bytes=48 << 20),
        cost_estimate=pl.CostEstimate(
            flops=10 * heads * length * length * HDIM,
            bytes_accessed=14 * heads * length * HDIM,
            transcendentals=heads * length * length,
        ),
        name="attend_backward",
    )(qkv, qkv, qkv, upper, place[:, None], place[None, :])


def gram_of(moment_ref, total_ref, n):
    span = pl.ds(n * HDIM, HDIM)
    state = decay_rate * moment_ref[:, span].astype(f32) + total_ref[:, span].astype(f32)
    return lax.dot_general(
        state, state, (((0,), (0,)), ((), ())), precision=highest, preferred_element_type=f32
    )


def gram_kernel(moment_ref, total_ref, out_ref):
    for n in range(out_ref.shape[0]):
        out_ref[n] = gram_of(moment_ref, total_ref, n)


def apply_kernel(moment_ref, total_ref, factor_ref, out_ref):
    for n in range(factor_ref.shape[0]):
        span = pl.ds(n * HDIM, HDIM)
        state = decay_rate * moment_ref[:, span].astype(f32) + total_ref[:, span].astype(f32)
        out_ref[:, span] = jnp.dot(
            state, factor_ref[n], precision=highest, preferred_element_type=f32
        ).astype(bf16)


def whole_call(kernel, name, out, *operands, flops):
    vmem = pl.BlockSpec(memory_space=pltpu.VMEM)
    return pl.pallas_call(
        kernel,
        out_shape=out,
        in_specs=[vmem] * len(operands),
        out_specs=vmem,
        compiler_params=pltpu.CompilerParams(vmem_limit_bytes=32 << 20),
        cost_estimate=pl.CostEstimate(
            flops=flops, bytes_accessed=sum(o.size * o.dtype.itemsize for o in operands), transcendentals=0
        ),
        name=name,
    )(*operands)


def polynomial(grams):
    width = grams[0].shape[0]
    same = lax.broadcasted_iota(jnp.int32, (width, width), 0) == lax.broadcasted_iota(
        jnp.int32, (width, width), 1
    )
    unit = same.astype(f32)
    dot = lambda a, b: jnp.dot(a, b, precision=highest, preferred_element_type=f32)
    scaled, totals = [], []
    for gram in grams:
        square = jnp.sum(jnp.sum(gram * unit, axis=1, keepdims=True), axis=0, keepdims=True)
        inverse = 1.0 / (jnp.sqrt(square) + ortho_epsilon)
        scaled.append(gram * (inverse * inverse))
        totals.append(unit * inverse)
    for step in range(NS_STEPS):
        squares = [dot(g, g) for g in scaled]
        polys = [
            coef_first * unit + coef_second * g + coef_third * s for g, s in zip(scaled, squares)
        ]
        totals = [dot(q, p) for q, p in zip(totals, polys)]
        if step + 1 < NS_STEPS:
            halves = [dot(g, p) for g, p in zip(scaled, polys)]
            scaled = [dot(p, h) for p, h in zip(polys, halves)]
    return totals


def polynomial_kernel(gram_ref, out_ref):
    for n, total in enumerate(polynomial([gram_ref[n] for n in range(gram_ref.shape[0])])):
        out_ref[n] = total


def fold(symmetric):
    half = symmetric.shape[0] // 2
    last = symmetric[half:, half:]
    sides = jnp.concatenate([last[: half // 2], last[half // 2 :]], axis=1)
    return jnp.concatenate([symmetric[:half], sides], axis=0)


def unfold(folded):
    half = folded.shape[1] // 2
    top, sides = folded[:half], folded[half:]
    last = jnp.concatenate([sides[:, :half], sides[:, half:]], axis=0)
    return jnp.concatenate([top, jnp.concatenate([top[:, half:].T, last], axis=1)], axis=0)


FOLDED = 3 * HDIM // 4


def summed_polynomials(moments, totals, grams, pieces, send, receive, keep, between):
    each_group = totals[0].shape[1] // HDIM
    count = grams.shape[0]
    size = min(each_group, count // 2)
    each = size // 4
    f = lax.axis_index("fsdp")
    planes = [(f + i) % 4 for i in range(4)]
    batches = range(count // size)
    copies = []
    for b in batches:
        first = b * size
        for n in range(first, first + size):
            g = n // each_group
            grams[n] = fold(gram_of(moments[g], totals[g], n % each_group))
        copies.append([])
        for i in (1, 2, 3):
            one = remote(
                grams.at[pl.ds(first + planes[i] * each, each)],
                pieces.at[i - 1, pl.ds(b * each, each)],
                send.at[b, i - 1],
                receive.at[b, i - 1],
                "fsdp",
                planes[i],
            )
            one.start()
            copies[b].append(one)
    between()
    for b in batches:
        sums = [grams[b * size + f * each + n] for n in range(each)]
        for i in (1, 2, 3):
            copies[b][i - 1].wait()
            sums = [s + pieces[i - 1, b * each + n] for n, s in enumerate(sums)]
        for n, value in enumerate(polynomial([unfold(v) for v in sums])):
            keep(b, n, fold(value))
        yield b


def rows_to_owners(totals, targets, send, receive, local, first=0):
    rows = totals[0].shape[0] // 4
    c = lax.axis_index("ctx")
    copies = []
    for g, (total, target) in enumerate(zip(totals, targets)):
        for i in (3, 1, 2, 0):
            side = (c + i) % 4
            source = total.at[pl.ds(pl.multiple_of(side * rows, rows), rows)]
            if i:
                sems = send.at[first + g, i - 1], receive.at[first + g, i - 1]
                copies.append(remote(source, target.at[c], *sems, "ctx", side))
            else:
                copies.append(pltpu.make_async_copy(source, target.at[c], local.at[0, g]))
            copies[-1].start()
    return copies


class Chain:
    def __init__(self, b, size, factors, send, receive):
        self.b, self.size, self.factors, self.send, self.receive_sem = b, size, factors, send, receive
        self.f = lax.axis_index("fsdp")

    def copy(self, up, k, block, plane):
        each = self.size // 4
        ref = self.factors.at[pl.ds(self.b * self.size + block * each, each)]
        at = 2 * self.b + up, k
        return remote(ref, ref, self.send.at[at], self.receive_sem.at[at], "fsdp", plane)

    def leaving(self, up, k):
        f = self.f
        return self.copy(up, k, f - k, f + 1) if up else self.copy(up, k, f + k, f - 1)

    def coming(self, up, k):
        f = self.f
        return self.copy(up, k, f - 1 - k, f - 1) if up else self.copy(up, k, f + 1 + k, f + 1)

    def leaves(self, up, k):
        f = self.f
        return jnp.logical_and(f < 3, f >= k) if up else jnp.logical_and(f > 0, f + k <= 3)

    def comes(self, up, k):
        return self.f >= k + 1 if up else self.f <= 2 - k

    def start(self, k):
        for up in (1, 0):
            pl.when(self.leaves(up, k))(lambda up=up: self.leaving(up, k).start())

    def receive(self, k):
        for up in (1, 0):
            pl.when(self.comes(up, k))(lambda up=up: self.coming(up, k).wait_recv())

    def end(self):
        for k in range(3):
            for up in (1, 0):
                pl.when(self.leaves(up, k))(lambda up=up: self.leaving(up, k).wait_send())


def all_sides():
    c, f, t = (lax.axis_index(axis) for axis in ("ctx", "fsdp", "tp"))
    over = [(axis, (at + i) % 4) for axis, at in (("ctx", c), ("fsdp", f)) for i in (1, 2, 3)]
    return [*over, ("tp", 1 - t)]


def share_core(share, shared, send, receive, local):
    t = lax.axis_index("tp")
    copies = [
        remote(share, shared.at[t], send.at[0], receive.at[0], "tp", 1 - t),
        pltpu.make_async_copy(share, shared.at[t], local.at[0]),
    ]
    for one in copies:
        one.start()
    return copies


def feed_forward_kernel(given, ready, *refs):
    moments, totals, (base, vector, share), refs = refs[:2], refs[2:4], refs[4:7], refs[7:]
    grads_low, weights, refs = refs[:2], refs[2:4], refs[4:]
    (out, *grads), (shared, summed, vector_out), refs = refs[:3], refs[3:6], refs[6:]
    factors, send_c, receive_c, local, send_t, receive_t, local_t, send_f, receive_f = refs[:9]
    gram_refs, (sent_v, got_v, send_v, receive_v) = refs[9:13], refs[13:17]
    part, row_refs = refs[17], refs[18:]
    c, f, t = (lax.axis_index(axis) for axis in ("ctx", "fsdp", "tp"))
    partners = [
        ("tp", 1 - t),
        ("ctx", c + 1 - 2 * (c % 2)),
        ("ctx", c + 2 - 4 * (c // 2)),
        ("fsdp", f + 1 - 2 * (f % 2)),
        ("fsdp", f + 2 - 4 * (f // 2)),
    ]
    greet(all_sides())
    vector_copies = []

    def vector_start(k):
        one = remote(sent_v.at[k], got_v.at[k], send_v.at[k], receive_v.at[k], *partners[k])
        one.start()
        vector_copies.append(one)

    def vector_next(k):
        vector_copies[k].wait_recv()
        if k < 4:
            sent_v[k + 1] = sent_v[k] + got_v[k]
            vector_start(k + 1)
        else:
            vector_out[...] = sent_v[k] + got_v[k]

    sum_rows = RowSums(part, *row_refs)
    half, width = part.shape[3:]
    depth = grads_low[0].shape[1]
    block = width // 4

    def make_part(k, carry):
        rows = pl.ds(pl.multiple_of(k * 2 * half, 2 * half), 2 * half)
        for n in range(4):
            column = pl.ds(n * block, block)
            value = sum(mm(grads_low[i][rows, :], weights[i][column, :depth], (1, 1)) for i in range(2))
            value = value.astype(bf16)
            part[k // 2, k % 2, 0, :, column] = value[:half]
            part[k // 2, k % 2, 1, :, column] = value[half:]
        return carry

    ready(0, 7)
    started = rows_to_owners(totals, grads, send_c, receive_c, local)
    started += share_core(share, shared, send_t, receive_t, local_t)
    sent_v[0] = vector[...]
    vector_start(0)
    size = totals[0].shape[1] // HDIM
    each = size // 4
    chains = [Chain(b, size, factors, send_f, receive_f) for b in range(2)]

    def keep(b, n, value):
        factors[b * size + f * each + n] = value

    def between():
        ready(7, 11)
        lax.fori_loop(0, 4, make_part, 0)
        sum_rows.first(part)
        vector_next(0)

    for b in summed_polynomials(moments, totals, *gram_refs, keep, between):
        chains[b].start(0)
        if b == 0:
            vector_next(1)
            sum_rows.second()
    vector_next(2)
    for j in range(sum_rows.pieces):
        span, total = sum_rows.third(j)
        for h in range(2):
            value = total[h * sum_rows.count : (h + 1) * sum_rows.count]
            summed[h, span] = base[h, span] + value
    for k in range(3):
        for chain in chains:
            chain.receive(k)
            if k < 2:
                chain.start(k + 1)
        if k == 0:
            vector_next(3)
    out[...] = factors[...]
    vector_next(4)
    for chain in chains:
        chain.end()
    for one in vector_copies:
        one.wait_send()
    for one in started:
        one.wait()
    sum_rows.end()


def last_kernel(given, ready, *refs):
    moments, totals, (others, share), refs = refs[:3], refs[3:6], refs[6:8], refs[8:]
    orthos, (grads, shared), refs = refs[:3], refs[3:5], refs[5:]
    factors, stage, send_c, receive_c, local, send_t, receive_t, local_t, send_f, receive_f = refs[:10]
    gram_refs = refs[10:]
    rows = totals[0].shape[0] // 4
    count = totals[0].shape[1] // HDIM
    c, f = lax.axis_index("ctx"), lax.axis_index("fsdp")
    greet(all_sides())
    ready(0, 8)
    started = rows_to_owners(totals[:1], [grads], send_c, receive_c, local)
    started += share_core(share, shared, send_t, receive_t, local_t)

    def send_ortho(g, first, size, kind, factor):
        made = {n: unfold(factor(n)) for n in range(first, first + size)}
        wide = pl.ds(first * HDIM, size * HDIM)
        for i in (3, 1, 2, 0):
            side = (c + i) % 4
            span = pl.ds(pl.multiple_of(side * rows, rows), rows)
            for n in range(first, first + size):
                column = pl.ds(n * HDIM, HDIM)
                state = decay_rate * moments[g][span, column].astype(f32)
                state = state + totals[g][span, column].astype(f32)
                stage[g, i, :, column] = jnp.dot(
                    state, made[n], precision=highest, preferred_element_type=f32
                ).astype(bf16)
            source, target = stage.at[g, i, :, wide], orthos[g].at[c, :, wide]
            if i:
                sems = send_c.at[kind, i - 1], receive_c.at[kind, i - 1]
                copy = remote(source, target, *sems, "ctx", side)
            else:
                copy = pltpu.make_async_copy(source, target, local.at[0, kind])
            copy.start()
            started.append(copy)

    def between():
        for g in (1, 2):
            send_ortho(g, 0, count, g, lambda n: others[(g - 1) * count + n])

    size = count // 2
    each = size // 4
    chains = [Chain(b, size, factors, send_f, receive_f) for b in range(2)]

    def keep(b, n, value):
        factors[b * size + f * each + n] = value

    for b in summed_polynomials(moments[:1], totals[:1], *gram_refs, keep, between):
        chains[b].start(0)
    for k in range(2):
        for chain in chains:
            chain.receive(k)
            chain.start(k + 1)
    for b, chain in enumerate(chains):
        chain.receive(2)
        send_ortho(0, b * size, size, 3 + b, lambda n: factors[n])
    for chain in chains:
        chain.end()
    for one in started:
        one.wait()


def fits_planes(columns):
    return lax.axis_size("fsdp") == 4 and lax.axis_size("ctx") == 4 and columns == 8 * HDIM


def polynomials_over_planes(moment, total):
    count = total.shape[1] // HDIM
    flops = 12 * total.size * HDIM
    shape = jax.ShapeDtypeStruct((count, HDIM, HDIM), f32)
    grams = whole_call(gram_kernel, "grams", shape, moment, total, flops=flops)
    summed = lax.psum(grams, "fsdp")
    return whole_call(polynomial_kernel, "polynomials", shape, summed, flops=flops)


def shared_by_cores(share):
    other, t = swap_core(share), lax.axis_index("tp")
    return jnp.stack([jnp.where(t == m, share, other) for m in range(2)])


def feed_forward_slabs(moments, totals, share, grads_low, weights, base, vector):
    rows, columns = totals[0].shape
    if not fits_planes(columns):
        factors = [polynomials_over_planes(m, v) for m, v in zip(moments, totals)]
        summed = lax.psum(vector, ("fsdp", "ctx", "tp"))
        blocks = [from_blocks(v) for v in totals]
        depth = grads_low[0].shape[1]
        part = sum(mm(g, w[:, :depth], (1, 1)) for g, w in zip(grads_low, weights)).astype(bf16)
        return factors, blocks, shared_by_cores(share), base + collect(part), summed
    count = 2 * columns // HDIM
    vmem = pl.BlockSpec(memory_space=pltpu.VMEM)
    anywhere = pl.BlockSpec(memory_space=pl.ANY)
    block = jax.ShapeDtypeStruct((4, rows // 4, columns), bf16)
    half, width = base.shape[0] // 2, base.shape[1]
    lines = vector.size // HDIM
    dma = pltpu.SemaphoreType.DMA
    operands = [
        *moments,
        *totals,
        base.reshape(2, half, width),
        vector.reshape(lines, HDIM),
        share,
        *grads_low,
        *weights,
    ]
    factors, up, down, shared, summed, vector_sum = pl.pallas_call(
        staged(feed_forward_kernel, 11, 11, 6),
        out_shape=[
            jax.ShapeDtypeStruct((count, FOLDED, HDIM), f32),
            block,
            block,
            jax.ShapeDtypeStruct((2, *share.shape), share.dtype),
            jax.ShapeDtypeStruct((2, half, width), f32),
            jax.ShapeDtypeStruct((lines, HDIM), f32),
        ],
        in_specs=[anywhere] * 11,
        out_specs=[vmem, anywhere, anywhere, anywhere, vmem, vmem],
        scratch_shapes=[
            *slots_for(operands),
            pltpu.VMEM((count, FOLDED, HDIM), f32),
            *[dma((2, 3))] * 2,
            dma((1, 2)),
            *[dma((1,))] * 3,
            *[dma((4, 3))] * 2,
            pltpu.VMEM((count, FOLDED, HDIM), f32),
            pltpu.VMEM((3, count // 4, FOLDED, HDIM), f32),
            *[dma((2, 3))] * 2,
            *[pltpu.VMEM((5, lines, HDIM), f32)] * 2,
            *[dma((5,))] * 2,
            pltpu.VMEM((2, 2, 2, half, width), bf16),
            *row_scratch(half, width),
        ],
        compiler_params=pltpu.CompilerParams(
            collective_id=4, has_side_effects=True, vmem_limit_bytes=56 << 20
        ),
        cost_estimate=pl.CostEstimate(
            flops=24 * totals[0].size * HDIM, bytes_accessed=150 << 20, transcendentals=0
        ),
        name="feed_forward_slabs",
    )(*operands)
    return factors, [up, down], shared, summed.reshape(base.shape), vector_sum.reshape(vector.shape)


def last_slabs(moments, totals, factors, share):
    rows, columns = totals[0].shape
    own = jax.ShapeDtypeStruct((rows, columns), bf16)
    if not fits_planes(columns):
        factors = [polynomials_over_planes(moments[0], totals[0]), *factors]
        flops = 12 * totals[0].size * HDIM
        orthos = [
            from_blocks(whole_call(apply_kernel, "apply", own, m, v, p, flops=flops))
            for m, v, p in zip(moments, totals, factors)
        ]
        return orthos, from_blocks(totals[0]), shared_by_cores(share)
    count = columns // HDIM
    anywhere = pl.BlockSpec(memory_space=pl.ANY)
    block = jax.ShapeDtypeStruct((4, rows // 4, columns), bf16)
    dma = pltpu.SemaphoreType.DMA
    operands = [*moments, *totals, factors, share]
    *orthos, grads, shared = pl.pallas_call(
        staged(last_kernel, 8, 8, 5),
        out_shape=[*[block] * 4, jax.ShapeDtypeStruct((2, *share.shape), share.dtype)],
        in_specs=[anywhere] * 8,
        out_specs=[anywhere] * 5,
        scratch_shapes=[
            *slots_for(operands),
            pltpu.VMEM((count, FOLDED, HDIM), f32),
            pltpu.VMEM((3, 4, rows // 4, columns), bf16),
            *[dma((5, 3))] * 2,
            dma((1, 5)),
            *[dma((1,))] * 3,
            *[dma((4, 3))] * 2,
            pltpu.VMEM((count, FOLDED, HDIM), f32),
            pltpu.VMEM((3, count // 4, FOLDED, HDIM), f32),
            *[dma((2, 3))] * 2,
        ],
        compiler_params=pltpu.CompilerParams(
            collective_id=5, has_side_effects=True, vmem_limit_bytes=56 << 20
        ),
        cost_estimate=pl.CostEstimate(
            flops=36 * totals[0].size * HDIM, bytes_accessed=100 << 20, transcendentals=0
        ),
        name="last_slabs",
    )(*operands)
    return orthos, grads, shared


def pack_attention_kernel(qkv_ref, out_ref, stack_ref):
    wide = qkv_ref.shape[2]
    for which in range(3):
        stack_ref[0, :, which * wide : (which + 1) * wide] = qkv_ref[which].astype(bf16)
    stack_ref[0, :, 3 * wide :] = out_ref[...].T.astype(bf16)


def pack_attention(qkv, out):
    count = lax.axis_size("ctx")
    _, rows, columns = qkv.shape
    wide = columns // count
    return pl.pallas_call(
        pack_attention_kernel,
        out_shape=jax.ShapeDtypeStruct((count, rows, 4 * wide), bf16),
        grid=(count,),
        in_specs=[
            pl.BlockSpec((3, rows, wide), lambda i: (0, 0, i)),
            pl.BlockSpec((wide, rows), lambda i: (i, 0)),
        ],
        out_specs=pl.BlockSpec((1, rows, 4 * wide), lambda i: (i, 0, 0)),
        compiler_params=pltpu.CompilerParams(vmem_limit_bytes=56 << 20),
        cost_estimate=pl.CostEstimate(
            flops=qkv.size, bytes_accessed=8 * qkv.size, transcendentals=0
        ),
        name="pack_attention",
    )(qkv, out)


def attention_block_kernel(given, ready, qkv_ref, out_ref, block_ref, stage, send, receive, local):
    wide = stage.shape[2] // 4
    c = lax.axis_index("ctx")
    greet([("ctx", (c + i) % 4) for i in (1, 2, 3)])
    ready(0, 2)
    copies = []
    for i in (3, 1, 2, 0):
        side = (c + i) % 4
        span = pl.ds(pl.multiple_of(side * wide, wide), wide)
        for which in range(3):
            stage[i, :, which * wide : (which + 1) * wide] = qkv_ref[which, :, span].astype(bf16)
        stage[i, :, 3 * wide :] = out_ref[span, :].T.astype(bf16)
        if i:
            sems = send.at[i - 1], receive.at[i - 1]
            copies.append(remote(stage.at[i], block_ref.at[c], *sems, "ctx", side))
        else:
            copies.append(pltpu.make_async_copy(stage.at[i], block_ref.at[c], local.at[0]))
        copies[-1].start()
    for one in copies:
        one.wait()


def attention_block(qkv, out):
    _, rows, columns = qkv.shape
    if lax.axis_size("ctx") != 4 or columns % 512 or rows % 16:
        return to_blocks(pack_attention(qkv, out))
    shape = (4, rows, columns)
    anywhere = pl.BlockSpec(memory_space=pl.ANY)
    block = pl.pallas_call(
        staged(attention_block_kernel, 2, 2, 1),
        out_shape=jax.ShapeDtypeStruct(shape, bf16),
        in_specs=[anywhere] * 2,
        out_specs=anywhere,
        scratch_shapes=[
            *slots_for([qkv, out]),
            pltpu.VMEM(shape, bf16),
            *[pltpu.SemaphoreType.DMA((3,))] * 2,
            pltpu.SemaphoreType.DMA((1,)),
        ],
        compiler_params=pltpu.CompilerParams(
            collective_id=6, has_side_effects=True, vmem_limit_bytes=56 << 20
        ),
        cost_estimate=pl.CostEstimate(flops=qkv.size, bytes_accessed=30 << 20, transcendentals=0),
        name="attention_block",
    )(qkv, out)
    return block.reshape(4 * rows, columns)


def pack_feed_forward(up, down):
    count = lax.axis_size("ctx")
    rows = up.shape[0]
    low = lambda v: v.astype(bf16)
    up_cut = low(up).reshape(rows, count, -1).transpose(1, 0, 2)
    down_cut = low(down).T.reshape(rows, count, -1).transpose(1, 0, 2)
    return up_cut, down_cut


def finish(name, scale, grads, orthos, moments, weights):
    count, rows, columns = grads.shape
    three = [len(s.shape) == 3 for s in weights]
    tall = [len(s.shape) == 2 and s.shape[0] != rows for s in weights]
    number = len(weights)
    wide = columns // 4 if any(three) else columns
    specs = []
    for is_three, is_tall in zip(three, tall):
        if is_three:
            specs.append(pl.BlockSpec((3, rows, wide), lambda i: (0, 0, i)))
        elif is_tall:
            specs.append(pl.BlockSpec((wide, rows), lambda i: (i, 0)))
        else:
            specs.append(pl.BlockSpec((rows, wide), lambda i: (0, i)))

    def kernel(grad_ref, ortho_ref, *refs):
        for j in range(number):
            moment, weight = refs[j], refs[number + j]
            grad_out, state_out, master_out = refs[2 * number + 3 * j : 2 * number + 3 * j + 3]
            for w in range(3) if three[j] else (None,):
                start = (3 if w is None and any(three) else w or 0) * wide
                cut = lambda ref: ref[0, :, start : start + wide].astype(f32)
                grad, ortho = cut(grad_ref), cut(ortho_ref)
                if tall[j]:
                    grad, ortho = grad.T, ortho.T
                at = ... if w is None else w
                grad_out[at] = grad
                state_out[at] = decay_rate * moment[at] + grad
                master_out[at] = weight[at] - scale * ortho

    outs = pl.pallas_call(
        kernel,
        out_shape=[jax.ShapeDtypeStruct(s.shape, f32) for s in weights for _ in range(3)],
        grid=(count,),
        in_specs=[*[pl.BlockSpec((1, rows, columns), lambda i: (i, 0, 0))] * 2, *specs, *specs],
        out_specs=[spec for spec in specs for _ in range(3)],
        compiler_params=pltpu.CompilerParams(vmem_limit_bytes=56 << 20),
        cost_estimate=pl.CostEstimate(
            flops=4 * grads.size, bytes_accessed=24 * grads.size, transcendentals=0
        ),
        name=name,
    )(grads, orthos, *moments, *weights)
    return outs[0::3], outs[1::3], outs[2::3]


def over_ctx(stack):
    return lax.all_to_all(stack, "ctx", split_axis=0, concat_axis=0, tiled=True)


def to_blocks(stack):
    moved = over_ctx(stack)
    return moved.reshape(-1, moved.shape[-1])


def from_blocks(block):
    return over_ctx(block.reshape(lax.axis_size("ctx"), -1, block.shape[-1]))


def body(
    inputs,
    segment_ids,
    cotangent,
    w_qkv,
    w_out,
    w_up,
    w_down,
    bias_qv,
    bias_up,
    bias_res,
    norm_gain,
    norm_shift,
    moment_qkv,
    moment_out,
    moment_up,
    moment_down,
    moment_bqv,
    moment_bup,
    moment_bres,
    moment_gain,
    moment_shift,
):
    count_c = lax.axis_size("ctx")
    count_f = lax.axis_size("fsdp")
    c = lax.axis_index("ctx")
    t = lax.axis_index("tp")
    rows = inputs.shape[2]
    width = inputs.shape[3]
    length = rows * count_c
    token_total = inputs.shape[0] * inputs.shape[1] * count_f * length
    e = w_qkv.shape[2] // count_c
    u = w_up.shape[1] // count_c

    own_micro = lambda v: lax.dynamic_index_in_dim(v, t, 0, keepdims=False)[0]
    row_low = own_micro(inputs)
    upper = own_micro(cotangent)
    segments = own_micro(segment_ids)
    index = jnp.arange(count_c)
    order = index ^ c if count_c == 4 else index
    place = (segments * (length + HALF + 1) + jnp.arange(length, dtype=jnp.int32)).reshape(count_c, rows)
    place = jnp.take(place, order, axis=0).reshape(length)

    after = lambda value, *others: lax.optimization_barrier((value, *others))[0]
    attn_block = attention_block(w_qkv, w_out)
    up_late, down_late, *moments_late, _ = lax.optimization_barrier(
        (w_up, w_down, moment_qkv, moment_out, moment_up, moment_down, attn_block)
    )
    up_stack, down_stack = pack_feed_forward(up_late, down_late)
    gather_z = lambda v: lax.all_gather(v, "fsdp", axis=0, tiled=True)
    row_first, upper, _ = lax.optimization_barrier((row_low, upper, attn_block))
    xs = jnp.concatenate(spread(row_first), axis=0)
    both_block = to_blocks(after(jnp.concatenate([up_stack, down_stack], axis=2), xs))
    up_block, down_block = both_block[:, :u], both_block[:, u:]
    attn_g, up_g, down_g = map(gather_z, (attn_block, up_block, down_block))
    attn_moments = to_blocks(after(pack_attention(*moments_late[:2]), both_block))
    moment_stack = jnp.concatenate(pack_feed_forward(*moments_late[2:]), axis=2)
    moment_stack = after(moment_stack, both_block)
    attn_g = after(attn_g, moment_stack)
    attn_w = (attn_g, swap_core(attn_g))

    bias_q = lax.dynamic_slice_in_dim(bias_qv, c * e, e, 1)
    bias_u = lax.dynamic_slice_in_dim(bias_up, c * u, u, 0)
    small = jnp.concatenate([bias_q.reshape(-1), bias_u])
    small_pair = (small, swap_core(small))
    cores = range(2)

    qkv = []
    for i in cores:
        shift = jnp.concatenate([small_pair[i][:e], jnp.zeros((e,), f32), small_pair[i][e : 2 * e]])
        qkv.append((mm(xs, attn_w[i][:, : 3 * e], (1, 0)) + shift).astype(bf16))
    context = [attend_forward(qkv[i], place) for i in cores]
    part = sum(mm(context[i], attn_w[i][:, 3 * e :], (1, 1)) for i in cores).astype(bf16)
    row = lambda matrix, index: matrix[index : index + 1]
    part = after(part, attn_moments)
    first_all, (first_unit, first_inverse), _ = exchange(
        "first_rows",
        1,
        first_step,
        part,
        [row_low],
        [row(bias_res, 0), row(norm_gain, 0), row(norm_shift, 0)],
        [f32, f32],
        0,
    )
    moment_block = to_blocks(after(moment_stack, first_all))
    moments = [attn_moments, moment_block[:, :u], moment_block[:, u:]]
    up_g = after(up_g, first_all)
    up_w = (up_g, swap_core(up_g))
    pre_act = [mm(first_all, up_w[i], (1, 0)) + small_pair[i][2 * e :] for i in cores]
    active = [gelu_tanh(p).astype(bf16) for p in pre_act]
    down_g = after(down_g, moment_block, *active)
    down_w = (down_g, swap_core(down_g))
    part = sum(mm(active[i], down_w[i], (1, 1)) for i in cores).astype(bf16)
    branch_all, (out_rows, grad_second), second_sums = exchange(
        "second_rows",
        2,
        second_step,
        part,
        [first_unit, upper],
        [row(bias_res, 1), row(norm_gain, 0), row(norm_shift, 0), row(norm_gain, 1), row(norm_shift, 1)],
        [bf16, f32],
        3,
    )

    def pair_sum(terms):
        own, other = (term.astype(bf16) for term in terms)
        return (own.astype(f32) + swap_core(other).astype(f32)).astype(bf16)

    scatter_z = lambda v: lax.psum_scatter(v, "fsdp", scatter_dimension=0, tiled=True)
    term_down = [None, mm(branch_all, active[1], (0, 0)).astype(bf16)]
    term_down[0] = mm(after(branch_all, term_down[1]), active[0], (0, 0))
    branch_all, *term_down = lax.optimization_barrier((branch_all, *term_down))
    down_sum = pair_sum(term_down)

    def before_gelu(i, rows):
        return jax.vjp(gelu_tanh, pre_act[i])[1](mm(rows, down_w[i], (1, 0)))[0].astype(bf16)

    grad_pre = [before_gelu(0, branch_all)]
    branch_all, down_sum, grad_pre[0] = lax.optimization_barrier((branch_all, down_sum, grad_pre[0]))
    grad_pre.append(before_gelu(1, branch_all))
    part = sum(mm(grad_pre[i], up_w[i], (1, 1)) for i in cores).astype(bf16)
    term_up = [None, mm(first_all, grad_pre[1], (0, 0)).astype(bf16)]
    term_up[0] = mm(after(first_all, term_up[1]), grad_pre[0], (0, 0))
    part, up_sum = lax.optimization_barrier((part, pair_sum(term_up)))
    attended_all, (grad_first,), first_sums = exchange(
        "third_rows",
        3,
        third_step,
        part,
        [first_unit, first_inverse, grad_second],
        [row(norm_gain, 0)],
        [f32],
        3,
    )
    grad_qkv_low, term_qkv, term_out = [None, None], [None, None], [None, None]
    rows_for = attended_all
    for i in (1, 0):
        grad_context = mm(rows_for, attn_w[i][:, 3 * e :], (1, 0)).astype(bf16)
        grad_qkv_low[i] = attend_backward(qkv[i], grad_context, place)
        term_qkv[i] = mm(xs, grad_qkv_low[i], (0, 0))
        term_out[i] = mm(rows_for, context[i], (0, 0))
        if i:
            term_qkv[i], term_out[i] = term_qkv[i].astype(bf16), term_out[i].astype(bf16)
            rows_for = after(attended_all, term_qkv[i], term_out[i])
    attn_sum = jnp.concatenate([pair_sum(term_qkv), pair_sum(term_out)], axis=1)
    down_total, up_total = map(scatter_z, (down_sum, up_sum))
    *lows, attn_sum = lax.optimization_barrier((*grad_qkv_low, attn_sum))

    qv_sums = []
    for i in cores:
        sums_i = jnp.sum(grad_qkv_low[i].astype(f32), axis=0)
        qv_sums.append(jnp.stack([sums_i[:e], sums_i[2 * e :]]))
    up_sums = [jnp.sum(g.astype(f32), axis=0) for g in grad_pre]
    side = lambda pair: [jnp.where(t == m, pair[0], pair[1]) for m in range(2)]
    bqv_all = jnp.stack(
        [
            lax.dynamic_update_slice_in_dim(jnp.zeros((2, count_c * e), f32), v, c * e, 1)
            for v in side(qv_sums)
        ]
    )
    bup_all = jnp.stack(
        [
            lax.dynamic_update_slice_in_dim(jnp.zeros((count_c * u,), f32), v, c * u, 0)
            for v in side(up_sums)
        ]
    )
    rest = jnp.concatenate(
        [
            first_sums[2],
            second_sums[2],
            first_sums[0],
            second_sums[0],
            first_sums[1],
            second_sums[1],
        ],
        axis=0,
    )
    flat = jnp.concatenate([bqv_all.reshape(-1), bup_all.reshape(-1), rest.reshape(-1)])

    attn_total = scatter_z(attn_sum)
    step_scale = matrix_rate * math.sqrt(width / HDIM)
    factors, gradient_blocks, layer_out, input_rows, flat = feed_forward_slabs(
        moments[1:], (up_total, down_total), after(out_rows, attn_sum), lows, attn_w, grad_first, flat
    )
    orthos, attn_gradients, input_grad = last_slabs(
        moments, (attn_total, up_total, down_total), factors, input_rows
    )
    gradient_blocks, flat, orthos = lax.optimization_barrier((gradient_blocks, flat, orthos))
    up_done, down_done = [
        finish(name, step_scale, *operands)
        for name, *operands in (
            ("up_finish", gradient_blocks[0], orthos[1], (moment_up,), (w_up,)),
            ("down_finish", gradient_blocks[1], orthos[2], (moment_down,), (w_down,)),
        )
    ]
    attn_done = finish(
        "attention_finish",
        step_scale,
        attn_gradients,
        orthos[0],
        (moment_qkv, moment_out),
        (w_qkv, w_out),
    )
    grads, states, masters = [
        [*attn_done[k], *up_done[k], *down_done[k]] for k in range(3)
    ]

    cut = bqv_all.size
    cut_two = cut + bup_all.size
    grad_bqv = lax.dynamic_index_in_dim(flat[:cut].reshape(bqv_all.shape), t, 0, keepdims=False)
    grad_bup = lax.dynamic_index_in_dim(flat[cut:cut_two].reshape(bup_all.shape), t, 0, keepdims=False)
    rest = flat[cut_two:].reshape(3, 2, width)
    vector_grads = (grad_bqv, grad_bup, rest[0], rest[1], rest[2])
    vector_states = [
        decay_rate * m + g
        for m, g in zip(
            (moment_bqv, moment_bup, moment_bres, moment_gain, moment_shift), vector_grads
        )
    ]
    vector_step = 1.0 / math.sqrt(token_total)
    vector_masters = [
        v - vector_step * s
        for v, s in zip((bias_qv, bias_up, bias_res, norm_gain, norm_shift), vector_states)
    ]
    return (
        layer_out[:, None],
        input_grad[:, None],
        *grads,
        *vector_grads,
        *states,
        *vector_states,
        *masters,
        *vector_masters,
    )


def solution(mesh):
    rows = P(None, "fsdp", "ctx", None)
    matrices = (
        P(None, ("fsdp", "ctx"), "tp"),
        P("tp", ("fsdp", "ctx")),
        P(("fsdp", "ctx"), "tp"),
        P("tp", ("fsdp", "ctx")),
    )
    vectors = (P(None, "tp"), P("tp"), P(), P(), P())
    return jax.shard_map(
        body,
        mesh=mesh,
        in_specs=(rows, P(None, "fsdp", None), rows, *matrices, *vectors, *matrices, *vectors),
        out_specs=(rows, rows, *((*matrices, *vectors) * 3)),
        check_vma=False,
    )
```
